256 devices in a mesh: dp: 32 (over y, x, core), tensor: 8 (over z).
Axes of the slice: x: 4, y: 4, z: 8, core: 2. Of those that a mesh axis runs over, the one named last changes fastest.
Arguments:
- patches: bfloat16 [65536, 1280], P('dp', 'tensor'), may hold values from -6 to 6
- norm_gain: bfloat16 [1280], P('tensor'), may hold values from 0.5 to 1.5
- w_first: bfloat16 [2560, 4, 1280], P('dp', None, 'tensor'), may hold values from -0.078125 to 0.078125
- b_first: bfloat16 [2560], P('tensor'), may hold values from -3 to 3
- w_second: bfloat16 [4096, 2560], P('dp', 'tensor'), may hold values from -0.125 to 0.125
- b_second: bfloat16 [4096], P('tensor'), may hold values from -3 to 3
- counts: int32 [32], replicated, may hold values from 1 to 32, 512 in all
- cotangent: bfloat16 [16384, 4096], P('dp', 'tensor'), may hold values from -0.0625 to 0.0625
Outputs:
- embeddings: bfloat16 [16384, 4096], P('dp', 'tensor')
- grad_w1: bfloat16 [2560, 4, 1280], P('dp', None, 'tensor')
- grad_w2: bfloat16 [4096, 2560], P('dp', 'tensor')
The draws below stay inside these ranges and needn't reach their ends.
Inputs may be any that keep to these rules, and one draw needn't show every extreme that they name: counts sum to 512 and one rank holds exactly 32 live windows; live windows occupy a rank's first slots.
All inputs are finite; a program needn't handle non-finite values.
Results may differ from the reference program's by a relative error of at most 0.028.
Values may be sent and summed in bfloat16 or wider, within the bound.
A program may use at most 64 MiB of HBM per device.

```python
import math
import jax
import jax.numpy as jnp
import numpy as np
from jax import lax

D = 1280
HID = 2560
OUT = 4096
PATCH = 64
OWN = 32
LIVE = 512
MERGED = 16384
N_DP = 32


def steps_of(key, extent, pieces, smallest, top_value):
    factor_of, own = 1.0, jax.random.fold_in(key, 6)
    for position, parts in pieces:
        draws = jnp.exp(jax.random.uniform(jax.random.fold_in(own, position), (parts,), jnp.float32, smallest / len(pieces), top_value / len(pieces)))
        factor_of = factor_of * jnp.repeat(draws, extent[position] // parts).reshape([-1 if axis == position else 1 for axis in range(len(extent))])
    return factor_of


def split_up(amount, total, reach, lean):
    weights = [(1 << 20) // math.isqrt(standing ** lean) + 1 for standing in range(2, amount + 1)]
    rest, given = total - reach - (amount - 1), [1] * (amount - 1)
    while rest > 0:
        candidates = [i for i in range(amount - 1) if given[i] < reach]
        mass, budget = sum([weights[i] for i in candidates]), rest
        for i in candidates:
            extra = min(reach - given[i], max(1, budget * weights[i] // mass), rest)
            given[i] = given[i] + extra
            rest = rest - extra
    return np.array([reach] + given)


def ragged_sizes(own_key, count, total, limit, lean):
    if count == 2:
        one = jax.random.randint(own_key, (), max(1, total - limit), min(limit, total - 1) + 1)
        return jnp.stack([one, total - one])
    sizes = jnp.asarray(split_up(count, total, limit, lean), jnp.int32)
    pairs = (count - 1) // 2
    donor, taker = sizes[1:1 + 2 * pairs:2], sizes[2:2 + 2 * pairs:2]
    room = jnp.minimum(donor - 1, limit - taker)
    passed = jax.random.randint(jax.random.fold_in(own_key, 1), (pairs,), 0, 1 << 20) % (room + 1)
    sizes = sizes.at[1:1 + 2 * pairs:2].set(donor - passed).at[2:2 + 2 * pairs:2].set(taker + passed)
    return sizes[jax.random.permutation(jax.random.fold_in(own_key, 2), count)]


def gaussian(rng, dims, scale, reach, shards=(), kind=jnp.bfloat16):
    loudness = steps_of(rng, dims, shards, -0.22, 0.18) if shards else 1.0
    result = jax.random.normal(rng, dims, jnp.float32) * scale * loudness
    return jnp.minimum(jnp.maximum(result, -reach), reach).astype(kind)


def setup_inputs(seed: int = 0) -> dict:
    keys = jax.random.split(jax.random.key(seed), 9)
    patches = gaussian(keys[0], (N_DP * OWN * PATCH, D), 1.0, 6.0, ((0, 32), (1, 8)))
    norm_gain = jnp.clip(1.0 + 0.1 * jax.random.normal(keys[1], (D,), jnp.float32), 0.5, 1.5).astype(jnp.bfloat16)
    w_first = gaussian(keys[2], (HID, 4, D), (4 * D) ** -0.5, 0.078125, ((0, 32), (2, 8)))
    b_first = gaussian(keys[3], (HID,), 0.5, 3.0, ((0, 8),))
    w_second = gaussian(keys[4], (OUT, HID), HID ** -0.5, 0.125, ((0, 32), (1, 8)))
    b_second = gaussian(keys[5], (OUT,), 0.5, 3.0, ((0, 8),))
    counts = ragged_sizes(keys[6], N_DP, LIVE, OWN, 2).astype(jnp.int32)
    cotangent = gaussian(keys[7], (MERGED, OUT), (LIVE * PATCH // 4) ** -0.5, 0.0625, ((0, 32), (1, 8)))
    return {"patches": patches, "norm_gain": norm_gain, "w_first": w_first, "b_first": b_first, "w_second": w_second, "b_second": b_second, "counts": counts, "cotangent": cotangent}


def gelu_parts(values):
    normal_cdf = 0.5 * (1.0 + lax.erf(values * 0.7071067811865476))
    density = jnp.exp(-0.5 * values * values) * 0.3989422804014327
    return (values * normal_cdf, normal_cdf + values * density)

def live_slots(counts):
    counts = counts.astype(jnp.int32)
    ends = jnp.cumsum(counts).astype(jnp.int32)
    starts = ends - counts
    ordinal = jnp.arange(LIVE, dtype=jnp.int32)
    owners = lax.optimization_barrier(jnp.sum((ends[None, :] <= ordinal[:, None]).astype(jnp.int32), axis=1)).astype(jnp.int32)
    slots = ordinal - starts[owners]
    return (owners * OWN + slots).astype(jnp.int32)

def reference(patches, norm_gain, w_first, b_first, w_second, b_second, counts, cotangent):
    live = live_slots(counts)
    chosen = patches.reshape(N_DP * OWN, PATCH, D)[live].reshape(LIVE * PATCH, D)
    floats = chosen.astype(jnp.float32)
    mean_sq = lax.optimization_barrier(jnp.mean(floats * floats, axis=1, keepdims=True))
    normed = (floats * lax.rsqrt(mean_sq + 1e-06) * norm_gain.astype(jnp.float32)).astype(jnp.bfloat16)
    merged = normed.reshape(LIVE * PATCH // 4, 4 * D)
    first = w_first.reshape(HID, 4 * D)
    pre_act = lax.dot_general(merged, first, (((1,), (1,)), ((), ())), preferred_element_type=jnp.float32)
    pre_act = pre_act + b_first.astype(jnp.float32)
    activated, slopes = gelu_parts(pre_act)
    hidden = activated.astype(jnp.bfloat16)
    embed = lax.dot_general(hidden, w_second, (((1,), (1,)), ((), ())), preferred_element_type=jnp.float32)
    embed = (embed + b_second.astype(jnp.float32)).astype(jnp.bfloat16)
    placed = jnp.zeros((N_DP * OWN, PATCH // 4, OUT), jnp.bfloat16)
    placed = placed.at[live].set(embed.reshape(LIVE, PATCH // 4, OUT))
    embeddings = placed.reshape(MERGED, OUT)
    grad_rows = cotangent.reshape(N_DP * OWN, PATCH // 4, OUT)[live].reshape(LIVE * PATCH // 4, OUT)
    grad_w2 = lax.dot_general(grad_rows, hidden, (((0,), (0,)), ((), ())), preferred_element_type=jnp.float32)
    grad_hidden = jnp.dot(grad_rows, w_second, preferred_element_type=jnp.float32)
    grad_pre = (grad_hidden * slopes).astype(jnp.bfloat16)
    grad_w1 = lax.dot_general(grad_pre, merged, (((0,), (0,)), ((), ())), preferred_element_type=jnp.float32)
    return (embeddings, grad_w1.reshape(HID, 4, D).astype(jnp.bfloat16), grad_w2.astype(jnp.bfloat16))
```

```python
import functools

import jax
import jax.numpy as jnp
from jax import lax
from jax.experimental import pallas as pl
from jax.experimental.pallas import tpu as pltpu
from jax.sharding import PartitionSpec as P

D = 1280
PATCH = 64
DP = 32
TP = 8
CHIPS = 16
SLOTS = 32
ROWS = PATCH // 4
TOK = 512
UNITS = 160
FEAT = 640
OUTW = 512
W1A = 48

MESH = pl.DeviceIdType.MESH
BF = jnp.bfloat16
F32 = jnp.float32
NT = (((1,), (1,)), ((), ()))
NN = (((1,), (0,)), ((), ()))
TN = (((0,), (0,)), ((), ()))


def dot(a, b, dims):
    return lax.dot_general(a, b, dims, preferred_element_type=F32)


def up(index, size):
    return lax.rem(index + size, size)


class Copies:
    def __init__(self, send, recv):
        self.send, self.recv, self.used, self.open = send, recv, 0, []

    def take(self, count):
        base = self.used
        self.used += count
        return base

    def make(self, src, dst, sem, dev, sent=None):
        return pltpu.make_async_remote_copy(
            src_ref=src,
            dst_ref=dst,
            send_sem=self.send.at[sem if sent is None else sent],
            recv_sem=self.recv.at[sem],
            device_id=dev,
            device_id_type=MESH,
        )

    def start(self, src, dst, sem, dev):
        copy = self.make(src, dst, sem, dev)
        copy.start()
        self.open.append(copy)

    def landed(self, dst, sem, dev):
        self.make(dst, dst, sem, dev).wait_recv()

    def finish(self):
        for item in self.open:
            if callable(item):
                item()
            else:
                item.wait_send()


def kernel(
    counts, pk, w1, w2p, b1, b2, gain, cot,
    emb, gw1, gw2,
    send, recv, lsem, starts, ends, srcs,
    sc, cc, g, nrm, sp, cp, x, sqx,
    w1f, w2t,
    pg, ph, zgr, zgl, zhr, zhl, og, oh,
    ht, gt,
    pe, ps, pr, sb, bk,
    g2, a2, c2, s2a, s2b, d2, e2, t2,
    g1, a1, c1, s1a, s1b, d1, e1,
):
    r = lax.axis_index("dp")
    t = lax.axis_index("tensor")
    m, c = lax.div(r, 2), lax.rem(r, 2)
    X, Y = lax.rem(m, 4), lax.div(m, 4)
    a, b = lax.div(m, 2), lax.rem(m, 2)
    links = Copies(send, recv)

    def plane(chip):
        return (2 * chip + c, t)

    def along_x(d):
        return plane(4 * Y + up(X + d, 4))

    def along_y(d):
        return plane(4 * up(Y + d, 4) + X)

    sibling = (2 * m + 1 - c, t)
    right, left = (r, up(t + 1, TP)), (r, up(t - 1, TP))
    mate = 2 * t + b
    same = a == t

    barrier = pltpu.get_barrier_semaphore()

    def greet(dev):
        pl.semaphore_signal(barrier, inc=1, device_id=dev, device_id_type=MESH)

    for d in range(1, CHIPS):
        greet(plane(up(m + d, CHIPS)))
    for d in range(1, TP):
        greet((r, up(t + d, TP)))
    greet(sibling)

    @pl.when(jnp.logical_not(same))
    def _():
        for e in range(2):
            greet((2 * mate + e, a))

    def prefix(s, total):
        starts[s] = total
        total = total + counts[s]
        ends[s] = total
        return total

    lax.fori_loop(0, DP, prefix, jnp.int32(0))
    mine_start, mine_count = starts[r], counts[r]

    def pack_cot(p, carry):
        sc[p] = cot[up(p - mine_start + 1024, SLOTS)]
        return carry

    lax.fori_loop(0, DP, pack_cot, 0)

    lane = lax.broadcasted_iota(jnp.int32, (8, FEAT), 1)
    row = lax.broadcasted_iota(jnp.int32, (8, FEAT), 0)
    lead = jnp.logical_and(lane >= row * 160, lane < row * 160 + 160)
    pick = jnp.where(lead, 1.0, 0.0).astype(F32)
    pick_bf = pick.astype(BF)
    for i in range(4):
        v = pk[8 * i : 8 * i + 8].reshape(128, FEAT).astype(F32)
        sq = v * v
        high = sq.astype(BF)
        low = (sq - high.astype(F32)).astype(BF)
        sqx[t, :, 128 * i : 128 * i + 128] = dot(pick_bf, high, NT) + dot(pick_bf, low, NT)

    w1f[Y, X] = w1[...]

    pl.semaphore_wait(barrier, 23 + jnp.where(same, 0, 2))

    relay = links.take(2)
    relay_out = w2t.at[
        lax.div(t, 2), lax.rem(t, 2), :, pl.ds(pl.multiple_of(b * 256 + c * 128, 128), 128)
    ]

    def relay_in(e):
        return w2t.at[
            lax.div(a, 2), lax.rem(a, 2), :, pl.ds(pl.multiple_of(b * 256 + e * 128, 128), 128)
        ]

    @pl.when(jnp.logical_not(same))
    def _():
        for e in range(2):
            links.make(w2p.at[e], relay_out, relay + c, (2 * mate + e, a), relay + e).start()

    @pl.when(same)
    def _():
        links.make(w2p.at[1 - c], relay_out, relay + c, sibling, relay + 1 - c).start()
        own = pltpu.make_async_copy(w2p.at[c], relay_out, lsem)
        own.start()
        own.wait()

    def relay_sent():
        @pl.when(jnp.logical_not(same))
        def _():
            for e in range(2):
                links.make(w2p.at[e], relay_out, relay + c, (2 * mate + e, a), relay + e).wait_send()

        @pl.when(same)
        def _():
            links.make(w2p.at[1 - c], relay_out, relay + c, sibling, relay + 1 - c).wait_send()

    links.open.append(relay_sent)

    def exchange(out, into, base):
        def step(d, carry):
            chip = up(m + d, CHIPS)
            links.make(out.at[pl.ds(2 * chip, 2)], into.at[m], base + d, plane(chip)).start()
            return carry

        lax.fori_loop(1, CHIPS, step, 0)

        def sent(d, carry):
            chip = up(m + d, CHIPS)
            links.make(out.at[pl.ds(2 * chip, 2)], into.at[m], base + d, plane(chip)).wait_send()
            return carry

        links.open.append(lambda: lax.fori_loop(1, CHIPS, sent, 0))
        into[m] = out[pl.ds(2 * m, 2)]

    def exchanged(into, base):
        def step(d, carry):
            links.landed(into.at[up(m - d, CHIPS)], base + d, plane(up(m - d, CHIPS)))
            return carry

        lax.fori_loop(1, CHIPS, step, 0)

    cot_base = links.take(CHIPS)
    exchange(sc, cc.at[c], cot_base)

    sq_base = links.take(TP)
    for d in range(1, TP):
        links.start(sqx.at[t], sqx.at[t], sq_base + d, (r, up(t + d, TP)))

    def gather_first(block_a, block_b, base):
        for d in range(1, 4):
            links.start(block_a, block_a, base + d, along_x(d))
            links.start(block_b, block_b, base + 3 + d, along_y(d))

    w1a = w1f.at[Y, X, 0:W1A]
    w1b = w1f.at[Y, X, W1A:80]
    w1_base = links.take(16)
    w2_base = links.take(16)
    w2lane = pl.ds(pl.multiple_of(b * 256, 256), 256)
    xh = lax.div(X, 2)
    w2a = w2t.at[Y, xh, 0:80, w2lane]
    w2b = w2t.at[Y, xh, 80:160, w2lane]

    def source(k, carry):
        p0 = 32 * k + 2 * m
        n0, n1 = jnp.int32(0), jnp.int32(0)
        for s in range(DP):
            v = ends[s]
            n0 = n0 + (v <= p0).astype(jnp.int32)
            n1 = n1 + (v <= p0 + 1).astype(jnp.int32)
        srcs[k] = jnp.minimum(n0, DP - 1)
        srcs[16 + k] = jnp.minimum(n1, DP - 1)
        return carry

    lax.fori_loop(0, 16, source, 0)

    for e in range(2):

        @pl.when(jnp.logical_or(jnp.logical_not(same), e != c))
        def _(e=e):
            links.landed(relay_in(e), relay + e, sibling)

    gather_first(w2a, w2b, w2_base)

    for d in range(1, TP):
        z = up(t - d, TP)
        links.landed(sqx.at[z], sq_base + d, (r, z))
    total = sqx[0]
    for z in range(1, TP):
        total = total + sqx[z]
    inv = lax.rsqrt(total / D + 1e-06)
    i1 = inv.astype(BF).astype(F32)
    i2 = (inv - i1).astype(BF).astype(F32)
    i3 = (inv - i1) - i2
    stack = jnp.concatenate([i1, i2, i3], axis=0)
    stack_t = stack.T.astype(BF)
    pick3 = jnp.concatenate([pick, pick, pick], axis=0).astype(BF)
    gains = gain[...]
    for i in range(4):
        scale = dot(stack_t[128 * i : 128 * i + 128], pick3, NN)
        v = pk[8 * i : 8 * i + 8].reshape(128, FEAT).astype(F32)
        nrm[8 * i : 8 * i + 8] = (v * scale * gains).astype(BF).reshape(8, ROWS, FEAT)

    def pack_rows(p, carry):
        sp[p] = nrm[up(p - mine_start + 1024, SLOTS)]
        return carry

    lax.fori_loop(0, DP, pack_rows, 0)
    row_base = links.take(CHIPS)
    exchange(sp, cp.at[c], row_base)
    gather_first(w1a, w1b, w1_base)

    def gather_second(wide_a, wide_b, arrived, base):
        for d in range(1, 4):
            ra, rb = arrived(d)
            links.landed(ra, base + d, along_x(-d))
            links.landed(rb, base + 3 + d, along_y(-d))
        for d in range(1, 4):
            links.start(wide_a, wide_a, base + 6 + d, along_y(d))
            links.start(wide_b, wide_b, base + 9 + d, along_x(d))

    def w2_first(d):
        xx, yy = up(X - d, 4), up(Y - d, 4)
        ra = w2t.at[Y, lax.div(xx, 2), 0:80, pl.ds(pl.multiple_of(lax.rem(xx, 2) * 256, 256), 256)]
        rb = w2t.at[yy, xh, 80:160, w2lane]
        return ra, rb

    def w1_first(d):
        return w1f.at[Y, up(X - d, 4), 0:W1A], w1f.at[up(Y - d, 4), X, W1A:80]

    gather_second(w2t.at[Y, :, 0:80], w2t.at[:, xh, 80:160, w2lane], w2_first, w2_base)

    exchanged(cc.at[c], cot_base)
    cot_sib = links.take(1)
    links.start(cc.at[c], cc.at[c], cot_sib, sibling)

    gather_second(w1f.at[Y, :, 0:W1A], w1f.at[:, X, W1A:80], w1_first, w1_base)

    links.landed(cc.at[1 - c], cot_sib, sibling)

    def choose(cand, out):
        def step(j, carry):
            s = srcs[j]
            out[j] = cand[lax.rem(s, 2), lax.div(s, 2), lax.div(j, 16)]
            return carry

        lax.fori_loop(0, 32, step, 0)

    choose(cc, g)

    for d in range(1, 4):
        xx, yy = up(X - d, 4), up(Y - d, 4)
        links.landed(w2t.at[yy, :, 0:80], w2_base + 6 + d, along_y(-d))
        links.landed(
            w2t.at[:, lax.div(xx, 2), 80:160, pl.ds(pl.multiple_of(lax.rem(xx, 2) * 256, 256), 256)],
            w2_base + 9 + d,
            along_x(-d),
        )

    def ring_sum(part, rr, rl, base, s):
        br, bl = up(t + 4 - s, TP), up(t - 4 + s, TP)
        if s == 0:
            links.start(part.at[br, 0:80], rr.at[0, 0:80], base, right)
            links.start(part.at[bl, 80:160], rl.at[0, 80:160], base + 4, left)
            return
        lo, hi = ((0, 80), (80, 160)) if s == 1 else ((0, 160), (0, 160))
        links.landed(rr.at[s - 1, lo[0] : lo[1]], base + s - 1, left)
        part[br, lo[0] : lo[1]] = (
            part[br, lo[0] : lo[1]].astype(F32) + rr[s - 1, lo[0] : lo[1]].astype(F32)
        ).astype(BF)
        links.start(part.at[br], rr.at[s], base + s, right)
        links.landed(rl.at[s - 1, hi[0] : hi[1]], base + 4 + s - 1, right)
        part[bl, hi[0] : hi[1]] = (
            part[bl, hi[0] : hi[1]].astype(F32) + rl[s - 1, hi[0] : hi[1]].astype(F32)
        ).astype(BF)
        links.start(part.at[bl], rl.at[s], base + 4 + s, left)

    def ring_end(rr, rl, base):
        links.landed(rr.at[3], base + 3, left)
        links.landed(rl.at[3], base + 7, right)

    def grad_block(z):
        gg = g[...].reshape(TOK, OUTW)
        return dot(w2t[lax.div(z, 2), lax.rem(z, 2)], gg, NT)

    def grad_blocks(i, carry):
        z = up(t + 4 + i, TP)
        pg[z] = grad_block(z).astype(BF)
        return carry

    pg_base = links.take(8)
    lax.fori_loop(0, 1, grad_blocks, 0)
    ring_sum(pg, zgr, zgl, pg_base, 0)
    lax.fori_loop(1, 8, grad_blocks, 0)
    og[...] = grad_block(t)
    ring_sum(pg, zgr, zgl, pg_base, 1)

    exchanged(cp.at[c], row_base)
    row_sib = links.take(1)
    links.start(cp.at[c], cp.at[c], row_sib, sibling)
    ring_sum(pg, zgr, zgl, pg_base, 2)
    links.landed(cp.at[1 - c], row_sib, sibling)
    choose(cp, x)
    ring_sum(pg, zgr, zgl, pg_base, 3)

    for d in range(1, 4):
        xx, yy = up(X - d, 4), up(Y - d, 4)
        links.landed(w1f.at[yy, :, 0:W1A], w1_base + 6 + d, along_y(-d))
        links.landed(w1f.at[:, xx, W1A:80], w1_base + 9 + d, along_x(-d))

    def pre_block(z):
        rows = w1f[lax.div(z, 2), pl.ds(2 * lax.rem(z, 2), 2)].reshape(UNITS, FEAT)
        return dot(rows, x[...].reshape(TOK, FEAT), NT)

    def pre_blocks(i, carry):
        z = up(t + 4 + i, TP)
        ph[z] = pre_block(z).astype(BF)
        return carry

    ph_base = links.take(8)
    lax.fori_loop(0, 1, pre_blocks, 0)
    ring_sum(ph, zhr, zhl, ph_base, 0)
    lax.fori_loop(1, 8, pre_blocks, 0)
    oh[...] = pre_block(t)
    for s in range(1, 4):
        ring_sum(ph, zhr, zhl, ph_base, s)
    ring_end(zgr, zgl, pg_base)
    ring_end(zhr, zhl, ph_base)

    def activate(i, carry):
        rows = pl.ds(pl.multiple_of(i * 32, 32), 32)
        bias = b1[c, rows]
        v = oh[rows] + zhr[3, rows].astype(F32) + zhl[3, rows].astype(F32)
        v = v + jnp.concatenate([bias] * 4, axis=1)
        cdf = 0.5 * (1.0 + lax.erf(v * 0.7071067811865476))
        density = jnp.exp(-0.5 * v * v) * 0.3989422804014327
        ht[t, rows] = (v * cdf).astype(BF)
        gh = og[rows] + zgr[3, rows].astype(F32) + zgl[3, rows].astype(F32)
        gt[t, rows] = (gh * (cdf + v * density)).astype(BF)
        return carry

    lax.fori_loop(0, 5, activate, 0)

    def ring_copy(buf, base, s):
        br, bl = up(t - s, TP), up(t + s, TP)
        if s > 0:
            links.landed(buf.at[br], base + s - 1, left)
            links.landed(buf.at[bl], base + 4 + s - 1, right)
        if s < 3:
            links.start(buf.at[br], buf.at[br], base + s, right)
            links.start(buf.at[bl], buf.at[bl], base + 4 + s, left)
        else:
            links.start(buf.at[br, 0:80], buf.at[br, 0:80], base + s, right)
            links.start(buf.at[bl, 80:160], buf.at[bl, 80:160], base + 4 + s, left)

    def ring_copied(buf, base):
        far = up(t + 4, TP)
        links.landed(buf.at[far, 0:80], base + 3, left)
        links.landed(buf.at[far, 80:160], base + 7, right)

    ht_base, gt_base = links.take(8), links.take(8)
    ring_copy(ht, ht_base, 0)
    ring_copy(gt, gt_base, 0)
    ring_copy(ht, ht_base, 1)
    ring_copy(gt, gt_base, 1)
    ring_copy(ht, ht_base, 2)
    ring_copy(ht, ht_base, 3)
    ring_copy(gt, gt_base, 2)
    ring_copied(ht, ht_base)

    def plane_sum_first(part, cut, ra, rb, base):
        for d in range(1, 4):
            yy, xx = up(Y + d, 4), up(X + d, 4)
            links.start(part.at[yy, :, 0:cut], ra.at[d - 1], base + d, along_y(d))
            links.start(part.at[:, xx, cut:], rb.at[d - 1], base + 3 + d, along_x(d))

    def plane_sum_second(part, cut, ra, rb, sa, sbx, rc, rd, base):
        for d in range(1, 4):
            links.landed(ra.at[d - 1], base + d, along_y(-d))
        for i in range(4):
            v = part[Y, i, 0:cut].astype(F32)
            for d in range(3):
                v = v + ra[d, i].astype(F32)
            sa[i] = v.astype(BF)
        for d in range(1, 4):
            links.start(sa.at[up(X + d, 4)], rc.at[d - 1], base + 6 + d, along_x(d))
        for d in range(1, 4):
            links.landed(rb.at[d - 1], base + 3 + d, along_x(-d))
        for i in range(4):
            v = part[i, X, cut:].astype(F32)
            for d in range(3):
                v = v + rb[d, i].astype(F32)
            sbx[i] = v.astype(BF)
        for d in range(1, 4):
            links.start(sbx.at[up(Y + d, 4)], rd.at[d - 1], base + 9 + d, along_y(d))

    def plane_sum_end(sa, sbx, rc, rd, base):
        for d in range(1, 4):
            links.landed(rc.at[d - 1], base + 6 + d, along_x(-d))
        va = sa[X].astype(F32)
        for d in range(3):
            va = va + rc[d].astype(F32)
        for d in range(1, 4):
            links.landed(rd.at[d - 1], base + 9 + d, along_y(-d))
        vb = sbx[Y].astype(F32)
        for d in range(3):
            vb = vb + rd[d].astype(F32)
        return va.astype(BF), vb.astype(BF)

    def second_grad(z, carry):
        v = dot(ht[z], g[...].reshape(TOK, OUTW), NN).astype(BF)
        for i in range(2):
            g2[lax.div(z, 2), 2 * lax.rem(z, 2) + i] = v[:, 256 * i : 256 * i + 256]
        return carry

    lax.fori_loop(0, TP, second_grad, 0)
    g2_base = links.take(16)
    plane_sum_first(g2, 80, a2, c2, g2_base)

    def embed(i, carry):
        lanes = pl.ds(pl.multiple_of(i * 128, 128), 128)
        acc = jnp.zeros((128, OUTW), F32)
        for z in range(TP):
            acc = acc + dot(ht[z, :, lanes].astype(F32).T.astype(BF), w2t[z // 2, z % 2], NN)
        pe[pl.ds(8 * i, 8)] = acc.reshape(8, ROWS, OUTW)
        return carry

    lax.fori_loop(0, 4, embed, 0)
    ring_copy(gt, gt_base, 3)

    def window_of(s, e):
        first = starts[s]
        slot = lax.rem(2 * m + e - first + 1024, SLOTS)
        return e * 16 + jnp.minimum(lax.div(first + slot, 32), 15)

    def pack_sibling(i, carry):
        for e in range(2):
            ps[2 * i + e] = pe[window_of(2 * i + 1 - c, e)].astype(BF)
        return carry

    lax.fori_loop(0, CHIPS, pack_sibling, 0)
    emb_sib = links.take(1)
    links.start(ps, pr, emb_sib, sibling)
    plane_sum_second(g2, 80, a2, c2, s2a, s2b, d2, e2, g2_base)
    links.landed(pr, emb_sib, sibling)
    bias2 = b2[...]

    def pack_home(i, carry):
        for e in range(2):
            v = pe[window_of(2 * i + c, e)] + pr[2 * i + e].astype(F32) + bias2
            sb[2 * i + e] = v.astype(BF)
        return carry

    lax.fori_loop(0, CHIPS, pack_home, 0)
    home_base = links.take(CHIPS)
    exchange(sb, bk, home_base)

    ring_copied(gt, gt_base)

    def first_grad(z, carry):
        v = dot(gt[z], x[...].reshape(TOK, FEAT), NN).astype(BF)
        for i in range(2):
            g1[lax.div(z, 2), 2 * lax.rem(z, 2) + i] = v[80 * i : 80 * i + 80]
        return carry

    lax.fori_loop(0, TP, first_grad, 0)
    g1_base = links.take(16)
    plane_sum_first(g1, W1A, a1, c1, g1_base)

    va, vb = plane_sum_end(s2a, s2b, d2, e2, g2_base)
    for e in range(2):
        t2[e, 0:80] = va[:, 128 * e : 128 * e + 128]
        t2[e, 80:160] = vb[:, 128 * e : 128 * e + 128]
    back = links.take(2)

    @pl.when(jnp.logical_not(same))
    def _():
        for e in range(2):
            links.make(t2.at[e], gw2.at[c], back + c, (2 * mate + e, a), back + e).start()

    @pl.when(same)
    def _():
        links.make(t2.at[1 - c], gw2.at[c], back + c, sibling, back + 1 - c).start()
        gw2[c] = t2[c]

    def back_sent():
        @pl.when(jnp.logical_not(same))
        def _():
            for e in range(2):
                links.make(t2.at[e], gw2.at[c], back + c, (2 * mate + e, a), back + e).wait_send()

        @pl.when(same)
        def _():
            links.make(t2.at[1 - c], gw2.at[c], back + c, sibling, back + 1 - c).wait_send()

    links.open.append(back_sent)

    plane_sum_second(g1, W1A, a1, c1, s1a, s1b, d1, e1, g1_base)

    exchanged(bk, home_base)

    def home(j, carry):
        p = lax.rem(mine_start + j, DP)
        v = bk[lax.div(p, 2), lax.rem(p, 2)].astype(F32)
        emb[j] = jnp.where(j < mine_count, v, 0.0).astype(BF)
        return carry

    lax.fori_loop(0, SLOTS, home, 0)

    for e in range(2):

        @pl.when(jnp.logical_or(jnp.logical_not(same), e != c))
        def _(e=e):
            links.landed(gw2.at[e], back + e, sibling)

    va, vb = plane_sum_end(s1a, s1b, d1, e1, g1_base)
    gw1[0:W1A] = va
    gw1[W1A:80] = vb
    links.finish()


def on_device(patches, norm_gain, w_first, b_first, w_second, b_second, counts, cotangent):
    pk = patches.reshape(SLOTS, ROWS, FEAT)
    w1 = w_first.reshape(80, FEAT)
    w2p = w_second.T.reshape(2, 2, 80, 128).transpose(1, 0, 2, 3).reshape(2, UNITS, 128)
    b1 = b_first.astype(F32).reshape(2, 2, 80).transpose(1, 0, 2).reshape(2, UNITS, 1)
    b1 = jnp.broadcast_to(b1, (2, UNITS, 128))
    b2 = b_second.astype(F32).reshape(1, OUTW)
    gain = jnp.tile(norm_gain.astype(F32).reshape(1, 160), (1, 4))
    cot = cotangent.reshape(SLOTS, ROWS, OUTW)

    vmem = pl.BlockSpec(memory_space=pltpu.VMEM)
    V = pltpu.VMEM
    S = pltpu.SMEM
    emb, gw1, gw2 = pl.pallas_call(
        kernel,
        name="merger",
        out_shape=(
            jax.ShapeDtypeStruct((SLOTS, ROWS, OUTW), BF),
            jax.ShapeDtypeStruct((80, FEAT), BF),
            jax.ShapeDtypeStruct((2, UNITS, 128), BF),
        ),
        in_specs=[pl.BlockSpec(memory_space=pltpu.SMEM)] + [vmem] * 7,
        out_specs=(vmem, vmem, vmem),
        scratch_shapes=[
            pltpu.SemaphoreType.DMA((200,)),
            pltpu.SemaphoreType.DMA((200,)),
            pltpu.SemaphoreType.DMA,
            S((DP,), jnp.int32),
            S((DP,), jnp.int32),
            S((DP,), jnp.int32),
            V((DP, ROWS, OUTW), BF),
            V((2, CHIPS, 2, ROWS, OUTW), BF),
            V((32, ROWS, OUTW), BF),
            V((SLOTS, ROWS, FEAT), BF),
            V((DP, ROWS, FEAT), BF),
            V((2, CHIPS, 2, ROWS, FEAT), BF),
            V((32, ROWS, FEAT), BF),
            V((TP, 8, TOK), F32),
            V((4, 4, 80, FEAT), BF),
            V((4, 2, UNITS, OUTW), BF),
            V((TP, UNITS, TOK), BF),
            V((TP, UNITS, TOK), BF),
            V((4, UNITS, TOK), BF),
            V((4, UNITS, TOK), BF),
            V((4, UNITS, TOK), BF),
            V((4, UNITS, TOK), BF),
            V((UNITS, TOK), F32),
            V((UNITS, TOK), F32),
            V((TP, UNITS, TOK), BF),
            V((TP, UNITS, TOK), BF),
            V((32, ROWS, OUTW), F32),
            V((32, ROWS, OUTW), BF),
            V((32, ROWS, OUTW), BF),
            V((32, ROWS, OUTW), BF),
            V((CHIPS, 2, ROWS, OUTW), BF),
            V((4, 4, UNITS, 256), BF),
            V((3, 4, 80, 256), BF),
            V((3, 4, 80, 256), BF),
            V((4, 80, 256), BF),
            V((4, 80, 256), BF),
            V((3, 80, 256), BF),
            V((3, 80, 256), BF),
            V((2, UNITS, 128), BF),
            V((4, 4, 80, FEAT), BF),
            V((3, 4, W1A, FEAT), BF),
            V((3, 4, 80 - W1A, FEAT), BF),
            V((4, W1A, FEAT), BF),
            V((4, 80 - W1A, FEAT), BF),
            V((3, W1A, FEAT), BF),
            V((3, 80 - W1A, FEAT), BF),
        ],
        compiler_params=pltpu.CompilerParams(
            collective_id=0, has_side_effects=True, vmem_limit_bytes=56 * 1024 * 1024
        ),
        cost_estimate=pl.CostEstimate(
            flops=3_700_000_000, bytes_accessed=3_000_000, transcendentals=200_000
        ),
    )(counts, pk, w1, w2p, b1, b2, gain, cot)
    embeddings = emb.reshape(SLOTS * ROWS, OUTW)
    grad_w1 = gw1.reshape(80, 4, 160)
    grad_w2 = gw2.reshape(2, 2, 80, 128).transpose(3, 1, 0, 2).reshape(128, 320)
    return embeddings, grad_w1, grad_w2


def solution(mesh):
    in_specs = (
        P("dp", "tensor"),
        P("tensor"),
        P("dp", None, "tensor"),
        P("tensor"),
        P("dp", "tensor"),
        P("tensor"),
        P(),
        P("dp", "tensor"),
    )
    out_specs = (P("dp", "tensor"), P("dp", None, "tensor"), P("dp", "tensor"))
    return jax.shard_map(
        on_device, mesh=mesh, in_specs=in_specs, out_specs=out_specs, check_vma=False
    )
```

```python
import functools

import jax
import jax.numpy as jnp
from jax import lax
from jax.experimental import pallas as pl
from jax.experimental.pallas import tpu as pltpu
from jax.sharding import PartitionSpec as P

D = 1280
PATCH = 64
DP = 32
TP = 8
CHIPS = 16
SLOTS = 32
ROWS = PATCH // 4
TOK = 512
UNITS = 160
FEAT = 640
OUTW = 512
W1A = 48

MESH = pl.DeviceIdType.MESH
BF = jnp.bfloat16
F32 = jnp.float32
NT = (((1,), (1,)), ((), ()))
NN = (((1,), (0,)), ((), ()))
TN = (((0,), (0,)), ((), ()))


def dot(a, b, dims):
    return lax.dot_general(a, b, dims, preferred_element_type=F32)


def up(index, size):
    return lax.rem(index + size, size)


class Copies:
    def __init__(self, send, recv):
        self.send, self.recv, self.used, self.open = send, recv, 0, []

    def take(self, count):
        base = self.used
        self.used += count
        return base

    def make(self, src, dst, sem, dev, sent=None):
        return pltpu.make_async_remote_copy(
            src_ref=src,
            dst_ref=dst,
            send_sem=self.send.at[sem if sent is None else sent],
            recv_sem=self.recv.at[sem],
            device_id=dev,
            device_id_type=MESH,
        )

    def start(self, src, dst, sem, dev):
        copy = self.make(src, dst, sem, dev)
        copy.start()
        self.open.append(copy)

    def landed(self, dst, sem, dev):
        self.make(dst, dst, sem, dev).wait_recv()

    def finish(self):
        for item in self.open:
            if callable(item):
                item()
            else:
                item.wait_send()


def kernel(
    counts, pk, w1, w2p, b1, b2, gain, cot,
    emb, gw1, gw2,
    send, recv, lsem, starts, ends, srcs,
    sc, cc, g, nrm, sp, cp, xf, sqx,
    w1f, w2t,
    pg, zgr, zgl, og, oh,
    ht, gt,
    pe, ps, pr, sb, bk,
    g2, a2, c2, s2a, s2b, d2, e2, t2,
    g1, a1, c1, s1a, s1b, d1, e1, t1,
    i1, i2, k1, k2,
):
    r = lax.axis_index("dp")
    t = lax.axis_index("tensor")
    m, c = lax.div(r, 2), lax.rem(r, 2)
    X, Y = lax.rem(m, 4), lax.div(m, 4)
    a, b = lax.div(m, 2), lax.rem(m, 2)
    links = Copies(send, recv)

    def plane(chip):
        return (2 * chip + c, t)

    def along_x(d):
        return plane(4 * Y + up(X + d, 4))

    def along_y(d):
        return plane(4 * up(Y + d, 4) + X)

    sibling = (2 * m + 1 - c, t)
    right, left = (r, up(t + 1, TP)), (r, up(t - 1, TP))
    mid_chip, old_chip = lax.rem(m + 2 * t, CHIPS), up(m - 2 * t, CHIPS)
    mate = up(a - t, TP)
    same, still = mate == t, t == 0

    barrier = pltpu.get_barrier_semaphore()

    def greet(dev):
        pl.semaphore_signal(barrier, inc=1, device_id=dev, device_id_type=MESH)

    for d in range(1, CHIPS):
        greet(plane(up(m + d, CHIPS)))
    for d in range(1, TP):
        greet((r, up(t + d, TP)))
    greet(sibling)

    @pl.when(jnp.logical_not(same))
    def _():
        greet((2 * m + 1 - c, mate))

    def prefix(s, total):
        starts[s] = total
        total = total + counts[s]
        ends[s] = total
        return total

    lax.fori_loop(0, DP, prefix, jnp.int32(0))
    mine_start, mine_count = starts[r], counts[r]

    def pack_cot(p, carry):
        sc[p] = cot[up(p - mine_start + 1024, SLOTS)]
        return carry

    lax.fori_loop(0, DP, pack_cot, 0)

    lane = lax.broadcasted_iota(jnp.int32, (8, FEAT), 1)
    row = lax.broadcasted_iota(jnp.int32, (8, FEAT), 0)
    lead = jnp.logical_and(lane >= row * 160, lane < row * 160 + 160)
    pick = jnp.where(lead, 1.0, 0.0).astype(F32)
    pick_bf = pick.astype(BF)
    for i in range(4):
        v = pk[8 * i : 8 * i + 8].reshape(128, FEAT).astype(F32)
        sq = v * v
        high = sq.astype(BF)
        low = (sq - high.astype(F32)).astype(BF)
        sqx[t, :, 128 * i : 128 * i + 128] = dot(pick_bf, high, NT) + dot(pick_bf, low, NT)

    pl.semaphore_wait(barrier, 23 + jnp.where(same, 0, 1))

    sq_base = links.take(TP)
    for d in range(1, TP):
        links.start(sqx.at[t], sqx.at[t], sq_base + d, (r, up(t + d, TP)))

    relay = links.take(2)
    relay1 = links.take(1)
    relay_mid = links.take(2)

    def relay_in(e):
        return w2t.at[Y, lax.div(X, 2), :, pl.ds(pl.multiple_of(b * 256 + e * 128, 128), 128)]

    def relay_steps(do):
        @pl.when(jnp.logical_not(still))
        def _():
            do(links.make(w2p, i2, relay_mid, plane(mid_chip)))
            do(links.make(w1, i1, relay_mid + 1, plane(mid_chip)))

    def relay_along_z(do):
        @pl.when(jnp.logical_not(same))
        def _():
            for e in range(2):
                do(links.make(i2.at[e], relay_in(c), relay + c, (2 * m + e, mate), relay + e))
            do(links.make(i1, w1f.at[Y, X], relay1, (r, mate)))

        @pl.when(same)
        def _():
            do(links.make(i2.at[1 - c], relay_in(c), relay + c, sibling, relay + 1 - c))

    relay_steps(lambda copy: copy.start())

    @pl.when(still)
    def _():
        i2[...] = w2p[...]
        i1[...] = w1[...]

    links.open.append(lambda: relay_steps(lambda copy: copy.wait_send()))
    links.open.append(lambda: relay_along_z(lambda copy: copy.wait_send()))

    def exchange(out, into, base):
        def step(d, carry):
            chip = up(m + d, CHIPS)
            links.make(out.at[pl.ds(2 * chip, 2)], into.at[m], base + d, plane(chip)).start()
            return carry

        lax.fori_loop(1, CHIPS, step, 0)

        def sent(d, carry):
            chip = up(m + d, CHIPS)
            links.make(out.at[pl.ds(2 * chip, 2)], into.at[m], base + d, plane(chip)).wait_send()
            return carry

        links.open.append(lambda: lax.fori_loop(1, CHIPS, sent, 0))
        into[m] = out[pl.ds(2 * m, 2)]

    def exchanged(into, base):
        def step(d, carry):
            links.landed(into.at[up(m - d, CHIPS)], base + d, plane(up(m - d, CHIPS)))
            return carry

        lax.fori_loop(1, CHIPS, step, 0)


    def gather_first(block_a, block_b, base):
        for d in range(1, 4):
            links.start(block_a, block_a, base + d, along_x(d))
            links.start(block_b, block_b, base + 3 + d, along_y(d))

    w1a = w1f.at[Y, X, 0:W1A]
    w1b = w1f.at[Y, X, W1A:80]
    w1_base = links.take(16)
    w2_base = links.take(16)
    w2lane = pl.ds(pl.multiple_of(b * 256, 256), 256)
    xh = lax.div(X, 2)
    w2a = w2t.at[Y, xh, 0:80, w2lane]
    w2b = w2t.at[Y, xh, 80:160, w2lane]

    def gather_second(wide_a, wide_b, arrived, base):
        for d in range(1, 4):
            ra, rb = arrived(d)
            links.landed(ra, base + d, along_x(-d))
            links.landed(rb, base + 3 + d, along_y(-d))
        for d in range(1, 4):
            links.start(wide_a, wide_a, base + 6 + d, along_y(d))
            links.start(wide_b, wide_b, base + 9 + d, along_x(d))

    def w2_first(d):
        xx, yy = up(X - d, 4), up(Y - d, 4)
        ra = w2t.at[Y, lax.div(xx, 2), 0:80, pl.ds(pl.multiple_of(lax.rem(xx, 2) * 256, 256), 256)]
        rb = w2t.at[yy, xh, 80:160, w2lane]
        return ra, rb

    def w1_first(d):
        return w1f.at[Y, up(X - d, 4), 0:W1A], w1f.at[up(Y - d, 4), X, W1A:80]

    def source(k, carry):
        p0 = 32 * k + 2 * m
        n0, n1 = jnp.int32(0), jnp.int32(0)
        for s in range(DP):
            v = ends[s]
            n0 = n0 + (v <= p0).astype(jnp.int32)
            n1 = n1 + (v <= p0 + 1).astype(jnp.int32)
        srcs[k] = jnp.minimum(n0, DP - 1)
        srcs[16 + k] = jnp.minimum(n1, DP - 1)
        return carry

    lax.fori_loop(0, 16, source, 0)

    for d in range(1, TP):
        z = up(t - d, TP)
        links.landed(sqx.at[z], sq_base + d, (r, z))
    total = sqx[0]
    for z in range(1, TP):
        total = total + sqx[z]
    inv = lax.rsqrt(total / D + 1e-06)
    part1 = inv.astype(BF).astype(F32)
    part2 = (inv - part1).astype(BF).astype(F32)
    stack = jnp.concatenate([part1, part2, (inv - part1) - part2], axis=0)
    stack_t = stack.T.astype(BF)
    pick3 = jnp.concatenate([pick, pick, pick], axis=0).astype(BF)
    gains = gain[...]
    for i in range(4):
        scale = dot(stack_t[128 * i : 128 * i + 128], pick3, NN)
        v = pk[8 * i : 8 * i + 8].reshape(128, FEAT).astype(F32)
        nrm[8 * i : 8 * i + 8] = (v * scale * gains).astype(BF).reshape(8, ROWS, FEAT)

    def pack_rows(p, carry):
        sp[p] = nrm[up(p - mine_start + 1024, SLOTS)]
        return carry

    lax.fori_loop(0, DP, pack_rows, 0)
    row_base = links.take(CHIPS)
    exchange(sp, cp.at[c], row_base)

    @pl.when(jnp.logical_not(still))
    def _():
        links.landed(i2, relay_mid, plane(old_chip))
        links.landed(i1, relay_mid + 1, plane(old_chip))

    relay_along_z(lambda copy: copy.start())

    @pl.when(same)
    def _():
        w1f[Y, X] = i1[...]
        own = pltpu.make_async_copy(i2.at[c], relay_in(c), lsem)
        own.start()
        own.wait()

    exchanged(cp.at[c], row_base)
    row_sib = links.take(1)
    links.start(cp.at[c, :, 1 - c], cp.at[c, :, 1 - c], row_sib, sibling)

    cot_base = links.take(CHIPS)
    exchange(sc, cc.at[c], cot_base)

    links.landed(cp.at[1 - c, :, c], row_sib, sibling)

    def choose_rows(k, carry):
        s = srcs[16 * c + k]
        xf[t, 16 * c + k] = cp[lax.rem(s, 2), lax.div(s, 2), c]
        return carry

    lax.fori_loop(0, 16, choose_rows, 0)

    def ring_sum(part, rr, rl, base, s):
        br, bl = up(t + 4 - s, TP), up(t - 4 + s, TP)
        for u in range(2):
            k = base + 8 * u
            w = slice(256 * u, 256 * u + 256)
            if s == 0:
                links.start(part.at[br, 0:80, w], rr.at[0, 0:80, w], k, right)
                links.start(part.at[bl, 80:160, w], rl.at[0, 80:160, w], k + 4, left)
                continue
            lo, hi = (slice(0, 80), slice(80, 160)) if s == 1 else (slice(0, 160),) * 2
            links.landed(rr.at[s - 1, lo, w], k + s - 1, left)
            part[br, lo, w] = (part[br, lo, w].astype(F32) + rr[s - 1, lo, w].astype(F32)).astype(BF)
            links.start(part.at[br, :, w], rr.at[s, :, w], k + s, right)
            links.landed(rl.at[s - 1, hi, w], k + 4 + s - 1, right)
            part[bl, hi, w] = (part[bl, hi, w].astype(F32) + rl[s - 1, hi, w].astype(F32)).astype(BF)
            links.start(part.at[bl, :, w], rl.at[s, :, w], k + 4 + s, left)

    def ring_end(rr, rl, base, u):
        w = slice(256 * u, 256 * u + 256)
        links.landed(rr.at[3, :, w], base + 8 * u + 3, left)
        links.landed(rl.at[3, :, w], base + 8 * u + 7, right)

    def ring_copy(buf, base, s):
        br, bl = up(t - s, TP), up(t + s, TP)
        for u in range(2):
            k = base + 8 * u
            w = slice(256 * u, 256 * u + 256)
            if s > 0:
                links.landed(buf.at[br, :, w], k + s - 1, left)
            lo, hi = (slice(0, 160),) * 2 if s < 3 else (slice(0, 80), slice(80, 160))
            links.start(buf.at[br, lo, w], buf.at[br, lo, w], k + s, right)
            if s > 0:
                links.landed(buf.at[bl, :, w], k + 4 + s - 1, right)
            links.start(buf.at[bl, hi, w], buf.at[bl, hi, w], k + 4 + s, left)

    def ring_copied(buf, base):
        far = up(t + 4, TP)
        for u in range(2):
            w = slice(256 * u, 256 * u + 256)
            links.landed(buf.at[far, 0:80, w], base + 8 * u + 3, left)
            links.landed(buf.at[far, 80:160, w], base + 8 * u + 7, right)

    def around(s, work):
        def step(i, carry):
            work(up(t + (2 * i - 1) * s, TP))
            return carry

        lax.fori_loop(0, 2, step, 0)

    x_base = links.take(16)
    xs_base = links.take(18)

    def rows_of(z, u, start, size):
        return xf.at[z, pl.ds(16 * c + 8 * u + start, size)]

    def hand_over(z, u):
        ref = rows_of(z, u, 0, 8)
        links.start(ref, ref, xs_base + 2 * z + u, sibling)

    def handed(z):
        for u in range(2):
            links.landed(xf.at[z, pl.ds(16 * (1 - c) + 8 * u, 8)], xs_base + 2 * z + u, sibling)

    def ring_rows(s):
        br, bl = up(t - s, TP), up(t + s, TP)
        for u in range(2):
            k = x_base + 8 * u
            size = 8 if s < 3 else 4
            if s > 0:
                links.landed(rows_of(br, u, 0, 8), k + s - 1, left)
            ref = rows_of(br, u, 0, size)
            links.start(ref, ref, k + s, right)
            if s > 0:
                links.landed(rows_of(bl, u, 0, 8), k + 4 + s - 1, right)
            ref = rows_of(bl, u, 8 - size, size)
            links.start(ref, ref, k + 4 + s, left)
            hand_over(br, u)
            if s > 0:
                hand_over(bl, u)

    def ring_rows_end():
        far = up(t + 4, TP)
        for u in range(2):
            links.landed(rows_of(far, u, 0, 4), x_base + 8 * u + 3, left)
            ref = rows_of(far, u, 0, 4)
            links.start(ref, ref, xs_base + 2 * far + u, sibling)
            links.landed(rows_of(far, u, 4, 4), x_base + 8 * u + 7, right)
            ref = rows_of(far, u, 4, 4)
            links.start(ref, ref, xs_base + 16 + u, sibling)

    ring_rows(0)

    for e in range(2):

        @pl.when(jnp.logical_or(jnp.logical_not(same), e != c))
        def _(e=e):
            links.landed(relay_in(e), relay + e, sibling)

    gather_first(w2a, w2b, w2_base)

    @pl.when(jnp.logical_not(same))
    def _():
        links.landed(w1f.at[Y, X], relay1, (r, mate))

    gather_first(w1a, w1b, w1_base)

    def place(z):
        return lax.rem(z + t, TP)

    def grad_block(z):
        p = place(z)
        return dot(w2t[lax.div(p, 2), lax.rem(p, 2)], g[...].reshape(TOK, OUTW), NT)

    def grad_store(z):
        pg[z] = grad_block(z).astype(BF)

    def pre_add(z):
        p = place(z)
        rows = w1f[lax.div(p, 2), pl.ds(2 * lax.rem(p, 2), 2)].reshape(UNITS, FEAT)
        oh[...] += dot(rows, xf[z].reshape(TOK, FEAT), NT)

    pg_base = links.take(16)
    ht_base = links.take(16)
    def activate(u):
        w = slice(256 * u, 256 * u + 256)

        def step(i, carry):
            rows = pl.ds(pl.multiple_of(i * 32, 32), 32)
            v = oh[rows, w]
            cdf = 0.5 * (1.0 + lax.erf(v * 0.7071067811865476))
            density = jnp.exp(-0.5 * v * v) * 0.3989422804014327
            ht[t, rows, w] = (v * cdf).astype(BF)
            oh[rows, w] = cdf + v * density
            return carry

        lax.fori_loop(0, 5, step, 0)

    def descend(u):
        w = slice(256 * u, 256 * u + 256)

        def step(i, carry):
            rows = pl.ds(pl.multiple_of(i * 32, 32), 32)
            v = og[rows, w] + zgr[3, rows, w].astype(F32) + zgl[3, rows, w].astype(F32)
            gt[rows, w] = (v * oh[rows, w]).astype(BF)
            return carry

        lax.fori_loop(0, 5, step, 0)

    ring_rows(1)
    exchanged(cc.at[c], cot_base)
    cot_sib = links.take(1)
    links.start(cc.at[c], cc.at[c], cot_sib, sibling)

    gather_second(w2t.at[Y, :, 0:80], w2t.at[:, xh, 80:160, w2lane], w2_first, w2_base)

    gather_second(w1f.at[Y, :, 0:W1A], w1f.at[:, X, W1A:80], w1_first, w1_base)
    ring_rows(2)
    links.landed(cc.at[1 - c], cot_sib, sibling)

    def choose(j, carry):
        s = srcs[j]
        g[j] = cc[lax.rem(s, 2), lax.div(s, 2), lax.div(j, 16)]
        return carry

    lax.fori_loop(0, 32, choose, 0)

    for d in range(1, 4):
        xx, yy = up(X - d, 4), up(Y - d, 4)
        links.landed(w2t.at[yy, :, 0:80], w2_base + 6 + d, along_y(-d))
        links.landed(
            w2t.at[:, lax.div(xx, 2), 80:160, pl.ds(pl.multiple_of(lax.rem(xx, 2) * 256, 256), 256)],
            w2_base + 9 + d,
            along_x(-d),
        )

    grad_store(up(t + 4, TP))
    ring_sum(pg, zgr, zgl, pg_base, 0)
    around(3, grad_store)
    ring_rows(3)
    ring_sum(pg, zgr, zgl, pg_base, 1)
    around(2, grad_store)
    ring_sum(pg, zgr, zgl, pg_base, 2)
    around(1, grad_store)
    og[...] = grad_block(t)
    for d in range(1, 4):
        xx, yy = up(X - d, 4), up(Y - d, 4)
        links.landed(w1f.at[yy, :, 0:W1A], w1_base + 6 + d, along_y(-d))
        links.landed(w1f.at[:, xx, W1A:80], w1_base + 9 + d, along_x(-d))
    oh[...] = jnp.concatenate([b1[c]] * 4, axis=1)
    handed(t)
    pre_add(t)
    for s in range(1, 3):
        handed(up(t - s, TP))
        handed(up(t + s, TP))
        around(s, pre_add)
    ring_rows_end()
    handed(up(t - 3, TP))
    handed(up(t + 3, TP))
    around(3, pre_add)
    ring_sum(pg, zgr, zgl, pg_base, 3)
    far_rows = xf.at[up(t + 4, TP)]
    for u in range(2):
        for i in range(2):
            ref = far_rows.at[pl.ds(16 * (1 - c) + 8 * u + 4 * i, 4)]
            links.landed(ref, xs_base + (2 * up(t + 4, TP) if i == 0 else 16) + u, sibling)
    pre_add(up(t + 4, TP))

    for u in range(2):
        activate(u)
    ring_copy(ht, ht_base, 0)
    def plane_send(part, cut, ra, rb, base, z):
        yy, par = lax.div(z, 2), lax.rem(z, 2)
        dy = up(yy - Y, 4)

        @pl.when(dy != 0)
        def _():
            links.make(
                part.at[yy, pl.ds(2 * par, 2), 0:cut],
                ra.at[dy - 1, pl.ds(2 * par, 2)],
                base + 2 * (dy - 1) + par,
                along_y(dy),
            ).start()

        for i in range(2):
            xx = 2 * par + i
            dx = up(xx - X, 4)

            @pl.when(dx != 0)
            def _(xx=xx, dx=dx):
                links.make(
                    part.at[yy, xx, cut:],
                    rb.at[dx - 1, yy],
                    base + 6 + 4 * (dx - 1) + yy,
                    along_x(dx),
                ).start()

    def plane_sent(part, cut, ra, rb, sa, sbx, rc, rd, base):
        def waits():
            for d in range(3):
                for i in range(2):
                    links.make(part.at[0, 0:2, 0:cut], ra.at[d, 0:2], base + 2 * d + i, along_y(1)).wait_send()
                for i in range(4):
                    links.make(part.at[0, 0, cut:], rb.at[d, 0], base + 6 + 4 * d + i, along_x(1)).wait_send()
                links.make(sa.at[0], rc.at[d], base + 19 + d, along_x(1)).wait_send()
                links.make(sbx.at[0], rd.at[d], base + 22 + d, along_y(1)).wait_send()

        links.open.append(waits)

    def plane_second(part, cut, ra, rb, sa, sbx, rc, rd, base, z):
        p = place(z)
        yy, par = lax.div(p, 2), lax.rem(p, 2)

        @pl.when(Y == yy)
        def _():
            for d in range(3):
                links.landed(ra.at[d, pl.ds(2 * par, 2)], base + 2 * d + par, along_y(-d - 1))
            for i in range(2):
                xx = 2 * par + i
                v = part[yy, xx, 0:cut].astype(F32)
                for d in range(3):
                    v = v + ra[d, xx].astype(F32)
                sa[xx] = v.astype(BF)
                dx = up(xx - X, 4)

                @pl.when(dx != 0)
                def _(xx=xx, dx=dx):
                    links.make(sa.at[xx], rc.at[dx - 1], base + 18 + dx, along_x(dx)).start()

        @pl.when(lax.div(X, 2) == par)
        def _():
            for d in range(3):
                links.landed(rb.at[d, yy], base + 6 + 4 * d + yy, along_x(-d - 1))
            v = part[yy, X, cut:].astype(F32)
            for d in range(3):
                v = v + rb[d, yy].astype(F32)
            sbx[yy] = v.astype(BF)
            dy = up(yy - Y, 4)

            @pl.when(dy != 0)
            def _():
                links.make(sbx.at[yy], rd.at[dy - 1], base + 21 + dy, along_y(dy)).start()

    def plane_sum_end(sa, sbx, rc, rd, base):
        for d in range(1, 4):
            links.landed(rc.at[d - 1], base + 18 + d, along_x(-d))
        va = sa[X].astype(F32)
        for d in range(3):
            va = va + rc[d].astype(F32)
        for d in range(1, 4):
            links.landed(rd.at[d - 1], base + 21 + d, along_y(-d))
        vb = sbx[Y].astype(F32)
        for d in range(3):
            vb = vb + rd[d].astype(F32)
        return va.astype(BF), vb.astype(BF)

    g2_base = links.take(25)

    def second_grad(z):
        p = place(z)
        v = dot(ht[z], g[...].reshape(TOK, OUTW), NN).astype(BF)
        for i in range(2):
            g2[lax.div(p, 2), 2 * lax.rem(p, 2) + i] = v[:, 256 * i : 256 * i + 256]
        plane_send(g2, 80, a2, c2, g2_base, p)

    def second_second(z):
        plane_second(g2, 80, a2, c2, s2a, s2b, d2, e2, g2_base, z)

    def embed(z):
        p = place(z)

        def step(i, carry):
            lanes = pl.ds(pl.multiple_of(i * 128, 128), 128)
            rows = ht[z, :, lanes].astype(F32).T.astype(BF)
            v = dot(rows, w2t[lax.div(p, 2), lax.rem(p, 2)], NN)
            pe[pl.ds(8 * i, 8)] += v.reshape(8, ROWS, OUTW)
            return carry

        lax.fori_loop(0, 4, step, 0)

    def use_hidden(z):
        second_grad(z)
        embed(z)

    plane_sent(g2, 80, a2, c2, s2a, s2b, d2, e2, g2_base)

    g1_base = links.take(25)

    def first_grad(z):
        p = place(z)
        v = dot(gt[...], xf[z].reshape(TOK, FEAT), NN).astype(BF)
        for i in range(2):
            g1[lax.div(p, 2), 2 * lax.rem(p, 2) + i] = v[80 * i : 80 * i + 80]
        plane_send(g1, W1A, a1, c1, g1_base, p)

    plane_sent(g1, W1A, a1, c1, s1a, s1b, d1, e1, g1_base)
    def first_second(z):
        plane_second(g1, W1A, a1, c1, s1a, s1b, d1, e1, g1_base, z)

    for u in range(2):
        ring_end(zgr, zgl, pg_base, u)
        descend(u)

    lax.fori_loop(0, TP, lambda z, carry: (first_grad(z), carry)[1], 0)
    pe[...] = jnp.zeros_like(pe)
    use_hidden(t)
    ring_copy(ht, ht_base, 1)
    around(1, use_hidden)
    ring_copy(ht, ht_base, 2)
    around(2, use_hidden)
    ring_copy(ht, ht_base, 3)
    lax.fori_loop(0, TP, lambda z, carry: (first_second(z), carry)[1], 0)

    around(3, use_hidden)
    second_second(t)
    around(1, second_second)
    va, vb = plane_sum_end(s1a, s1b, d1, e1, g1_base)
    t1[0:W1A] = va
    t1[W1A:80] = vb
    back1 = links.take(2)

    def back1_z(do):
        @pl.when(jnp.logical_not(same))
        def _():
            do(links.make(t1, k1, back1, (r, mate)))

    back1_z(lambda copy: copy.start())

    @pl.when(same)
    def _():
        k1[...] = t1[...]

    links.open.append(lambda: back1_z(lambda copy: copy.wait_send()))

    ring_copied(ht, ht_base)
    use_hidden(up(t + 4, TP))

    def window_of(s, e):
        first = starts[s]
        slot = lax.rem(2 * m + e - first + 1024, SLOTS)
        return e * 16 + jnp.minimum(lax.div(first + slot, 32), 15)

    def pack_sibling(i, carry):
        for e in range(2):
            ps[2 * i + e] = pe[window_of(2 * i + 1 - c, e)].astype(BF)
        return carry

    lax.fori_loop(0, CHIPS, pack_sibling, 0)
    emb_sib = links.take(1)
    links.start(ps, pr, emb_sib, sibling)

    around(2, second_second)
    @pl.when(jnp.logical_not(same))
    def _():
        links.landed(k1, back1, (r, mate))

    def back1_plane(do):
        @pl.when(jnp.logical_not(still))
        def _():
            do(links.make(k1, gw1, back1 + 1, plane(old_chip)))

    back1_plane(lambda copy: copy.start())

    @pl.when(still)
    def _():
        gw1[...] = k1[...]

    links.open.append(lambda: back1_plane(lambda copy: copy.wait_send()))

    links.landed(pr, emb_sib, sibling)
    bias2 = b2[...]

    def pack_home(i, carry):
        for e in range(2):
            v = pe[window_of(2 * i + c, e)] + pr[2 * i + e].astype(F32) + bias2
            sb[2 * i + e] = v.astype(BF)
        return carry

    lax.fori_loop(0, CHIPS, pack_home, 0)
    home_base = links.take(CHIPS)
    exchange(sb, bk, home_base)

    around(3, second_second)
    second_second(up(t + 4, TP))
    va, vb = plane_sum_end(s2a, s2b, d2, e2, g2_base)
    for e in range(2):
        t2[e, 0:80] = va[:, 128 * e : 128 * e + 128]
        t2[e, 80:160] = vb[:, 128 * e : 128 * e + 128]
    back = links.take(3)

    def back_z(do):
        @pl.when(jnp.logical_not(same))
        def _():
            for e in range(2):
                do(links.make(t2.at[e], k2.at[c], back + c, (2 * m + e, mate), back + e))

        @pl.when(same)
        def _():
            do(links.make(t2.at[1 - c], k2.at[c], back + c, sibling, back + 1 - c))

    back_z(lambda copy: copy.start())

    @pl.when(same)
    def _():
        k2[c] = t2[c]

    links.open.append(lambda: back_z(lambda copy: copy.wait_send()))

    for e in range(2):

        @pl.when(jnp.logical_or(jnp.logical_not(same), e != c))
        def _(e=e):
            links.landed(k2.at[e], back + e, (2 * m + e, mate))

    def back_plane(do):
        @pl.when(jnp.logical_not(still))
        def _():
            do(links.make(k2, gw2, back + 2, plane(old_chip)))

    back_plane(lambda copy: copy.start())

    @pl.when(still)
    def _():
        gw2[...] = k2[...]

    links.open.append(lambda: back_plane(lambda copy: copy.wait_send()))

    exchanged(bk, home_base)

    def home(j, carry):
        p = lax.rem(mine_start + j, DP)
        v = bk[lax.div(p, 2), lax.rem(p, 2)].astype(F32)
        emb[j] = jnp.where(j < mine_count, v, 0.0).astype(BF)
        return carry

    lax.fori_loop(0, SLOTS, home, 0)

    @pl.when(jnp.logical_not(still))
    def _():
        links.landed(gw1, back1 + 1, plane(mid_chip))
        links.landed(gw2, back + 2, plane(mid_chip))

    links.finish()


def on_device(patches, norm_gain, w_first, b_first, w_second, b_second, counts, cotangent):
    pk = patches.reshape(SLOTS, ROWS, FEAT)
    w1 = w_first.reshape(80, FEAT)
    w2p = w_second.T.reshape(2, 2, 80, 128).transpose(1, 0, 2, 3).reshape(2, UNITS, 128)
    b1 = b_first.astype(F32).reshape(2, 2, 80).transpose(1, 0, 2).reshape(2, UNITS, 1)
    b1 = jnp.broadcast_to(b1, (2, UNITS, 128))
    b2 = b_second.astype(F32).reshape(1, OUTW)
    gain = jnp.tile(norm_gain.astype(F32).reshape(1, 160), (1, 4))
    cot = cotangent.reshape(SLOTS, ROWS, OUTW)

    vmem = pl.BlockSpec(memory_space=pltpu.VMEM)
    V = pltpu.VMEM
    S = pltpu.SMEM
    emb, gw1, gw2 = pl.pallas_call(
        kernel,
        name="merger",
        out_shape=(
            jax.ShapeDtypeStruct((SLOTS, ROWS, OUTW), BF),
            jax.ShapeDtypeStruct((80, FEAT), BF),
            jax.ShapeDtypeStruct((2, UNITS, 128), BF),
        ),
        in_specs=[pl.BlockSpec(memory_space=pltpu.SMEM)] + [vmem] * 7,
        out_specs=(vmem, vmem, vmem),
        scratch_shapes=[
            pltpu.SemaphoreType.DMA((256,)),
            pltpu.SemaphoreType.DMA((256,)),
            pltpu.SemaphoreType.DMA,
            S((DP,), jnp.int32),
            S((DP,), jnp.int32),
            S((DP,), jnp.int32),
            V((DP, ROWS, OUTW), BF),
            V((2, CHIPS, 2, ROWS, OUTW), BF),
            V((32, ROWS, OUTW), BF),
            V((SLOTS, ROWS, FEAT), BF),
            V((DP, ROWS, FEAT), BF),
            V((2, CHIPS, 2, ROWS, FEAT), BF),
            V((TP, 32, ROWS, FEAT), BF),
            V((TP, 8, TOK), F32),
            V((4, 4, 80, FEAT), BF),
            V((4, 2, UNITS, OUTW), BF),
            V((TP, UNITS, TOK), BF),
            V((4, UNITS, TOK), BF),
            V((4, UNITS, TOK), BF),
            V((UNITS, TOK), F32),
            V((UNITS, TOK), F32),
            V((TP, UNITS, TOK), BF),
            V((UNITS, TOK), BF),
            V((32, ROWS, OUTW), F32),
            V((32, ROWS, OUTW), BF),
            V((32, ROWS, OUTW), BF),
            V((32, ROWS, OUTW), BF),
            V((CHIPS, 2, ROWS, OUTW), BF),
            V((4, 4, UNITS, 256), BF),
            V((3, 4, 80, 256), BF),
            V((3, 4, 80, 256), BF),
            V((4, 80, 256), BF),
            V((4, 80, 256), BF),
            V((3, 80, 256), BF),
            V((3, 80, 256), BF),
            V((2, UNITS, 128), BF),
            V((4, 4, 80, FEAT), BF),
            V((3, 4, W1A, FEAT), BF),
            V((3, 4, 80 - W1A, FEAT), BF),
            V((4, W1A, FEAT), BF),
            V((4, 80 - W1A, FEAT), BF),
            V((3, W1A, FEAT), BF),
            V((3, 80 - W1A, FEAT), BF),
            V((80, FEAT), BF),
            V((80, FEAT), BF),
            V((2, UNITS, 128), BF),
            V((80, FEAT), BF),
            V((2, UNITS, 128), BF),
        ],
        compiler_params=pltpu.CompilerParams(
            collective_id=0, has_side_effects=True, vmem_limit_bytes=56 * 1024 * 1024
        ),
        cost_estimate=pl.CostEstimate(
            flops=3_700_000_000, bytes_accessed=3_000_000, transcendentals=200_000
        ),
    )(counts, pk, w1, w2p, b1, b2, gain, cot)
    embeddings = emb.reshape(SLOTS * ROWS, OUTW)
    grad_w1 = gw1.reshape(80, 4, 160)
    grad_w2 = gw2.reshape(2, 2, 80, 128).transpose(3, 1, 0, 2).reshape(128, 320)
    return embeddings, grad_w1, grad_w2


def solution(mesh):
    in_specs = (
        P("dp", "tensor"),
        P("tensor"),
        P("dp", None, "tensor"),
        P("tensor"),
        P("dp", "tensor"),
        P("tensor"),
        P(),
        P("dp", "tensor"),
    )
    out_specs = (P("dp", "tensor"), P("dp", None, "tensor"), P("dp", "tensor"))
    return jax.shard_map(
        on_device, mesh=mesh, in_specs=in_specs, out_specs=out_specs, check_vma=False
    )
```

```python
import functools

import jax
import jax.numpy as jnp
from jax import lax
from jax.experimental import pallas as pl
from jax.experimental.pallas import tpu as pltpu
from jax.sharding import PartitionSpec as P

D = 1280
PATCH = 64
DP = 32
TP = 8
CHIPS = 16
SLOTS = 32
ROWS = PATCH // 4
TOK = 512
UNITS = 160
FEAT = 640
OUTW = 512
W1A = 48

MESH = pl.DeviceIdType.MESH
BF = jnp.bfloat16
F32 = jnp.float32
NT = (((1,), (1,)), ((), ()))
NN = (((1,), (0,)), ((), ()))
TN = (((0,), (0,)), ((), ()))


def dot(a, b, dims):
    return lax.dot_general(a, b, dims, preferred_element_type=F32)


def up(index, size):
    return lax.rem(index + size, size)


class Copies:
    def __init__(self, send, recv):
        self.send, self.recv, self.used, self.open = send, recv, 0, []

    def take(self, count):
        base = self.used
        self.used += count
        return base

    def make(self, src, dst, sem, dev, sent=None):
        return pltpu.make_async_remote_copy(
            src_ref=src,
            dst_ref=dst,
            send_sem=self.send.at[sem if sent is None else sent],
            recv_sem=self.recv.at[sem],
            device_id=dev,
            device_id_type=MESH,
        )

    def start(self, src, dst, sem, dev):
        copy = self.make(src, dst, sem, dev)
        copy.start()
        self.open.append(copy)

    def landed(self, dst, sem, dev):
        self.make(dst, dst, sem, dev).wait_recv()

    def finish(self):
        for item in self.open:
            if callable(item):
                item()
            else:
                item.wait_send()


def kernel(
    counts, patches_t, w1, w2p, b1, b2, gain, cot,
    emb, gw1, gw2,
    send, recv, lsem, starts, ends, srcs,
    sc, cc, g, nrm, sp, cp, xf, sqx,
    w1f, w2t,
    pg, zgr, zgl, og, oh,
    ht, gt,
    pe, ps, pr, sb, bk,
    g2, a2, c2, s2a, s2b, d2, e2, t2,
    g1, a1, c1, s1a, s1b, d1, e1, t1,
    i1, i2, k1, k2, b1s, pk,
):
    r = lax.axis_index("dp")
    t = lax.axis_index("tensor")
    m, c = lax.div(r, 2), lax.rem(r, 2)
    X, Y = lax.rem(m, 4), lax.div(m, 4)
    a, b = lax.div(m, 2), lax.rem(m, 2)
    links = Copies(send, recv)

    def plane(chip):
        return (2 * chip + c, t)

    def along_x(d):
        return plane(4 * Y + up(X + d, 4))

    def along_y(d):
        return plane(4 * up(Y + d, 4) + X)

    sibling = (2 * m + 1 - c, t)
    right, left = (r, up(t + 1, TP)), (r, up(t - 1, TP))
    mid_chip, old_chip = lax.rem(m + 2 * t, CHIPS), up(m - 2 * t, CHIPS)
    mate = up(a - t, TP)
    same, still = mate == t, t == 0

    barrier = pltpu.get_barrier_semaphore()

    def greet(dev):
        pl.semaphore_signal(barrier, inc=1, device_id=dev, device_id_type=MESH)

    for d in range(1, CHIPS):
        greet(plane(up(m + d, CHIPS)))
    for d in range(1, TP):
        greet((r, up(t + d, TP)))
    greet(sibling)

    @pl.when(jnp.logical_not(same))
    def _():
        greet((2 * m + 1 - c, mate))

    def prefix(s, total):
        starts[s] = total
        total = total + counts[s]
        ends[s] = total
        return total

    lax.fori_loop(0, DP, prefix, jnp.int32(0))
    mine_start, mine_count = starts[r], counts[r]

    def pack_cot(p, carry):
        sc[p] = cot[up(p - mine_start + 1024, SLOTS)]
        return carry

    lax.fori_loop(0, DP, pack_cot, 0)

    lane = lax.broadcasted_iota(jnp.int32, (8, FEAT), 1)
    row = lax.broadcasted_iota(jnp.int32, (8, FEAT), 0)
    lead = jnp.logical_and(lane >= row * 160, lane < row * 160 + 160)
    pick = jnp.where(lead, 1.0, 0.0).astype(F32)
    pick_bf = pick.astype(BF)
    line = lax.broadcasted_iota(jnp.int32, (256, 256), 0)
    col = lax.broadcasted_iota(jnp.int32, (256, 256), 1)
    order = jnp.where(col == 4 * lax.rem(line, 64) + lax.div(line, 64), 1.0, 0.0).astype(BF)
    for i in range(4):
        halves = []
        for j in range(2):
            at = 512 * i + 256 * j
            v = dot(order, patches_t[:, at : at + 256], NT)
            halves.append(jnp.concatenate([v[64 * p : 64 * p + 64] for p in range(4)], axis=1))
        v = jnp.concatenate(halves, axis=0)
        pk[8 * i : 8 * i + 8] = v.astype(BF).reshape(8, ROWS, FEAT)
        sq = v * v
        high = sq.astype(BF)
        low = (sq - high.astype(F32)).astype(BF)
        sqx[t, :, 128 * i : 128 * i + 128] = dot(pick_bf, high, NT) + dot(pick_bf, low, NT)
    gains = jnp.concatenate([gain[...].astype(F32).reshape(1, 160)] * 4, axis=1)
    b1s[...] = jnp.broadcast_to(b1[...].astype(F32).reshape(1, 320), (128, 320)).T.reshape(2, 2, 80, 128)

    pl.semaphore_wait(barrier, 23 + jnp.where(same, 0, 1))

    sq_base = links.take(TP)
    for d in range(1, TP):
        links.start(sqx.at[t], sqx.at[t], sq_base + d, (r, up(t + d, TP)))

    relay = links.take(2)
    relay1 = links.take(1)
    relay_mid = links.take(2)

    def relay_in(e):
        return w2t.at[Y, lax.div(X, 2), :, pl.ds(pl.multiple_of(b * 256 + e * 128, 128), 128)]

    def relay_steps(do):
        @pl.when(jnp.logical_not(still))
        def _():
            do(links.make(w2p, i2, relay_mid, plane(mid_chip)))
            do(links.make(w1, i1, relay_mid + 1, plane(mid_chip)))

    def relay_along_z(do):
        @pl.when(jnp.logical_not(same))
        def _():
            for e in range(2):
                do(links.make(i2.at[e], relay_in(c), relay + c, (2 * m + e, mate), relay + e))
            do(links.make(i1, w1f.at[Y, X], relay1, (r, mate)))

        @pl.when(same)
        def _():
            do(links.make(i2.at[1 - c], relay_in(c), relay + c, sibling, relay + 1 - c))

    relay_steps(lambda copy: copy.start())

    @pl.when(still)
    def _():
        i2[...] = w2p[...]
        i1[...] = w1[...]

    links.open.append(lambda: relay_steps(lambda copy: copy.wait_send()))
    links.open.append(lambda: relay_along_z(lambda copy: copy.wait_send()))

    def exchange(out, into, base):
        def step(d, carry):
            chip = up(m + d, CHIPS)
            links.make(out.at[pl.ds(2 * chip, 2)], into.at[m], base + d, plane(chip)).start()
            return carry

        lax.fori_loop(1, CHIPS, step, 0)

        def sent(d, carry):
            chip = up(m + d, CHIPS)
            links.make(out.at[pl.ds(2 * chip, 2)], into.at[m], base + d, plane(chip)).wait_send()
            return carry

        links.open.append(lambda: lax.fori_loop(1, CHIPS, sent, 0))
        into[m] = out[pl.ds(2 * m, 2)]

    def exchanged(into, base):
        def step(d, carry):
            links.landed(into.at[up(m - d, CHIPS)], base + d, plane(up(m - d, CHIPS)))
            return carry

        lax.fori_loop(1, CHIPS, step, 0)


    def gather_first(block_a, block_b, base):
        for d in range(1, 4):
            links.start(block_a, block_a, base + d, along_x(d))
            links.start(block_b, block_b, base + 3 + d, along_y(d))

    w1a = w1f.at[Y, X, 0:W1A]
    w1b = w1f.at[Y, X, W1A:80]
    w1_base = links.take(16)
    w2_base = links.take(16)
    w2lane = pl.ds(pl.multiple_of(b * 256, 256), 256)
    xh = lax.div(X, 2)
    w2a = w2t.at[Y, xh, 0:80, w2lane]
    w2b = w2t.at[Y, xh, 80:160, w2lane]

    def gather_second(wide_a, wide_b, arrived, base):
        for d in range(1, 4):
            ra, rb = arrived(d)
            links.landed(ra, base + d, along_x(-d))
            links.landed(rb, base + 3 + d, along_y(-d))
        for d in range(1, 4):
            links.start(wide_a, wide_a, base + 6 + d, along_y(d))
            links.start(wide_b, wide_b, base + 9 + d, along_x(d))

    def w2_first(d):
        xx, yy = up(X - d, 4), up(Y - d, 4)
        ra = w2t.at[Y, lax.div(xx, 2), 0:80, pl.ds(pl.multiple_of(lax.rem(xx, 2) * 256, 256), 256)]
        rb = w2t.at[yy, xh, 80:160, w2lane]
        return ra, rb

    def w1_first(d):
        return w1f.at[Y, up(X - d, 4), 0:W1A], w1f.at[up(Y - d, 4), X, W1A:80]

    def source(k, carry):
        p0 = 32 * k + 2 * m
        n0, n1 = jnp.int32(0), jnp.int32(0)
        for s in range(DP):
            v = ends[s]
            n0 = n0 + (v <= p0).astype(jnp.int32)
            n1 = n1 + (v <= p0 + 1).astype(jnp.int32)
        srcs[k] = jnp.minimum(n0, DP - 1)
        srcs[16 + k] = jnp.minimum(n1, DP - 1)
        return carry

    lax.fori_loop(0, 16, source, 0)

    for d in range(1, TP):
        z = up(t - d, TP)
        links.landed(sqx.at[z], sq_base + d, (r, z))
    total = sqx[0]
    for z in range(1, TP):
        total = total + sqx[z]
    inv = lax.rsqrt(total / D + 1e-06)
    part1 = inv.astype(BF).astype(F32)
    part2 = (inv - part1).astype(BF).astype(F32)
    stack = jnp.concatenate([part1, part2, (inv - part1) - part2], axis=0)
    stack_t = stack.T.astype(BF)
    pick3 = jnp.concatenate([pick, pick, pick], axis=0).astype(BF)
    for i in range(4):
        scale = dot(stack_t[128 * i : 128 * i + 128], pick3, NN)
        v = pk[8 * i : 8 * i + 8].reshape(128, FEAT).astype(F32)
        nrm[8 * i : 8 * i + 8] = (v * scale * gains).astype(BF).reshape(8, ROWS, FEAT)

    def pack_rows(p, carry):
        sp[p] = nrm[up(p - mine_start + 1024, SLOTS)]
        return carry

    lax.fori_loop(0, DP, pack_rows, 0)
    row_base = links.take(CHIPS)
    exchange(sp, cp.at[c], row_base)

    @pl.when(jnp.logical_not(still))
    def _():
        links.landed(i2, relay_mid, plane(old_chip))
        links.landed(i1, relay_mid + 1, plane(old_chip))

    relay_along_z(lambda copy: copy.start())

    @pl.when(same)
    def _():
        w1f[Y, X] = i1[...]
        own = pltpu.make_async_copy(i2.at[c], relay_in(c), lsem)
        own.start()
        own.wait()

    for e in range(2):

        @pl.when(jnp.logical_or(jnp.logical_not(same), e != c))
        def _(e=e):
            links.landed(relay_in(e), relay + e, sibling)

    gather_first(w2a, w2b, w2_base)

    exchanged(cp.at[c], row_base)
    row_sib = links.take(1)
    links.start(cp.at[c, :, 1 - c], cp.at[c, :, 1 - c], row_sib, sibling)

    cot_base = links.take(CHIPS)
    exchange(sc, cc.at[c], cot_base)

    links.landed(cp.at[1 - c, :, c], row_sib, sibling)

    def choose_rows(k, carry):
        s = srcs[16 * c + k]
        xf[t, 16 * c + k] = cp[lax.rem(s, 2), lax.div(s, 2), c]
        return carry

    lax.fori_loop(0, 16, choose_rows, 0)

    def ring_sum(part, rr, rl, base, s):
        br, bl = up(t + 4 - s, TP), up(t - 4 + s, TP)
        for u in range(2):
            k = base + 8 * u
            w = slice(256 * u, 256 * u + 256)
            if s == 0:
                links.start(part.at[br, 0:80, w], rr.at[0, 0:80, w], k, right)
                links.start(part.at[bl, 80:160, w], rl.at[0, 80:160, w], k + 4, left)
                continue
            lo, hi = (slice(0, 80), slice(80, 160)) if s == 1 else (slice(0, 160),) * 2
            links.landed(rr.at[s - 1, lo, w], k + s - 1, left)
            part[br, lo, w] = (part[br, lo, w].astype(F32) + rr[s - 1, lo, w].astype(F32)).astype(BF)
            links.start(part.at[br, :, w], rr.at[s, :, w], k + s, right)
            links.landed(rl.at[s - 1, hi, w], k + 4 + s - 1, right)
            part[bl, hi, w] = (part[bl, hi, w].astype(F32) + rl[s - 1, hi, w].astype(F32)).astype(BF)
            links.start(part.at[bl, :, w], rl.at[s, :, w], k + 4 + s, left)

    def ring_end(rr, rl, base, u):
        w = slice(256 * u, 256 * u + 256)
        links.landed(rr.at[3, :, w], base + 8 * u + 3, left)
        links.landed(rl.at[3, :, w], base + 8 * u + 7, right)

    def ring_copy(buf, base, s):
        br, bl = up(t - s, TP), up(t + s, TP)
        for u in range(2):
            k = base + 8 * u
            w = slice(256 * u, 256 * u + 256)
            if s > 0:
                links.landed(buf.at[br, :, w], k + s - 1, left)
            lo, hi = (slice(0, 160),) * 2 if s < 3 else (slice(0, 80), slice(80, 160))
            links.start(buf.at[br, lo, w], buf.at[br, lo, w], k + s, right)
            if s > 0:
                links.landed(buf.at[bl, :, w], k + 4 + s - 1, right)
            links.start(buf.at[bl, hi, w], buf.at[bl, hi, w], k + 4 + s, left)

    def ring_copied(buf, base):
        far = up(t + 4, TP)
        for u in range(2):
            w = slice(256 * u, 256 * u + 256)
            links.landed(buf.at[far, 0:80, w], base + 8 * u + 3, left)
            links.landed(buf.at[far, 80:160, w], base + 8 * u + 7, right)

    def around(s, work):
        def step(i, carry):
            work(up(t + (2 * i - 1) * s, TP))
            return carry

        lax.fori_loop(0, 2, step, 0)

    x_base = links.take(16)
    xs_base = links.take(18)

    def rows_of(z, u, start, size):
        return xf.at[z, pl.ds(16 * c + 8 * u + start, size)]

    def hand_over(z, u):
        ref = rows_of(z, u, 0, 8)
        links.start(ref, ref, xs_base + 2 * z + u, sibling)

    def handed(z):
        for u in range(2):
            links.landed(xf.at[z, pl.ds(16 * (1 - c) + 8 * u, 8)], xs_base + 2 * z + u, sibling)

    def ring_rows(s):
        br, bl = up(t - s, TP), up(t + s, TP)
        for u in range(2):
            k = x_base + 8 * u
            size = 8 if s < 3 else 4
            if s > 0:
                links.landed(rows_of(br, u, 0, 8), k + s - 1, left)
            ref = rows_of(br, u, 0, size)
            links.start(ref, ref, k + s, right)
            if s > 0:
                links.landed(rows_of(bl, u, 0, 8), k + 4 + s - 1, right)
            ref = rows_of(bl, u, 8 - size, size)
            links.start(ref, ref, k + 4 + s, left)
            hand_over(br, u)
            if s > 0:
                hand_over(bl, u)

    def ring_rows_end():
        far = up(t + 4, TP)
        for u in range(2):
            links.landed(rows_of(far, u, 0, 4), x_base + 8 * u + 3, left)
            ref = rows_of(far, u, 0, 4)
            links.start(ref, ref, xs_base + 2 * far + u, sibling)
            links.landed(rows_of(far, u, 4, 4), x_base + 8 * u + 7, right)
            ref = rows_of(far, u, 4, 4)
            links.start(ref, ref, xs_base + 16 + u, sibling)

    ring_rows(0)

    gather_second(w2t.at[Y, :, 0:80], w2t.at[:, xh, 80:160, w2lane], w2_first, w2_base)

    @pl.when(jnp.logical_not(same))
    def _():
        links.landed(w1f.at[Y, X], relay1, (r, mate))

    gather_first(w1a, w1b, w1_base)

    def place(z):
        return lax.rem(z + t, TP)

    def grad_block(z):
        p = place(z)
        return dot(w2t[lax.div(p, 2), lax.rem(p, 2)], g[...].reshape(TOK, OUTW), NT)

    def grad_store(z):
        pg[z] = grad_block(z).astype(BF)

    def pre_add(z):
        p = place(z)
        rows = w1f[lax.div(p, 2), pl.ds(2 * lax.rem(p, 2), 2)].reshape(UNITS, FEAT)
        oh[...] += dot(rows, xf[z].reshape(TOK, FEAT), NT)

    pg_base = links.take(16)
    ht_base = links.take(16)
    def activate(u):
        w = slice(256 * u, 256 * u + 256)

        def step(i, carry):
            rows = pl.ds(pl.multiple_of(i * 32, 32), 32)
            v = oh[rows, w]
            cdf = 0.5 * (1.0 + lax.erf(v * 0.7071067811865476))
            density = jnp.exp(-0.5 * v * v) * 0.3989422804014327
            ht[t, rows, w] = (v * cdf).astype(BF)
            oh[rows, w] = cdf + v * density
            return carry

        lax.fori_loop(0, 5, step, 0)

    def descend(u):
        w = slice(256 * u, 256 * u + 256)

        def step(i, carry):
            rows = pl.ds(pl.multiple_of(i * 32, 32), 32)
            v = og[rows, w] + zgr[3, rows, w].astype(F32) + zgl[3, rows, w].astype(F32)
            gt[rows, w] = (v * oh[rows, w]).astype(BF)
            return carry

        lax.fori_loop(0, 5, step, 0)

    exchanged(cc.at[c], cot_base)
    cot_sib = links.take(1)
    links.start(cc.at[c], cc.at[c], cot_sib, sibling)

    ring_rows(1)
    links.landed(cc.at[1 - c], cot_sib, sibling)

    def choose(j, carry):
        s = srcs[j]
        g[j] = cc[lax.rem(s, 2), lax.div(s, 2), lax.div(j, 16)]
        return carry

    lax.fori_loop(0, 32, choose, 0)

    for d in range(1, 4):
        xx, yy = up(X - d, 4), up(Y - d, 4)
        links.landed(w2t.at[yy, :, 0:80], w2_base + 6 + d, along_y(-d))
        links.landed(
            w2t.at[:, lax.div(xx, 2), 80:160, pl.ds(pl.multiple_of(lax.rem(xx, 2) * 256, 256), 256)],
            w2_base + 9 + d,
            along_x(-d),
        )

    grad_store(up(t + 4, TP))
    ring_sum(pg, zgr, zgl, pg_base, 0)
    around(3, grad_store)
    gather_second(w1f.at[Y, :, 0:W1A], w1f.at[:, X, W1A:80], w1_first, w1_base)
    ring_rows(2)
    ring_sum(pg, zgr, zgl, pg_base, 1)
    around(2, grad_store)
    ring_rows(3)
    ring_sum(pg, zgr, zgl, pg_base, 2)
    around(1, grad_store)
    og[...] = grad_block(t)
    for d in range(1, 4):
        xx, yy = up(X - d, 4), up(Y - d, 4)
        links.landed(w1f.at[yy, :, 0:W1A], w1_base + 6 + d, along_y(-d))
        links.landed(w1f.at[:, xx, W1A:80], w1_base + 9 + d, along_x(-d))
    oh[...] = jnp.concatenate([b1s[:, c].reshape(UNITS, 128)] * 4, axis=1)
    handed(t)
    pre_add(t)
    for s in range(1, 3):
        handed(up(t - s, TP))
        handed(up(t + s, TP))
        around(s, pre_add)
    ring_sum(pg, zgr, zgl, pg_base, 3)
    ring_rows_end()
    handed(up(t - 3, TP))
    handed(up(t + 3, TP))
    around(3, pre_add)
    far_rows = xf.at[up(t + 4, TP)]
    for u in range(2):
        for i in range(2):
            ref = far_rows.at[pl.ds(16 * (1 - c) + 8 * u + 4 * i, 4)]
            links.landed(ref, xs_base + (2 * up(t + 4, TP) if i == 0 else 16) + u, sibling)
    pre_add(up(t + 4, TP))

    for u in range(2):
        activate(u)
    ring_copy(ht, ht_base, 0)
    def plane_send(part, cut, ra, rb, base, z):
        yy, par = lax.div(z, 2), lax.rem(z, 2)
        dy = up(yy - Y, 4)

        @pl.when(dy != 0)
        def _():
            links.make(
                part.at[yy, pl.ds(2 * par, 2), 0:cut],
                ra.at[dy - 1, pl.ds(2 * par, 2)],
                base + 2 * (dy - 1) + par,
                along_y(dy),
            ).start()

        for i in range(2):
            xx = 2 * par + i
            dx = up(xx - X, 4)

            @pl.when(dx != 0)
            def _(xx=xx, dx=dx):
                links.make(
                    part.at[yy, xx, cut:],
                    rb.at[dx - 1, yy],
                    base + 6 + 4 * (dx - 1) + yy,
                    along_x(dx),
                ).start()

    def plane_sent(part, cut, ra, rb, sa, sbx, rc, rd, base):
        def waits():
            for d in range(3):
                for i in range(2):
                    links.make(part.at[0, 0:2, 0:cut], ra.at[d, 0:2], base + 2 * d + i, along_y(1)).wait_send()
                for i in range(4):
                    links.make(part.at[0, 0, cut:], rb.at[d, 0], base + 6 + 4 * d + i, along_x(1)).wait_send()
                links.make(sa.at[0], rc.at[d], base + 19 + d, along_x(1)).wait_send()
                links.make(sbx.at[0], rd.at[d], base + 22 + d, along_y(1)).wait_send()

        links.open.append(waits)

    def plane_second(part, cut, ra, rb, sa, sbx, rc, rd, base, z):
        p = place(z)
        yy, par = lax.div(p, 2), lax.rem(p, 2)

        @pl.when(Y == yy)
        def _():
            for d in range(3):
                links.landed(ra.at[d, pl.ds(2 * par, 2)], base + 2 * d + par, along_y(-d - 1))
            for i in range(2):
                xx = 2 * par + i
                v = part[yy, xx, 0:cut].astype(F32)
                for d in range(3):
                    v = v + ra[d, xx].astype(F32)
                sa[xx] = v.astype(BF)
                dx = up(xx - X, 4)

                @pl.when(dx != 0)
                def _(xx=xx, dx=dx):
                    links.make(sa.at[xx], rc.at[dx - 1], base + 18 + dx, along_x(dx)).start()

        @pl.when(lax.div(X, 2) == par)
        def _():
            for d in range(3):
                links.landed(rb.at[d, yy], base + 6 + 4 * d + yy, along_x(-d - 1))
            v = part[yy, X, cut:].astype(F32)
            for d in range(3):
                v = v + rb[d, yy].astype(F32)
            sbx[yy] = v.astype(BF)
            dy = up(yy - Y, 4)

            @pl.when(dy != 0)
            def _():
                links.make(sbx.at[yy], rd.at[dy - 1], base + 21 + dy, along_y(dy)).start()

    def plane_sum_end(sa, sbx, rc, rd, base):
        for d in range(1, 4):
            links.landed(rc.at[d - 1], base + 18 + d, along_x(-d))
        va = sa[X].astype(F32)
        for d in range(3):
            va = va + rc[d].astype(F32)
        for d in range(1, 4):
            links.landed(rd.at[d - 1], base + 21 + d, along_y(-d))
        vb = sbx[Y].astype(F32)
        for d in range(3):
            vb = vb + rd[d].astype(F32)
        return va.astype(BF), vb.astype(BF)

    g2_base = links.take(25)

    def second_grad(z):
        p = place(z)
        v = dot(ht[z], g[...].reshape(TOK, OUTW), NN).astype(BF)
        for i in range(2):
            g2[lax.div(p, 2), 2 * lax.rem(p, 2) + i] = v[:, 256 * i : 256 * i + 256]
        plane_send(g2, 80, a2, c2, g2_base, p)

    def second_second(z):
        plane_second(g2, 80, a2, c2, s2a, s2b, d2, e2, g2_base, z)

    def embed(z):
        p = place(z)

        def step(i, carry):
            lanes = pl.ds(pl.multiple_of(i * 128, 128), 128)
            rows = ht[z, :, lanes].astype(F32).T.astype(BF)
            v = dot(rows, w2t[lax.div(p, 2), lax.rem(p, 2)], NN)
            pe[pl.ds(8 * i, 8)] += v.reshape(8, ROWS, OUTW)
            return carry

        lax.fori_loop(0, 4, step, 0)

    def use_hidden(z):
        second_grad(z)
        embed(z)

    plane_sent(g2, 80, a2, c2, s2a, s2b, d2, e2, g2_base)

    g1_base = links.take(25)

    def first_grad(z):
        p = place(z)
        v = dot(gt[...], xf[z].reshape(TOK, FEAT), NN).astype(BF)
        for i in range(2):
            g1[lax.div(p, 2), 2 * lax.rem(p, 2) + i] = v[80 * i : 80 * i + 80]
        plane_send(g1, W1A, a1, c1, g1_base, p)

    plane_sent(g1, W1A, a1, c1, s1a, s1b, d1, e1, g1_base)
    def first_second(z):
        plane_second(g1, W1A, a1, c1, s1a, s1b, d1, e1, g1_base, z)

    for u in range(2):
        ring_end(zgr, zgl, pg_base, u)
        descend(u)

    lax.fori_loop(0, TP, lambda z, carry: (first_grad(z), carry)[1], 0)
    pe[...] = jnp.zeros_like(pe)
    use_hidden(t)
    ring_copy(ht, ht_base, 1)
    around(1, use_hidden)
    ring_copy(ht, ht_base, 2)
    around(2, use_hidden)
    ring_copy(ht, ht_base, 3)
    around(3, use_hidden)
    lax.fori_loop(0, TP, lambda z, carry: (first_second(z), carry)[1], 0)

    ring_copied(ht, ht_base)
    use_hidden(up(t + 4, TP))

    def window_of(s, e):
        first = starts[s]
        slot = lax.rem(2 * m + e - first + 1024, SLOTS)
        return e * 16 + jnp.minimum(lax.div(first + slot, 32), 15)

    def pack_sibling(i, carry):
        for e in range(2):
            ps[2 * i + e] = pe[window_of(2 * i + 1 - c, e)].astype(BF)
        return carry

    lax.fori_loop(0, CHIPS, pack_sibling, 0)
    emb_sib = links.take(1)
    links.start(ps, pr, emb_sib, sibling)

    second_second(t)
    around(1, second_second)
    around(2, second_second)
    around(3, second_second)
    second_second(up(t + 4, TP))
    va, vb = plane_sum_end(s1a, s1b, d1, e1, g1_base)
    t1[0:W1A] = va
    t1[W1A:80] = vb
    back1 = links.take(2)

    def back1_z(do):
        @pl.when(jnp.logical_not(same))
        def _():
            do(links.make(t1, k1, back1, (r, mate)))

    back1_z(lambda copy: copy.start())

    @pl.when(same)
    def _():
        k1[...] = t1[...]

    links.open.append(lambda: back1_z(lambda copy: copy.wait_send()))

    va, vb = plane_sum_end(s2a, s2b, d2, e2, g2_base)
    for e in range(2):
        t2[e, 0:80] = va[:, 128 * e : 128 * e + 128]
        t2[e, 80:160] = vb[:, 128 * e : 128 * e + 128]
    back = links.take(3)

    def back_z(do):
        @pl.when(jnp.logical_not(same))
        def _():
            for e in range(2):
                do(links.make(t2.at[e], k2.at[c], back + c, (2 * m + e, mate), back + e))

        @pl.when(same)
        def _():
            do(links.make(t2.at[1 - c], k2.at[c], back + c, sibling, back + 1 - c))

    back_z(lambda copy: copy.start())

    @pl.when(same)
    def _():
        k2[c] = t2[c]

    links.open.append(lambda: back_z(lambda copy: copy.wait_send()))

    links.landed(pr, emb_sib, sibling)
    bias2 = b2[...].astype(F32).reshape(1, OUTW)

    def pack_home(i, carry):
        for e in range(2):
            v = pe[window_of(2 * i + c, e)] + pr[2 * i + e].astype(F32) + bias2
            sb[2 * i + e] = v.astype(BF)
        return carry

    lax.fori_loop(0, CHIPS, pack_home, 0)
    home_base = links.take(CHIPS)
    exchange(sb, bk, home_base)

    @pl.when(jnp.logical_not(same))
    def _():
        links.landed(k1, back1, (r, mate))

    def back1_plane(do):
        @pl.when(jnp.logical_not(still))
        def _():
            do(links.make(k1, gw1, back1 + 1, plane(old_chip)))

    back1_plane(lambda copy: copy.start())

    @pl.when(still)
    def _():
        gw1[...] = k1[...]

    links.open.append(lambda: back1_plane(lambda copy: copy.wait_send()))

    for e in range(2):

        @pl.when(jnp.logical_or(jnp.logical_not(same), e != c))
        def _(e=e):
            links.landed(k2.at[e], back + e, (2 * m + e, mate))

    def back_plane(do):
        @pl.when(jnp.logical_not(still))
        def _():
            do(links.make(k2, gw2, back + 2, plane(old_chip)))

    back_plane(lambda copy: copy.start())

    @pl.when(still)
    def _():
        gw2[...] = k2[...]

    links.open.append(lambda: back_plane(lambda copy: copy.wait_send()))

    exchanged(bk, home_base)

    def home(j, carry):
        p = lax.rem(mine_start + j, DP)
        v = bk[lax.div(p, 2), lax.rem(p, 2)].astype(F32)
        emb[j] = jnp.where(j < mine_count, v, 0.0).astype(BF)
        return carry

    lax.fori_loop(0, SLOTS, home, 0)

    @pl.when(jnp.logical_not(still))
    def _():
        links.landed(gw1, back1 + 1, plane(mid_chip))
        links.landed(gw2, back + 2, plane(mid_chip))

    links.finish()


def on_device(patches, norm_gain, w_first, b_first, w_second, b_second, counts, cotangent):
    patches_t = patches.T
    w1 = w_first.reshape(80, FEAT)
    w2p = w_second.T.reshape(2, 2, 80, 128).transpose(1, 0, 2, 3).reshape(2, UNITS, 128)
    cot = cotangent.reshape(SLOTS, ROWS, OUTW)

    vmem = pl.BlockSpec(memory_space=pltpu.VMEM)
    V = pltpu.VMEM
    S = pltpu.SMEM
    emb, gw1, gw2 = pl.pallas_call(
        kernel,
        name="merger",
        out_shape=(
            jax.ShapeDtypeStruct((SLOTS, ROWS, OUTW), BF),
            jax.ShapeDtypeStruct((80, FEAT), BF),
            jax.ShapeDtypeStruct((2, UNITS, 128), BF),
        ),
        in_specs=[pl.BlockSpec(memory_space=pltpu.SMEM)] + [vmem] * 7,
        out_specs=(vmem, vmem, vmem),
        scratch_shapes=[
            pltpu.SemaphoreType.DMA((256,)),
            pltpu.SemaphoreType.DMA((256,)),
            pltpu.SemaphoreType.DMA,
            S((DP,), jnp.int32),
            S((DP,), jnp.int32),
            S((DP,), jnp.int32),
            V((DP, ROWS, OUTW), BF),
            V((2, CHIPS, 2, ROWS, OUTW), BF),
            V((32, ROWS, OUTW), BF),
            V((SLOTS, ROWS, FEAT), BF),
            V((DP, ROWS, FEAT), BF),
            V((2, CHIPS, 2, ROWS, FEAT), BF),
            V((TP, 32, ROWS, FEAT), BF),
            V((TP, 8, TOK), F32),
            V((4, 4, 80, FEAT), BF),
            V((4, 2, UNITS, OUTW), BF),
            V((TP, UNITS, TOK), BF),
            V((4, UNITS, TOK), BF),
            V((4, UNITS, TOK), BF),
            V((UNITS, TOK), F32),
            V((UNITS, TOK), F32),
            V((TP, UNITS, TOK), BF),
            V((UNITS, TOK), BF),
            V((32, ROWS, OUTW), F32),
            V((32, ROWS, OUTW), BF),
            V((32, ROWS, OUTW), BF),
            V((32, ROWS, OUTW), BF),
            V((CHIPS, 2, ROWS, OUTW), BF),
            V((4, 4, UNITS, 256), BF),
            V((3, 4, 80, 256), BF),
            V((3, 4, 80, 256), BF),
            V((4, 80, 256), BF),
            V((4, 80, 256), BF),
            V((3, 80, 256), BF),
            V((3, 80, 256), BF),
            V((2, UNITS, 128), BF),
            V((4, 4, 80, FEAT), BF),
            V((3, 4, W1A, FEAT), BF),
            V((3, 4, 80 - W1A, FEAT), BF),
            V((4, W1A, FEAT), BF),
            V((4, 80 - W1A, FEAT), BF),
            V((3, W1A, FEAT), BF),
            V((3, 80 - W1A, FEAT), BF),
            V((80, FEAT), BF),
            V((80, FEAT), BF),
            V((2, UNITS, 128), BF),
            V((80, FEAT), BF),
            V((2, UNITS, 128), BF),
            V((2, 2, 80, 128), F32),
            V((SLOTS, ROWS, FEAT), BF),
        ],
        compiler_params=pltpu.CompilerParams(
            collective_id=0, has_side_effects=True, vmem_limit_bytes=56 * 1024 * 1024
        ),
        cost_estimate=pl.CostEstimate(
            flops=3_700_000_000, bytes_accessed=3_000_000, transcendentals=200_000
        ),
    )(counts, patches_t, w1, w2p, b_first, b_second, norm_gain, cot)
    embeddings = emb.reshape(SLOTS * ROWS, OUTW)
    grad_w1 = gw1.reshape(80, 4, 160)
    grad_w2 = gw2.reshape(2, 2, 80, 128).transpose(3, 1, 0, 2).reshape(128, 320)
    return embeddings, grad_w1, grad_w2


def solution(mesh):
    in_specs = (
        P("dp", "tensor"),
        P("tensor"),
        P("dp", None, "tensor"),
        P("tensor"),
        P("dp", "tensor"),
        P("tensor"),
        P(),
        P("dp", "tensor"),
    )
    out_specs = (P("dp", "tensor"), P("dp", None, "tensor"), P("dp", "tensor"))
    return jax.shard_map(
        on_device, mesh=mesh, in_specs=in_specs, out_specs=out_specs, check_vma=False
    )
```

```python
import functools

import jax
import jax.numpy as jnp
from jax import lax
from jax.experimental import pallas as pl
from jax.experimental.pallas import tpu as pltpu
from jax.sharding import PartitionSpec as P

D = 1280
PATCH = 64
DP = 32
TP = 8
CHIPS = 16
SLOTS = 32
ROWS = PATCH // 4
TOK = 512
UNITS = 160
FEAT = 640
OUTW = 512
W1A = 48

MESH = pl.DeviceIdType.MESH
BF = jnp.bfloat16
F32 = jnp.float32
NT = (((1,), (1,)), ((), ()))
NN = (((1,), (0,)), ((), ()))
TN = (((0,), (0,)), ((), ()))


def dot(a, b, dims):
    return lax.dot_general(a, b, dims, preferred_element_type=F32)


def up(index, size):
    return lax.rem(index + size, size)


class Copies:
    def __init__(self, send, recv):
        self.send, self.recv, self.used, self.open = send, recv, 0, []

    def take(self, count):
        base = self.used
        self.used += count
        return base

    def make(self, src, dst, sem, dev, sent=None):
        return pltpu.make_async_remote_copy(
            src_ref=src,
            dst_ref=dst,
            send_sem=self.send.at[sem if sent is None else sent],
            recv_sem=self.recv.at[sem],
            device_id=dev,
            device_id_type=MESH,
        )

    def start(self, src, dst, sem, dev):
        copy = self.make(src, dst, sem, dev)
        copy.start()
        self.open.append(copy)

    def landed(self, dst, sem, dev):
        self.make(dst, dst, sem, dev).wait_recv()

    def finish(self):
        for item in self.open:
            if callable(item):
                item()
            else:
                item.wait_send()


def kernel(
    counts, patches_t, w1v, w2v, b1, b2, gain, cot,
    emb, gw1, gw2,
    send, recv, lsem, starts, ends, srcs,
    sc, cc, g, nrm, sp, cp, xf, sqx,
    w1f, w2t,
    pg, zgr, zgl, og, oh,
    ht, gt,
    pe, ps, pr, sb, bk,
    g2, a2, c2, s2a, s2b, d2, e2, t2,
    g1, a1, c1, s1a, s1b, d1, e1, t1,
    i1, i2, k1, k2, b1s, pk, w2p, w1,
):
    r = lax.axis_index("dp")
    t = lax.axis_index("tensor")
    m, c = lax.div(r, 2), lax.rem(r, 2)
    X, Y = lax.rem(m, 4), lax.div(m, 4)
    a, b = lax.div(m, 2), lax.rem(m, 2)
    links = Copies(send, recv)

    def plane(chip):
        return (2 * chip + c, t)

    def along_x(d):
        return plane(4 * Y + up(X + d, 4))

    def along_y(d):
        return plane(4 * up(Y + d, 4) + X)

    sibling = (2 * m + 1 - c, t)
    right, left = (r, up(t + 1, TP)), (r, up(t - 1, TP))
    mid_chip, old_chip = lax.rem(m + 2 * t, CHIPS), up(m - 2 * t, CHIPS)
    mate = up(a - t, TP)
    same, still = mate == t, t == 0

    barrier = pltpu.get_barrier_semaphore()

    def greet(dev):
        pl.semaphore_signal(barrier, inc=1, device_id=dev, device_id_type=MESH)

    for d in range(1, CHIPS):
        greet(plane(up(m + d, CHIPS)))
    for d in range(1, TP):
        greet((r, up(t + d, TP)))
    greet(sibling)

    @pl.when(jnp.logical_not(same))
    def _():
        greet((2 * m + 1 - c, mate))

    def prefix(s, total):
        starts[s] = total
        total = total + counts[s]
        ends[s] = total
        return total

    lax.fori_loop(0, DP, prefix, jnp.int32(0))
    mine_start, mine_count = starts[r], counts[r]

    def pack_cot(p, carry):
        sc[p] = cot[up(p - mine_start + 1024, SLOTS)]
        return carry

    lax.fori_loop(0, DP, pack_cot, 0)

    lane = lax.broadcasted_iota(jnp.int32, (8, FEAT), 1)
    row = lax.broadcasted_iota(jnp.int32, (8, FEAT), 0)
    lead = jnp.logical_and(lane >= row * 160, lane < row * 160 + 160)
    pick = jnp.where(lead, 1.0, 0.0).astype(F32)
    pick_bf = pick.astype(BF)
    line = lax.broadcasted_iota(jnp.int32, (256, 256), 0)
    col = lax.broadcasted_iota(jnp.int32, (256, 256), 1)
    order = jnp.where(col == 4 * lax.rem(line, 64) + lax.div(line, 64), 1.0, 0.0).astype(BF)
    for i in range(4):
        halves = []
        for j in range(2):
            at = 512 * i + 256 * j
            v = dot(order, patches_t[:, at : at + 256], NT)
            halves.append(jnp.concatenate([v[64 * p : 64 * p + 64] for p in range(4)], axis=1))
        v = jnp.concatenate(halves, axis=0)
        pk[8 * i : 8 * i + 8] = v.astype(BF).reshape(8, ROWS, FEAT)
        sq = v * v
        high = sq.astype(BF)
        low = (sq - high.astype(F32)).astype(BF)
        sqx[t, :, 128 * i : 128 * i + 128] = dot(pick_bf, high, NT) + dot(pick_bf, low, NT)
    for i in range(2):
        for e in range(2):
            w2p[e, 80 * i : 80 * i + 80] = w2v[i, e]
    wide = w1v[...].astype(F32)
    w1[...] = jnp.concatenate([wide[:, p] for p in range(4)], axis=1).astype(BF)
    gains = jnp.concatenate([gain[...].astype(F32).reshape(1, 160)] * 4, axis=1)
    b1s[...] = jnp.broadcast_to(b1[...].astype(F32).reshape(1, 320), (128, 320)).T.reshape(2, 2, 80, 128)

    pl.semaphore_wait(barrier, 23 + jnp.where(same, 0, 1))

    sq_base = links.take(TP)
    for d in range(1, TP):
        links.start(sqx.at[t], sqx.at[t], sq_base + d, (r, up(t + d, TP)))

    relay = links.take(2)
    relay1 = links.take(1)
    relay_mid = links.take(2)

    def relay_in(e):
        return w2t.at[Y, lax.div(X, 2), :, pl.ds(pl.multiple_of(b * 256 + e * 128, 128), 128)]

    def relay_steps(do):
        @pl.when(jnp.logical_not(still))
        def _():
            do(links.make(w2p, i2, relay_mid, plane(mid_chip)))
            do(links.make(w1, i1, relay_mid + 1, plane(mid_chip)))

    def relay_along_z(do):
        @pl.when(jnp.logical_not(same))
        def _():
            for e in range(2):
                do(links.make(i2.at[e], relay_in(c), relay + c, (2 * m + e, mate), relay + e))
            do(links.make(i1, w1f.at[Y, X], relay1, (r, mate)))

        @pl.when(same)
        def _():
            do(links.make(i2.at[1 - c], relay_in(c), relay + c, sibling, relay + 1 - c))

    relay_steps(lambda copy: copy.start())

    @pl.when(still)
    def _():
        i2[...] = w2p[...]
        i1[...] = w1[...]

    links.open.append(lambda: relay_steps(lambda copy: copy.wait_send()))
    links.open.append(lambda: relay_along_z(lambda copy: copy.wait_send()))

    def exchange(out, into, base):
        def step(d, carry):
            chip = up(m + d, CHIPS)
            links.make(out.at[pl.ds(2 * chip, 2)], into.at[m], base + d, plane(chip)).start()
            return carry

        lax.fori_loop(1, CHIPS, step, 0)

        def sent(d, carry):
            chip = up(m + d, CHIPS)
            links.make(out.at[pl.ds(2 * chip, 2)], into.at[m], base + d, plane(chip)).wait_send()
            return carry

        links.open.append(lambda: lax.fori_loop(1, CHIPS, sent, 0))
        into[m] = out[pl.ds(2 * m, 2)]

    def exchanged(into, base):
        def step(d, carry):
            links.landed(into.at[up(m - d, CHIPS)], base + d, plane(up(m - d, CHIPS)))
            return carry

        lax.fori_loop(1, CHIPS, step, 0)


    def gather_first(block_a, block_b, base):
        for d in range(1, 4):
            links.start(block_a, block_a, base + d, along_x(d))
            links.start(block_b, block_b, base + 3 + d, along_y(d))

    w1a = w1f.at[Y, X, 0:W1A]
    w1b = w1f.at[Y, X, W1A:80]
    w1_base = links.take(16)
    w2_base = links.take(16)
    w2lane = pl.ds(pl.multiple_of(b * 256, 256), 256)
    xh = lax.div(X, 2)
    w2a = w2t.at[Y, xh, 0:80, w2lane]
    w2b = w2t.at[Y, xh, 80:160, w2lane]

    def gather_second(wide_a, wide_b, arrived, base):
        for d in range(1, 4):
            ra, rb = arrived(d)
            links.landed(ra, base + d, along_x(-d))
            links.landed(rb, base + 3 + d, along_y(-d))
        for d in range(1, 4):
            links.start(wide_a, wide_a, base + 6 + d, along_y(d))
            links.start(wide_b, wide_b, base + 9 + d, along_x(d))

    def w2_first(d):
        xx, yy = up(X - d, 4), up(Y - d, 4)
        ra = w2t.at[Y, lax.div(xx, 2), 0:80, pl.ds(pl.multiple_of(lax.rem(xx, 2) * 256, 256), 256)]
        rb = w2t.at[yy, xh, 80:160, w2lane]
        return ra, rb

    def w1_first(d):
        return w1f.at[Y, up(X - d, 4), 0:W1A], w1f.at[up(Y - d, 4), X, W1A:80]

    def source(k, carry):
        p0 = 32 * k + 2 * m
        n0, n1 = jnp.int32(0), jnp.int32(0)
        for s in range(DP):
            v = ends[s]
            n0 = n0 + (v <= p0).astype(jnp.int32)
            n1 = n1 + (v <= p0 + 1).astype(jnp.int32)
        srcs[k] = jnp.minimum(n0, DP - 1)
        srcs[16 + k] = jnp.minimum(n1, DP - 1)
        return carry

    lax.fori_loop(0, 16, source, 0)

    for d in range(1, TP):
        z = up(t - d, TP)
        links.landed(sqx.at[z], sq_base + d, (r, z))
    total = sqx[0]
    for z in range(1, TP):
        total = total + sqx[z]
    inv = lax.rsqrt(total / D + 1e-06)
    part1 = inv.astype(BF).astype(F32)
    part2 = (inv - part1).astype(BF).astype(F32)
    stack = jnp.concatenate([part1, part2, (inv - part1) - part2], axis=0)
    stack_t = stack.T.astype(BF)
    pick3 = jnp.concatenate([pick, pick, pick], axis=0).astype(BF)
    for i in range(4):
        scale = dot(stack_t[128 * i : 128 * i + 128], pick3, NN)
        v = pk[8 * i : 8 * i + 8].reshape(128, FEAT).astype(F32)
        nrm[8 * i : 8 * i + 8] = (v * scale * gains).astype(BF).reshape(8, ROWS, FEAT)

    def pack_rows(p, carry):
        sp[p] = nrm[up(p - mine_start + 1024, SLOTS)]
        return carry

    lax.fori_loop(0, DP, pack_rows, 0)
    row_base = links.take(CHIPS)
    exchange(sp, cp.at[c], row_base)

    @pl.when(jnp.logical_not(still))
    def _():
        links.landed(i2, relay_mid, plane(old_chip))
        links.landed(i1, relay_mid + 1, plane(old_chip))

    relay_along_z(lambda copy: copy.start())

    @pl.when(same)
    def _():
        w1f[Y, X] = i1[...]
        own = pltpu.make_async_copy(i2.at[c], relay_in(c), lsem)
        own.start()
        own.wait()

    for e in range(2):

        @pl.when(jnp.logical_or(jnp.logical_not(same), e != c))
        def _(e=e):
            links.landed(relay_in(e), relay + e, sibling)

    gather_first(w2a, w2b, w2_base)

    exchanged(cp.at[c], row_base)
    row_sib = links.take(1)
    links.start(cp.at[c, :, 1 - c], cp.at[c, :, 1 - c], row_sib, sibling)

    cot_base = links.take(CHIPS)
    exchange(sc, cc.at[c], cot_base)

    links.landed(cp.at[1 - c, :, c], row_sib, sibling)

    def choose_rows(k, carry):
        s = srcs[16 * c + k]
        xf[t, 16 * c + k] = cp[lax.rem(s, 2), lax.div(s, 2), c]
        return carry

    lax.fori_loop(0, 16, choose_rows, 0)

    def ring_sum(part, rr, rl, base, s):
        br, bl = up(t + 4 - s, TP), up(t - 4 + s, TP)
        for u in range(2):
            k = base + 8 * u
            w = slice(256 * u, 256 * u + 256)
            if s == 0:
                links.start(part.at[br, 0:80, w], rr.at[0, 0:80, w], k, right)
                links.start(part.at[bl, 80:160, w], rl.at[0, 80:160, w], k + 4, left)
                continue
            lo, hi = (slice(0, 80), slice(80, 160)) if s == 1 else (slice(0, 160),) * 2
            links.landed(rr.at[s - 1, lo, w], k + s - 1, left)
            part[br, lo, w] = (part[br, lo, w].astype(F32) + rr[s - 1, lo, w].astype(F32)).astype(BF)
            links.start(part.at[br, :, w], rr.at[s, :, w], k + s, right)
            links.landed(rl.at[s - 1, hi, w], k + 4 + s - 1, right)
            part[bl, hi, w] = (part[bl, hi, w].astype(F32) + rl[s - 1, hi, w].astype(F32)).astype(BF)
            links.start(part.at[bl, :, w], rl.at[s, :, w], k + 4 + s, left)

    def ring_end(rr, rl, base, u):
        w = slice(256 * u, 256 * u + 256)
        links.landed(rr.at[3, :, w], base + 8 * u + 3, left)
        links.landed(rl.at[3, :, w], base + 8 * u + 7, right)

    def ring_copy(buf, base, s):
        br, bl = up(t - s, TP), up(t + s, TP)
        for u in range(2):
            k = base + 8 * u
            w = slice(256 * u, 256 * u + 256)
            if s > 0:
                links.landed(buf.at[br, :, w], k + s - 1, left)
            lo, hi = (slice(0, 160),) * 2 if s < 3 else (slice(0, 80), slice(80, 160))
            links.start(buf.at[br, lo, w], buf.at[br, lo, w], k + s, right)
            if s > 0:
                links.landed(buf.at[bl, :, w], k + 4 + s - 1, right)
            links.start(buf.at[bl, hi, w], buf.at[bl, hi, w], k + 4 + s, left)

    def ring_copied(buf, base):
        far = up(t + 4, TP)
        for u in range(2):
            w = slice(256 * u, 256 * u + 256)
            links.landed(buf.at[far, 0:80, w], base + 8 * u + 3, left)
            links.landed(buf.at[far, 80:160, w], base + 8 * u + 7, right)

    def around(s, work):
        def step(i, carry):
            work(up(t + (2 * i - 1) * s, TP))
            return carry

        lax.fori_loop(0, 2, step, 0)

    x_base = links.take(16)
    xs_base = links.take(18)

    def rows_of(z, u, start, size):
        return xf.at[z, pl.ds(16 * c + 8 * u + start, size)]

    def hand_over(z, u):
        ref = rows_of(z, u, 0, 8)
        links.start(ref, ref, xs_base + 2 * z + u, sibling)

    def handed(z):
        for u in range(2):
            links.landed(xf.at[z, pl.ds(16 * (1 - c) + 8 * u, 8)], xs_base + 2 * z + u, sibling)

    def ring_rows(s):
        br, bl = up(t - s, TP), up(t + s, TP)
        for u in range(2):
            k = x_base + 8 * u
            size = 8 if s < 3 else 4
            if s > 0:
                links.landed(rows_of(br, u, 0, 8), k + s - 1, left)
            ref = rows_of(br, u, 0, size)
            links.start(ref, ref, k + s, right)
            if s > 0:
                links.landed(rows_of(bl, u, 0, 8), k + 4 + s - 1, right)
            ref = rows_of(bl, u, 8 - size, size)
            links.start(ref, ref, k + 4 + s, left)
            hand_over(br, u)
            if s > 0:
                hand_over(bl, u)

    def ring_rows_end():
        far = up(t + 4, TP)
        for u in range(2):
            links.landed(rows_of(far, u, 0, 4), x_base + 8 * u + 3, left)
            ref = rows_of(far, u, 0, 4)
            links.start(ref, ref, xs_base + 2 * far + u, sibling)
            links.landed(rows_of(far, u, 4, 4), x_base + 8 * u + 7, right)
            ref = rows_of(far, u, 4, 4)
            links.start(ref, ref, xs_base + 16 + u, sibling)

    ring_rows(0)

    gather_second(w2t.at[Y, :, 0:80], w2t.at[:, xh, 80:160, w2lane], w2_first, w2_base)

    @pl.when(jnp.logical_not(same))
    def _():
        links.landed(w1f.at[Y, X], relay1, (r, mate))

    gather_first(w1a, w1b, w1_base)

    def place(z):
        return lax.rem(z + t, TP)

    def grad_block(z):
        p = place(z)
        return dot(w2t[lax.div(p, 2), lax.rem(p, 2)], g[...].reshape(TOK, OUTW), NT)

    def grad_store(z):
        pg[z] = grad_block(z).astype(BF)

    def pre_add(z):
        p = place(z)
        rows = w1f[lax.div(p, 2), pl.ds(2 * lax.rem(p, 2), 2)].reshape(UNITS, FEAT)
        oh[...] += dot(rows, xf[z].reshape(TOK, FEAT), NT)

    pg_base = links.take(16)
    ht_base = links.take(16)
    def activate(u):
        w = slice(256 * u, 256 * u + 256)

        def step(i, carry):
            rows = pl.ds(pl.multiple_of(i * 32, 32), 32)
            v = oh[rows, w]
            cdf = 0.5 * (1.0 + lax.erf(v * 0.7071067811865476))
            density = jnp.exp(-0.5 * v * v) * 0.3989422804014327
            ht[t, rows, w] = (v * cdf).astype(BF)
            oh[rows, w] = cdf + v * density
            return carry

        lax.fori_loop(0, 5, step, 0)

    def descend(u):
        w = slice(256 * u, 256 * u + 256)

        def step(i, carry):
            rows = pl.ds(pl.multiple_of(i * 32, 32), 32)
            v = og[rows, w] + zgr[3, rows, w].astype(F32) + zgl[3, rows, w].astype(F32)
            gt[rows, w] = (v * oh[rows, w]).astype(BF)
            return carry

        lax.fori_loop(0, 5, step, 0)

    exchanged(cc.at[c], cot_base)
    cot_sib = links.take(1)
    links.start(cc.at[c], cc.at[c], cot_sib, sibling)

    ring_rows(1)
    links.landed(cc.at[1 - c], cot_sib, sibling)

    def choose(j, carry):
        s = srcs[j]
        g[j] = cc[lax.rem(s, 2), lax.div(s, 2), lax.div(j, 16)]
        return carry

    lax.fori_loop(0, 32, choose, 0)

    for d in range(1, 4):
        xx, yy = up(X - d, 4), up(Y - d, 4)
        links.landed(w2t.at[yy, :, 0:80], w2_base + 6 + d, along_y(-d))
        links.landed(
            w2t.at[:, lax.div(xx, 2), 80:160, pl.ds(pl.multiple_of(lax.rem(xx, 2) * 256, 256), 256)],
            w2_base + 9 + d,
            along_x(-d),
        )

    grad_store(up(t + 4, TP))
    ring_sum(pg, zgr, zgl, pg_base, 0)
    around(3, grad_store)
    gather_second(w1f.at[Y, :, 0:W1A], w1f.at[:, X, W1A:80], w1_first, w1_base)
    ring_rows(2)
    ring_sum(pg, zgr, zgl, pg_base, 1)
    around(2, grad_store)
    ring_rows(3)
    ring_sum(pg, zgr, zgl, pg_base, 2)
    around(1, grad_store)
    og[...] = grad_block(t)
    for d in range(1, 4):
        xx, yy = up(X - d, 4), up(Y - d, 4)
        links.landed(w1f.at[yy, :, 0:W1A], w1_base + 6 + d, along_y(-d))
        links.landed(w1f.at[:, xx, W1A:80], w1_base + 9 + d, along_x(-d))
    oh[...] = jnp.concatenate([b1s[:, c].reshape(UNITS, 128)] * 4, axis=1)
    handed(t)
    pre_add(t)
    for s in range(1, 3):
        handed(up(t - s, TP))
        handed(up(t + s, TP))
        around(s, pre_add)
    ring_sum(pg, zgr, zgl, pg_base, 3)
    ring_rows_end()
    handed(up(t - 3, TP))
    handed(up(t + 3, TP))
    around(3, pre_add)
    far_rows = xf.at[up(t + 4, TP)]
    for u in range(2):
        for i in range(2):
            ref = far_rows.at[pl.ds(16 * (1 - c) + 8 * u + 4 * i, 4)]
            links.landed(ref, xs_base + (2 * up(t + 4, TP) if i == 0 else 16) + u, sibling)
    pre_add(up(t + 4, TP))

    for u in range(2):
        activate(u)
    ring_copy(ht, ht_base, 0)
    def plane_send(part, cut, ra, rb, base, z):
        yy, par = lax.div(z, 2), lax.rem(z, 2)
        dy = up(yy - Y, 4)

        @pl.when(dy != 0)
        def _():
            links.make(
                part.at[yy, pl.ds(2 * par, 2), 0:cut],
                ra.at[dy - 1, pl.ds(2 * par, 2)],
                base + 2 * (dy - 1) + par,
                along_y(dy),
            ).start()

        for i in range(2):
            xx = 2 * par + i
            dx = up(xx - X, 4)

            @pl.when(dx != 0)
            def _(xx=xx, dx=dx):
                links.make(
                    part.at[yy, xx, cut:],
                    rb.at[dx - 1, yy],
                    base + 6 + 4 * (dx - 1) + yy,
                    along_x(dx),
                ).start()

    def plane_sent(part, cut, ra, rb, sa, sbx, rc, rd, base):
        def waits():
            for d in range(3):
                for i in range(2):
                    links.make(part.at[0, 0:2, 0:cut], ra.at[d, 0:2], base + 2 * d + i, along_y(1)).wait_send()
                for i in range(4):
                    links.make(part.at[0, 0, cut:], rb.at[d, 0], base + 6 + 4 * d + i, along_x(1)).wait_send()
                links.make(sa.at[0], rc.at[d], base + 19 + d, along_x(1)).wait_send()
                links.make(sbx.at[0], rd.at[d], base + 22 + d, along_y(1)).wait_send()

        links.open.append(waits)

    def plane_second(part, cut, ra, rb, sa, sbx, rc, rd, base, z):
        p = place(z)
        yy, par = lax.div(p, 2), lax.rem(p, 2)

        @pl.when(Y == yy)
        def _():
            for d in range(3):
                links.landed(ra.at[d, pl.ds(2 * par, 2)], base + 2 * d + par, along_y(-d - 1))
            for i in range(2):
                xx = 2 * par + i
                v = part[yy, xx, 0:cut].astype(F32)
                for d in range(3):
                    v = v + ra[d, xx].astype(F32)
                sa[xx] = v.astype(BF)
                dx = up(xx - X, 4)

                @pl.when(dx != 0)
                def _(xx=xx, dx=dx):
                    links.make(sa.at[xx], rc.at[dx - 1], base + 18 + dx, along_x(dx)).start()

        @pl.when(lax.div(X, 2) == par)
        def _():
            for d in range(3):
                links.landed(rb.at[d, yy], base + 6 + 4 * d + yy, along_x(-d - 1))
            v = part[yy, X, cut:].astype(F32)
            for d in range(3):
                v = v + rb[d, yy].astype(F32)
            sbx[yy] = v.astype(BF)
            dy = up(yy - Y, 4)

            @pl.when(dy != 0)
            def _():
                links.make(sbx.at[yy], rd.at[dy - 1], base + 21 + dy, along_y(dy)).start()

    def plane_sum_end(sa, sbx, rc, rd, base):
        for d in range(1, 4):
            links.landed(rc.at[d - 1], base + 18 + d, along_x(-d))
        va = sa[X].astype(F32)
        for d in range(3):
            va = va + rc[d].astype(F32)
        for d in range(1, 4):
            links.landed(rd.at[d - 1], base + 21 + d, along_y(-d))
        vb = sbx[Y].astype(F32)
        for d in range(3):
            vb = vb + rd[d].astype(F32)
        return va.astype(BF), vb.astype(BF)

    g2_base = links.take(25)

    def second_grad(z):
        p = place(z)
        v = dot(ht[z], g[...].reshape(TOK, OUTW), NN).astype(BF)
        for i in range(2):
            g2[lax.div(p, 2), 2 * lax.rem(p, 2) + i] = v[:, 256 * i : 256 * i + 256]
        plane_send(g2, 80, a2, c2, g2_base, p)

    def second_second(z):
        plane_second(g2, 80, a2, c2, s2a, s2b, d2, e2, g2_base, z)

    def embed(z):
        p = place(z)

        def step(i, carry):
            lanes = pl.ds(pl.multiple_of(i * 128, 128), 128)
            rows = ht[z, :, lanes].astype(F32).T.astype(BF)
            v = dot(rows, w2t[lax.div(p, 2), lax.rem(p, 2)], NN)
            pe[pl.ds(8 * i, 8)] += v.reshape(8, ROWS, OUTW)
            return carry

        lax.fori_loop(0, 4, step, 0)

    def use_hidden(z):
        second_grad(z)
        embed(z)

    plane_sent(g2, 80, a2, c2, s2a, s2b, d2, e2, g2_base)

    g1_base = links.take(25)

    def first_grad(z):
        p = place(z)
        v = dot(gt[...], xf[z].reshape(TOK, FEAT), NN).astype(BF)
        for i in range(2):
            g1[lax.div(p, 2), 2 * lax.rem(p, 2) + i] = v[80 * i : 80 * i + 80]
        plane_send(g1, W1A, a1, c1, g1_base, p)

    plane_sent(g1, W1A, a1, c1, s1a, s1b, d1, e1, g1_base)
    def first_second(z):
        plane_second(g1, W1A, a1, c1, s1a, s1b, d1, e1, g1_base, z)

    for u in range(2):
        ring_end(zgr, zgl, pg_base, u)
        descend(u)

    lax.fori_loop(0, TP, lambda z, carry: (first_grad(z), carry)[1], 0)
    pe[...] = jnp.zeros_like(pe)
    use_hidden(t)
    ring_copy(ht, ht_base, 1)
    around(1, use_hidden)
    ring_copy(ht, ht_base, 2)
    around(2, use_hidden)
    ring_copy(ht, ht_base, 3)
    around(3, use_hidden)
    lax.fori_loop(0, TP, lambda z, carry: (first_second(z), carry)[1], 0)

    ring_copied(ht, ht_base)
    use_hidden(up(t + 4, TP))

    def window_of(s, e):
        first = starts[s]
        slot = lax.rem(2 * m + e - first + 1024, SLOTS)
        return e * 16 + jnp.minimum(lax.div(first + slot, 32), 15)

    def pack_sibling(i, carry):
        for e in range(2):
            ps[2 * i + e] = pe[window_of(2 * i + 1 - c, e)].astype(BF)
        return carry

    lax.fori_loop(0, CHIPS, pack_sibling, 0)
    emb_sib = links.take(1)
    links.start(ps, pr, emb_sib, sibling)

    second_second(t)
    around(1, second_second)
    around(2, second_second)
    around(3, second_second)
    second_second(up(t + 4, TP))
    va, vb = plane_sum_end(s1a, s1b, d1, e1, g1_base)
    t1[0:W1A] = va
    t1[W1A:80] = vb
    back1 = links.take(2)

    def back1_z(do):
        @pl.when(jnp.logical_not(same))
        def _():
            do(links.make(t1, k1, back1, (r, mate)))

    back1_z(lambda copy: copy.start())

    @pl.when(same)
    def _():
        k1[...] = t1[...]

    links.open.append(lambda: back1_z(lambda copy: copy.wait_send()))

    va, vb = plane_sum_end(s2a, s2b, d2, e2, g2_base)
    for e in range(2):
        t2[e, 0:80] = va[:, 128 * e : 128 * e + 128]
        t2[e, 80:160] = vb[:, 128 * e : 128 * e + 128]
    back = links.take(3)

    def back_z(do):
        @pl.when(jnp.logical_not(same))
        def _():
            for e in range(2):
                do(links.make(t2.at[e], k2.at[c], back + c, (2 * m + e, mate), back + e))

        @pl.when(same)
        def _():
            do(links.make(t2.at[1 - c], k2.at[c], back + c, sibling, back + 1 - c))

    back_z(lambda copy: copy.start())

    @pl.when(same)
    def _():
        k2[c] = t2[c]

    links.open.append(lambda: back_z(lambda copy: copy.wait_send()))

    links.landed(pr, emb_sib, sibling)
    bias2 = b2[...].astype(F32).reshape(1, OUTW)

    def pack_home(i, carry):
        for e in range(2):
            v = pe[window_of(2 * i + c, e)] + pr[2 * i + e].astype(F32) + bias2
            sb[2 * i + e] = v.astype(BF)
        return carry

    lax.fori_loop(0, CHIPS, pack_home, 0)
    home_base = links.take(CHIPS)
    exchange(sb, bk, home_base)

    @pl.when(jnp.logical_not(same))
    def _():
        links.landed(k1, back1, (r, mate))

    def back1_plane(do):
        @pl.when(jnp.logical_not(still))
        def _():
            do(links.make(k1, gw1, back1 + 1, plane(old_chip)))

    back1_plane(lambda copy: copy.start())

    @pl.when(still)
    def _():
        gw1[...] = k1[...]

    links.open.append(lambda: back1_plane(lambda copy: copy.wait_send()))

    for e in range(2):

        @pl.when(jnp.logical_or(jnp.logical_not(same), e != c))
        def _(e=e):
            links.landed(k2.at[e], back + e, (2 * m + e, mate))

    def back_plane(do):
        @pl.when(jnp.logical_not(still))
        def _():
            do(links.make(k2, gw2, back + 2, plane(old_chip)))

    back_plane(lambda copy: copy.start())

    @pl.when(still)
    def _():
        gw2[...] = k2[...]

    links.open.append(lambda: back_plane(lambda copy: copy.wait_send()))

    exchanged(bk, home_base)

    def home(j, carry):
        p = lax.rem(mine_start + j, DP)
        v = bk[lax.div(p, 2), lax.rem(p, 2)].astype(F32)
        emb[j] = jnp.where(j < mine_count, v, 0.0).astype(BF)
        return carry

    lax.fori_loop(0, SLOTS, home, 0)

    @pl.when(jnp.logical_not(still))
    def _():
        links.landed(gw1, back1 + 1, plane(mid_chip))
        links.landed(gw2, back + 2, plane(mid_chip))

    links.finish()


def on_device(patches, norm_gain, w_first, b_first, w_second, b_second, counts, cotangent):
    patches_t = patches.T
    w2v = w_second.T.reshape(2, 2, 80, 128)
    cot = cotangent.reshape(SLOTS, ROWS, OUTW)

    vmem = pl.BlockSpec(memory_space=pltpu.VMEM)
    V = pltpu.VMEM
    S = pltpu.SMEM
    emb, gw1, gw2 = pl.pallas_call(
        kernel,
        name="merger",
        out_shape=(
            jax.ShapeDtypeStruct((SLOTS, ROWS, OUTW), BF),
            jax.ShapeDtypeStruct((80, FEAT), BF),
            jax.ShapeDtypeStruct((2, UNITS, 128), BF),
        ),
        in_specs=[pl.BlockSpec(memory_space=pltpu.SMEM)] + [vmem] * 7,
        out_specs=(vmem, vmem, vmem),
        scratch_shapes=[
            pltpu.SemaphoreType.DMA((256,)),
            pltpu.SemaphoreType.DMA((256,)),
            pltpu.SemaphoreType.DMA,
            S((DP,), jnp.int32),
            S((DP,), jnp.int32),
            S((DP,), jnp.int32),
            V((DP, ROWS, OUTW), BF),
            V((2, CHIPS, 2, ROWS, OUTW), BF),
            V((32, ROWS, OUTW), BF),
            V((SLOTS, ROWS, FEAT), BF),
            V((DP, ROWS, FEAT), BF),
            V((2, CHIPS, 2, ROWS, FEAT), BF),
            V((TP, 32, ROWS, FEAT), BF),
            V((TP, 8, TOK), F32),
            V((4, 4, 80, FEAT), BF),
            V((4, 2, UNITS, OUTW), BF),
            V((TP, UNITS, TOK), BF),
            V((4, UNITS, TOK), BF),
            V((4, UNITS, TOK), BF),
            V((UNITS, TOK), F32),
            V((UNITS, TOK), F32),
            V((TP, UNITS, TOK), BF),
            V((UNITS, TOK), BF),
            V((32, ROWS, OUTW), F32),
            V((32, ROWS, OUTW), BF),
            V((32, ROWS, OUTW), BF),
            V((32, ROWS, OUTW), BF),
            V((CHIPS, 2, ROWS, OUTW), BF),
            V((4, 4, UNITS, 256), BF),
            V((3, 4, 80, 256), BF),
            V((3, 4, 80, 256), BF),
            V((4, 80, 256), BF),
            V((4, 80, 256), BF),
            V((3, 80, 256), BF),
            V((3, 80, 256), BF),
            V((2, UNITS, 128), BF),
            V((4, 4, 80, FEAT), BF),
            V((3, 4, W1A, FEAT), BF),
            V((3, 4, 80 - W1A, FEAT), BF),
            V((4, W1A, FEAT), BF),
            V((4, 80 - W1A, FEAT), BF),
            V((3, W1A, FEAT), BF),
            V((3, 80 - W1A, FEAT), BF),
            V((80, FEAT), BF),
            V((80, FEAT), BF),
            V((2, UNITS, 128), BF),
            V((80, FEAT), BF),
            V((2, UNITS, 128), BF),
            V((2, 2, 80, 128), F32),
            V((SLOTS, ROWS, FEAT), BF),
            V((2, UNITS, 128), BF),
            V((80, FEAT), BF),
        ],
        compiler_params=pltpu.CompilerParams(
            collective_id=0, has_side_effects=True, vmem_limit_bytes=56 * 1024 * 1024
        ),
        cost_estimate=pl.CostEstimate(
            flops=3_700_000_000, bytes_accessed=3_000_000, transcendentals=200_000
        ),
    )(counts, patches_t, w_first, w2v, b_first, b_second, norm_gain, cot)
    embeddings = emb.reshape(SLOTS * ROWS, OUTW)
    grad_w1 = gw1.reshape(80, 4, 160)
    grad_w2 = gw2.reshape(2, 2, 80, 128).transpose(3, 1, 0, 2).reshape(128, 320)
    return embeddings, grad_w1, grad_w2


def solution(mesh):
    in_specs = (
        P("dp", "tensor"),
        P("tensor"),
        P("dp", None, "tensor"),
        P("tensor"),
        P("dp", "tensor"),
        P("tensor"),
        P(),
        P("dp", "tensor"),
    )
    out_specs = (P("dp", "tensor"), P("dp", None, "tensor"), P("dp", "tensor"))
    return jax.shard_map(
        on_device, mesh=mesh, in_specs=in_specs, out_specs=out_specs, check_vma=False
    )
```

```python
import functools

import jax
import jax.numpy as jnp
from jax import lax
from jax.experimental import pallas as pl
from jax.experimental.pallas import tpu as pltpu
from jax.sharding import PartitionSpec as P

D = 1280
PATCH = 64
DP = 32
TP = 8
CHIPS = 16
SLOTS = 32
ROWS = PATCH // 4
TOK = 512
UNITS = 160
FEAT = 640
OUTW = 512
W1A = 48

MESH = pl.DeviceIdType.MESH
BF = jnp.bfloat16
F32 = jnp.float32
NT = (((1,), (1,)), ((), ()))
NN = (((1,), (0,)), ((), ()))
TN = (((0,), (0,)), ((), ()))


def dot(a, b, dims):
    return lax.dot_general(a, b, dims, preferred_element_type=F32)


def up(index, size):
    return lax.rem(index + size, size)


class Copies:
    def __init__(self, send, recv):
        self.send, self.recv, self.used, self.open = send, recv, 0, []

    def take(self, count):
        base = self.used
        self.used += count
        return base

    def make(self, src, dst, sem, dev, sent=None):
        return pltpu.make_async_remote_copy(
            src_ref=src,
            dst_ref=dst,
            send_sem=self.send.at[sem if sent is None else sent],
            recv_sem=self.recv.at[sem],
            device_id=dev,
            device_id_type=MESH,
        )

    def start(self, src, dst, sem, dev):
        copy = self.make(src, dst, sem, dev)
        copy.start()
        self.open.append(copy)

    def landed(self, dst, sem, dev):
        self.make(dst, dst, sem, dev).wait_recv()

    def finish(self, items):
        for item in items:
            if callable(item):
                item()
            else:
                item.wait_send()


def kernel(
    counts, patches_t, w1v, w2v, b1, b2, gain, cot,
    emb, gw1, gw2,
    send, recv, lsem, starts, ends, srcs,
    sc, cc, g, nrm, sp, cp, xf, sqx,
    w1f, w2t,
    pg, zgr, zgl, og, oh,
    ht, gt,
    pe, ps, pr, sb, bk,
    g2, a2, c2, s2a, s2b, d2, e2, t2,
    g1, a1, c1, s1a, s1b, d1, e1, t1,
    i1, i2, k1, k2, b1s, pk, w2p, w1,
):
    r = lax.axis_index("dp")
    t = lax.axis_index("tensor")
    m, c = lax.div(r, 2), lax.rem(r, 2)
    X, Y = lax.rem(m, 4), lax.div(m, 4)
    a, b = lax.div(m, 2), lax.rem(m, 2)
    links = Copies(send, recv)

    def plane(chip):
        return (2 * chip + c, t)

    def along_x(d):
        return plane(4 * Y + up(X + d, 4))

    def along_y(d):
        return plane(4 * up(Y + d, 4) + X)

    sibling = (2 * m + 1 - c, t)
    right, left = (r, up(t + 1, TP)), (r, up(t - 1, TP))
    mid_chip, old_chip = lax.rem(m + 2 * t, CHIPS), up(m - 2 * t, CHIPS)
    mate = up(a - t, TP)
    same, still = mate == t, t == 0

    barrier = pltpu.get_barrier_semaphore()

    def greet(dev):
        pl.semaphore_signal(barrier, inc=1, device_id=dev, device_id_type=MESH)

    for d in range(1, CHIPS):
        greet(plane(up(m + d, CHIPS)))
    for d in range(1, TP):
        greet((r, up(t + d, TP)))
    greet(sibling)

    @pl.when(jnp.logical_not(same))
    def _():
        greet((2 * m + 1 - c, mate))

    def prefix(s, total):
        starts[s] = total
        total = total + counts[s]
        ends[s] = total
        return total

    lax.fori_loop(0, DP, prefix, jnp.int32(0))
    mine_start, mine_count = starts[r], counts[r]

    def pack_cot(p, carry):
        sc[p] = cot[up(p - mine_start + 1024, SLOTS)]
        return carry

    lax.fori_loop(0, DP, pack_cot, 0)

    lane = lax.broadcasted_iota(jnp.int32, (8, FEAT), 1)
    row = lax.broadcasted_iota(jnp.int32, (8, FEAT), 0)
    lead = jnp.logical_and(lane >= row * 160, lane < row * 160 + 160)
    pick = jnp.where(lead, 1.0, 0.0).astype(F32)
    pick_bf = pick.astype(BF)
    line = lax.broadcasted_iota(jnp.int32, (256, 256), 0)
    col = lax.broadcasted_iota(jnp.int32, (256, 256), 1)
    order = jnp.where(col == 4 * lax.rem(line, 64) + lax.div(line, 64), 1.0, 0.0).astype(BF)
    for i in range(4):
        halves = []
        for j in range(2):
            at = 512 * i + 256 * j
            v = dot(order, patches_t[:, at : at + 256], NT)
            halves.append(jnp.concatenate([v[64 * p : 64 * p + 64] for p in range(4)], axis=1))
        v = jnp.concatenate(halves, axis=0)
        pk[8 * i : 8 * i + 8] = v.astype(BF).reshape(8, ROWS, FEAT)
        sq = v * v
        high = sq.astype(BF)
        low = (sq - high.astype(F32)).astype(BF)
        sqx[t, :, 128 * i : 128 * i + 128] = dot(pick_bf, high, NT) + dot(pick_bf, low, NT)
    for i in range(2):
        for e in range(2):
            w2p[e, 80 * i : 80 * i + 80] = w2v[i, e]
    wide = w1v[...].astype(F32)
    w1[...] = jnp.concatenate([wide[:, p] for p in range(4)], axis=1).astype(BF)
    gains = jnp.concatenate([gain[...].astype(F32).reshape(1, 160)] * 4, axis=1)
    b1s[...] = jnp.broadcast_to(b1[...].astype(F32).reshape(1, 320), (128, 320)).T.reshape(2, 2, 80, 128)

    pl.semaphore_wait(barrier, 23 + jnp.where(same, 0, 1))

    sq_base = links.take(TP)
    for d in range(1, TP):
        links.start(sqx.at[t], sqx.at[t], sq_base + d, (r, up(t + d, TP)))

    relay = links.take(2)
    relay1 = links.take(1)
    relay_mid = links.take(2)

    def relay_in(e):
        return w2t.at[Y, lax.div(X, 2), :, pl.ds(pl.multiple_of(b * 256 + e * 128, 128), 128)]

    def relay_steps(do):
        @pl.when(jnp.logical_not(still))
        def _():
            do(links.make(w2p, i2, relay_mid, plane(mid_chip)))
            do(links.make(w1, i1, relay_mid + 1, plane(mid_chip)))

    def relay_along_z(do):
        @pl.when(jnp.logical_not(same))
        def _():
            for e in range(2):
                do(links.make(i2.at[e], relay_in(c), relay + c, (2 * m + e, mate), relay + e))
            do(links.make(i1, w1f.at[Y, X], relay1, (r, mate)))

        @pl.when(same)
        def _():
            do(links.make(i2.at[1 - c], relay_in(c), relay + c, sibling, relay + 1 - c))

    relay_steps(lambda copy: copy.start())

    @pl.when(still)
    def _():
        i2[...] = w2p[...]
        i1[...] = w1[...]

    links.open.append(lambda: relay_steps(lambda copy: copy.wait_send()))
    links.open.append(lambda: relay_along_z(lambda copy: copy.wait_send()))

    def exchange(out, into, base):
        def step(d, carry):
            chip = up(m + d, CHIPS)
            links.make(out.at[pl.ds(2 * chip, 2)], into.at[m], base + d, plane(chip)).start()
            return carry

        lax.fori_loop(1, CHIPS, step, 0)

        def sent(d, carry):
            chip = up(m + d, CHIPS)
            links.make(out.at[pl.ds(2 * chip, 2)], into.at[m], base + d, plane(chip)).wait_send()
            return carry

        links.open.append(lambda: lax.fori_loop(1, CHIPS, sent, 0))
        into[m] = out[pl.ds(2 * m, 2)]

    def exchanged(into, base):
        def step(d, carry):
            links.landed(into.at[up(m - d, CHIPS)], base + d, plane(up(m - d, CHIPS)))
            return carry

        lax.fori_loop(1, CHIPS, step, 0)


    def gather_first(block_a, block_b, base):
        for d in range(1, 4):
            links.start(block_a, block_a, base + d, along_x(d))
            links.start(block_b, block_b, base + 3 + d, along_y(d))

    w1a = w1f.at[Y, X, 0:W1A]
    w1b = w1f.at[Y, X, W1A:80]
    w1_base = links.take(16)
    w2_base = links.take(16)
    w2lane = pl.ds(pl.multiple_of(b * 256, 256), 256)
    xh = lax.div(X, 2)
    w2a = w2t.at[Y, xh, 0:80, w2lane]
    w2b = w2t.at[Y, xh, 80:160, w2lane]

    def gather_second(wide_a, wide_b, arrived, base):
        for d in range(1, 4):
            ra, rb = arrived(d)
            links.landed(ra, base + d, along_x(-d))
            links.landed(rb, base + 3 + d, along_y(-d))
        for d in range(1, 4):
            links.start(wide_a, wide_a, base + 6 + d, along_y(d))
            links.start(wide_b, wide_b, base + 9 + d, along_x(d))

    def w2_first(d):
        xx, yy = up(X - d, 4), up(Y - d, 4)
        ra = w2t.at[Y, lax.div(xx, 2), 0:80, pl.ds(pl.multiple_of(lax.rem(xx, 2) * 256, 256), 256)]
        rb = w2t.at[yy, xh, 80:160, w2lane]
        return ra, rb

    def w1_first(d):
        return w1f.at[Y, up(X - d, 4), 0:W1A], w1f.at[up(Y - d, 4), X, W1A:80]

    def source(k, carry):
        p0 = 32 * k + 2 * m
        n0, n1 = jnp.int32(0), jnp.int32(0)
        for s in range(DP):
            v = ends[s]
            n0 = n0 + (v <= p0).astype(jnp.int32)
            n1 = n1 + (v <= p0 + 1).astype(jnp.int32)
        srcs[k] = jnp.minimum(n0, DP - 1)
        srcs[16 + k] = jnp.minimum(n1, DP - 1)
        return carry

    lax.fori_loop(0, 16, source, 0)

    for d in range(1, TP):
        z = up(t - d, TP)
        links.landed(sqx.at[z], sq_base + d, (r, z))
    total = sqx[0]
    for z in range(1, TP):
        total = total + sqx[z]
    inv = lax.rsqrt(total / D + 1e-06)
    part1 = inv.astype(BF).astype(F32)
    part2 = (inv - part1).astype(BF).astype(F32)
    stack = jnp.concatenate([part1, part2, (inv - part1) - part2], axis=0)
    stack_t = stack.T.astype(BF)
    pick3 = jnp.concatenate([pick, pick, pick], axis=0).astype(BF)
    for i in range(4):
        scale = dot(stack_t[128 * i : 128 * i + 128], pick3, NN)
        v = pk[8 * i : 8 * i + 8].reshape(128, FEAT).astype(F32)
        nrm[8 * i : 8 * i + 8] = (v * scale * gains).astype(BF).reshape(8, ROWS, FEAT)

    def pack_rows(p, carry):
        sp[p] = nrm[up(p - mine_start + 1024, SLOTS)]
        return carry

    lax.fori_loop(0, DP, pack_rows, 0)
    row_base = links.take(CHIPS)
    exchange(sp, cp.at[c], row_base)

    @pl.when(jnp.logical_not(still))
    def _():
        links.landed(i2, relay_mid, plane(old_chip))
        links.landed(i1, relay_mid + 1, plane(old_chip))

    relay_along_z(lambda copy: copy.start())

    @pl.when(same)
    def _():
        w1f[Y, X] = i1[...]
        own = pltpu.make_async_copy(i2.at[c], relay_in(c), lsem)
        own.start()
        own.wait()

    for e in range(2):

        @pl.when(jnp.logical_or(jnp.logical_not(same), e != c))
        def _(e=e):
            links.landed(relay_in(e), relay + e, sibling)

    gather_first(w2a, w2b, w2_base)

    exchanged(cp.at[c], row_base)
    row_sib = links.take(1)
    links.start(cp.at[c, :, 1 - c], cp.at[c, :, 1 - c], row_sib, sibling)

    cot_base = links.take(CHIPS)
    exchange(sc, cc.at[c], cot_base)

    links.landed(cp.at[1 - c, :, c], row_sib, sibling)

    def choose_rows(k, carry):
        s = srcs[16 * c + k]
        xf[t, 16 * c + k] = cp[lax.rem(s, 2), lax.div(s, 2), c]
        return carry

    lax.fori_loop(0, 16, choose_rows, 0)

    def ring_sum(part, rr, rl, base, s):
        br, bl = up(t + 4 - s, TP), up(t - 4 + s, TP)
        for u in range(2):
            k = base + 8 * u
            w = slice(256 * u, 256 * u + 256)
            if s == 0:
                links.start(part.at[br, 0:80, w], rr.at[0, 0:80, w], k, right)
                links.start(part.at[bl, 80:160, w], rl.at[0, 80:160, w], k + 4, left)
                continue
            lo, hi = (slice(0, 80), slice(80, 160)) if s == 1 else (slice(0, 160),) * 2
            links.landed(rr.at[s - 1, lo, w], k + s - 1, left)
            part[br, lo, w] = (part[br, lo, w].astype(F32) + rr[s - 1, lo, w].astype(F32)).astype(BF)
            links.start(part.at[br, :, w], rr.at[s, :, w], k + s, right)
            links.landed(rl.at[s - 1, hi, w], k + 4 + s - 1, right)
            part[bl, hi, w] = (part[bl, hi, w].astype(F32) + rl[s - 1, hi, w].astype(F32)).astype(BF)
            links.start(part.at[bl, :, w], rl.at[s, :, w], k + 4 + s, left)

    def ring_end(rr, rl, base, u):
        w = slice(256 * u, 256 * u + 256)
        links.landed(rr.at[3, :, w], base + 8 * u + 3, left)
        links.landed(rl.at[3, :, w], base + 8 * u + 7, right)

    def ring_copy(buf, base, s):
        br, bl = up(t - s, TP), up(t + s, TP)
        for u in range(2):
            k = base + 8 * u
            w = slice(256 * u, 256 * u + 256)
            if s > 0:
                links.landed(buf.at[br, :, w], k + s - 1, left)
            lo, hi = (slice(0, 160),) * 2 if s < 3 else (slice(0, 80), slice(80, 160))
            links.start(buf.at[br, lo, w], buf.at[br, lo, w], k + s, right)
            if s > 0:
                links.landed(buf.at[bl, :, w], k + 4 + s - 1, right)
            links.start(buf.at[bl, hi, w], buf.at[bl, hi, w], k + 4 + s, left)

    def ring_copied(buf, base):
        far = up(t + 4, TP)
        for u in range(2):
            w = slice(256 * u, 256 * u + 256)
            links.landed(buf.at[far, 0:80, w], base + 8 * u + 3, left)
            links.landed(buf.at[far, 80:160, w], base + 8 * u + 7, right)

    def around(s, work):
        def step(i, carry):
            work(up(t + (2 * i - 1) * s, TP))
            return carry

        lax.fori_loop(0, 2, step, 0)

    x_base = links.take(16)
    xs_base = links.take(18)

    def rows_of(z, u, start, size):
        return xf.at[z, pl.ds(16 * c + 8 * u + start, size)]

    def hand_over(z, u):
        ref = rows_of(z, u, 0, 8)
        links.start(ref, ref, xs_base + 2 * z + u, sibling)

    def handed(z):
        for u in range(2):
            links.landed(xf.at[z, pl.ds(16 * (1 - c) + 8 * u, 8)], xs_base + 2 * z + u, sibling)

    def ring_rows(s):
        br, bl = up(t - s, TP), up(t + s, TP)
        for u in range(2):
            k = x_base + 8 * u
            size = 8 if s < 3 else 4
            if s > 0:
                links.landed(rows_of(br, u, 0, 8), k + s - 1, left)
            ref = rows_of(br, u, 0, size)
            links.start(ref, ref, k + s, right)
            if s > 0:
                links.landed(rows_of(bl, u, 0, 8), k + 4 + s - 1, right)
            ref = rows_of(bl, u, 8 - size, size)
            links.start(ref, ref, k + 4 + s, left)
            hand_over(br, u)
            if s > 0:
                hand_over(bl, u)

    def ring_rows_end():
        far = up(t + 4, TP)
        for u in range(2):
            links.landed(rows_of(far, u, 0, 4), x_base + 8 * u + 3, left)
            ref = rows_of(far, u, 0, 4)
            links.start(ref, ref, xs_base + 2 * far + u, sibling)
            links.landed(rows_of(far, u, 4, 4), x_base + 8 * u + 7, right)
            ref = rows_of(far, u, 4, 4)
            links.start(ref, ref, xs_base + 16 + u, sibling)

    ring_rows(0)

    gather_second(w2t.at[Y, :, 0:80], w2t.at[:, xh, 80:160, w2lane], w2_first, w2_base)

    @pl.when(jnp.logical_not(same))
    def _():
        links.landed(w1f.at[Y, X], relay1, (r, mate))

    gather_first(w1a, w1b, w1_base)

    def place(z):
        return lax.rem(z + t, TP)

    def grad_block(z):
        p = place(z)
        return dot(w2t[lax.div(p, 2), lax.rem(p, 2)], g[...].reshape(TOK, OUTW), NT)

    def grad_store(z):
        pg[z] = grad_block(z).astype(BF)

    def pre_add(z):
        p = place(z)
        rows = w1f[lax.div(p, 2), pl.ds(2 * lax.rem(p, 2), 2)].reshape(UNITS, FEAT)
        oh[...] += dot(rows, xf[z].reshape(TOK, FEAT), NT)

    pg_base = links.take(16)
    ht_base = links.take(16)
    def activate(u):
        w = slice(256 * u, 256 * u + 256)

        def step(i, carry):
            rows = pl.ds(pl.multiple_of(i * 32, 32), 32)
            v = oh[rows, w]
            cdf = 0.5 * (1.0 + lax.erf(v * 0.7071067811865476))
            density = jnp.exp(-0.5 * v * v) * 0.3989422804014327
            ht[t, rows, w] = (v * cdf).astype(BF)
            oh[rows, w] = cdf + v * density
            return carry

        lax.fori_loop(0, 5, step, 0)

    def descend(u):
        w = slice(256 * u, 256 * u + 256)

        def step(i, carry):
            rows = pl.ds(pl.multiple_of(i * 32, 32), 32)
            v = og[rows, w] + zgr[3, rows, w].astype(F32) + zgl[3, rows, w].astype(F32)
            gt[rows, w] = (v * oh[rows, w]).astype(BF)
            return carry

        lax.fori_loop(0, 5, step, 0)

    exchanged(cc.at[c], cot_base)
    cot_sib = links.take(1)
    links.start(cc.at[c], cc.at[c], cot_sib, sibling)

    ring_rows(1)
    links.landed(cc.at[1 - c], cot_sib, sibling)

    def choose(j, carry):
        s = srcs[j]
        g[j] = cc[lax.rem(s, 2), lax.div(s, 2), lax.div(j, 16)]
        return carry

    lax.fori_loop(0, 32, choose, 0)

    for d in range(1, 4):
        xx, yy = up(X - d, 4), up(Y - d, 4)
        links.landed(w2t.at[yy, :, 0:80], w2_base + 6 + d, along_y(-d))
        links.landed(
            w2t.at[:, lax.div(xx, 2), 80:160, pl.ds(pl.multiple_of(lax.rem(xx, 2) * 256, 256), 256)],
            w2_base + 9 + d,
            along_x(-d),
        )

    grad_store(up(t + 4, TP))
    ring_sum(pg, zgr, zgl, pg_base, 0)
    around(3, grad_store)
    gather_second(w1f.at[Y, :, 0:W1A], w1f.at[:, X, W1A:80], w1_first, w1_base)
    ring_rows(2)
    ring_sum(pg, zgr, zgl, pg_base, 1)
    around(2, grad_store)
    ring_rows(3)
    ring_sum(pg, zgr, zgl, pg_base, 2)
    around(1, grad_store)
    og[...] = grad_block(t)
    for d in range(1, 4):
        xx, yy = up(X - d, 4), up(Y - d, 4)
        links.landed(w1f.at[yy, :, 0:W1A], w1_base + 6 + d, along_y(-d))
        links.landed(w1f.at[:, xx, W1A:80], w1_base + 9 + d, along_x(-d))
    oh[...] = jnp.concatenate([b1s[:, c].reshape(UNITS, 128)] * 4, axis=1)
    handed(t)
    pre_add(t)
    for s in range(1, 3):
        handed(up(t - s, TP))
        handed(up(t + s, TP))
        around(s, pre_add)
    ring_sum(pg, zgr, zgl, pg_base, 3)
    ring_rows_end()
    handed(up(t - 3, TP))
    handed(up(t + 3, TP))
    around(3, pre_add)
    far_rows = xf.at[up(t + 4, TP)]
    for u in range(2):
        for i in range(2):
            ref = far_rows.at[pl.ds(16 * (1 - c) + 8 * u + 4 * i, 4)]
            links.landed(ref, xs_base + (2 * up(t + 4, TP) if i == 0 else 16) + u, sibling)
    pre_add(up(t + 4, TP))

    for u in range(2):
        activate(u)
    ring_copy(ht, ht_base, 0)
    def plane_send(part, cut, ra, rb, base, z):
        yy, par = lax.div(z, 2), lax.rem(z, 2)
        dy = up(yy - Y, 4)

        @pl.when(dy != 0)
        def _():
            links.make(
                part.at[yy, pl.ds(2 * par, 2), 0:cut],
                ra.at[dy - 1, pl.ds(2 * par, 2)],
                base + 2 * (dy - 1) + par,
                along_y(dy),
            ).start()

        for i in range(2):
            xx = 2 * par + i
            dx = up(xx - X, 4)

            @pl.when(dx != 0)
            def _(xx=xx, dx=dx):
                links.make(
                    part.at[yy, xx, cut:],
                    rb.at[dx - 1, yy],
                    base + 6 + 4 * (dx - 1) + yy,
                    along_x(dx),
                ).start()

    def plane_sent(part, cut, ra, rb, sa, sbx, rc, rd, base):
        def waits():
            for d in range(3):
                for i in range(2):
                    links.make(part.at[0, 0:2, 0:cut], ra.at[d, 0:2], base + 2 * d + i, along_y(1)).wait_send()
                for i in range(4):
                    links.make(part.at[0, 0, cut:], rb.at[d, 0], base + 6 + 4 * d + i, along_x(1)).wait_send()
                links.make(sa.at[0], rc.at[d], base + 19 + d, along_x(1)).wait_send()
                links.make(sbx.at[0], rd.at[d], base + 22 + d, along_y(1)).wait_send()

        links.open.append(waits)

    def plane_second(part, cut, ra, rb, sa, sbx, rc, rd, base, z):
        p = place(z)
        yy, par = lax.div(p, 2), lax.rem(p, 2)

        @pl.when(Y == yy)
        def _():
            for d in range(3):
                links.landed(ra.at[d, pl.ds(2 * par, 2)], base + 2 * d + par, along_y(-d - 1))
            for i in range(2):
                xx = 2 * par + i
                v = part[yy, xx, 0:cut].astype(F32)
                for d in range(3):
                    v = v + ra[d, xx].astype(F32)
                sa[xx] = v.astype(BF)
                dx = up(xx - X, 4)

                @pl.when(dx != 0)
                def _(xx=xx, dx=dx):
                    links.make(sa.at[xx], rc.at[dx - 1], base + 18 + dx, along_x(dx)).start()

        @pl.when(lax.div(X, 2) == par)
        def _():
            for d in range(3):
                links.landed(rb.at[d, yy], base + 6 + 4 * d + yy, along_x(-d - 1))
            v = part[yy, X, cut:].astype(F32)
            for d in range(3):
                v = v + rb[d, yy].astype(F32)
            sbx[yy] = v.astype(BF)
            dy = up(yy - Y, 4)

            @pl.when(dy != 0)
            def _():
                links.make(sbx.at[yy], rd.at[dy - 1], base + 21 + dy, along_y(dy)).start()

    def plane_sum_end(sa, sbx, rc, rd, base):
        for d in range(1, 4):
            links.landed(rc.at[d - 1], base + 18 + d, along_x(-d))
        va = sa[X].astype(F32)
        for d in range(3):
            va = va + rc[d].astype(F32)
        for d in range(1, 4):
            links.landed(rd.at[d - 1], base + 21 + d, along_y(-d))
        vb = sbx[Y].astype(F32)
        for d in range(3):
            vb = vb + rd[d].astype(F32)
        return va.astype(BF), vb.astype(BF)

    g2_base = links.take(25)

    def second_grad(z):
        p = place(z)
        v = dot(ht[z], g[...].reshape(TOK, OUTW), NN).astype(BF)
        for i in range(2):
            g2[lax.div(p, 2), 2 * lax.rem(p, 2) + i] = v[:, 256 * i : 256 * i + 256]
        plane_send(g2, 80, a2, c2, g2_base, p)

    def second_second(z):
        plane_second(g2, 80, a2, c2, s2a, s2b, d2, e2, g2_base, z)

    def embed(z):
        p = place(z)

        def step(i, carry):
            lanes = pl.ds(pl.multiple_of(i * 128, 128), 128)
            rows = ht[z, :, lanes].astype(F32).T.astype(BF)
            v = dot(rows, w2t[lax.div(p, 2), lax.rem(p, 2)], NN)
            pe[pl.ds(8 * i, 8)] += v.reshape(8, ROWS, OUTW)
            return carry

        lax.fori_loop(0, 4, step, 0)

    def use_hidden(z):
        second_grad(z)
        embed(z)

    plane_sent(g2, 80, a2, c2, s2a, s2b, d2, e2, g2_base)

    g1_base = links.take(25)

    def first_grad(z):
        p = place(z)
        v = dot(gt[...], xf[z].reshape(TOK, FEAT), NN).astype(BF)
        for i in range(2):
            g1[lax.div(p, 2), 2 * lax.rem(p, 2) + i] = v[80 * i : 80 * i + 80]
        plane_send(g1, W1A, a1, c1, g1_base, p)

    plane_sent(g1, W1A, a1, c1, s1a, s1b, d1, e1, g1_base)
    def first_second(z):
        plane_second(g1, W1A, a1, c1, s1a, s1b, d1, e1, g1_base, z)

    for u in range(2):
        ring_end(zgr, zgl, pg_base, u)
        descend(u)

    lax.fori_loop(0, TP, lambda z, carry: (first_grad(z), carry)[1], 0)
    pe[...] = jnp.zeros_like(pe)
    use_hidden(t)
    ring_copy(ht, ht_base, 1)
    around(1, use_hidden)
    ring_copy(ht, ht_base, 2)
    around(2, use_hidden)
    ring_copy(ht, ht_base, 3)
    around(3, use_hidden)
    lax.fori_loop(0, TP, lambda z, carry: (first_second(z), carry)[1], 0)

    ring_copied(ht, ht_base)
    use_hidden(up(t + 4, TP))

    def window_of(s, e):
        first = starts[s]
        slot = lax.rem(2 * m + e - first + 1024, SLOTS)
        return e * 16 + jnp.minimum(lax.div(first + slot, 32), 15)

    def pack_sibling(i, carry):
        for e in range(2):
            ps[2 * i + e] = pe[window_of(2 * i + 1 - c, e)].astype(BF)
        return carry

    lax.fori_loop(0, CHIPS, pack_sibling, 0)
    emb_sib = links.take(1)
    links.start(ps, pr, emb_sib, sibling)

    second_second(t)
    around(1, second_second)
    around(2, second_second)
    around(3, second_second)
    second_second(up(t + 4, TP))
    va, vb = plane_sum_end(s1a, s1b, d1, e1, g1_base)
    t1[0:W1A] = va
    t1[W1A:80] = vb
    back1 = links.take(2)

    def back1_z(do):
        @pl.when(jnp.logical_not(same))
        def _():
            do(links.make(t1, k1, back1, (r, mate)))

    back1_z(lambda copy: copy.start())

    @pl.when(same)
    def _():
        k1[...] = t1[...]

    links.open.append(lambda: back1_z(lambda copy: copy.wait_send()))

    va, vb = plane_sum_end(s2a, s2b, d2, e2, g2_base)
    for e in range(2):
        t2[e, 0:80] = va[:, 128 * e : 128 * e + 128]
        t2[e, 80:160] = vb[:, 128 * e : 128 * e + 128]
    back = links.take(3)

    def back_z(do):
        @pl.when(jnp.logical_not(same))
        def _():
            for e in range(2):
                do(links.make(t2.at[e], k2.at[c], back + c, (2 * m + e, mate), back + e))

        @pl.when(same)
        def _():
            do(links.make(t2.at[1 - c], k2.at[c], back + c, sibling, back + 1 - c))

    back_z(lambda copy: copy.start())

    @pl.when(same)
    def _():
        k2[c] = t2[c]

    links.open.append(lambda: back_z(lambda copy: copy.wait_send()))

    links.landed(pr, emb_sib, sibling)
    bias2 = b2[...].astype(F32).reshape(1, OUTW)

    def pack_home(i, carry):
        for e in range(2):
            v = pe[window_of(2 * i + c, e)] + pr[2 * i + e].astype(F32) + bias2
            sb[2 * i + e] = v.astype(BF)
        return carry

    lax.fori_loop(0, CHIPS, pack_home, 0)
    before = links.open
    links.open = []
    home_base = links.take(CHIPS)
    exchange(sb, bk, home_base)

    @pl.when(jnp.logical_not(same))
    def _():
        links.landed(k1, back1, (r, mate))

    def back1_plane(do):
        @pl.when(jnp.logical_not(still))
        def _():
            do(links.make(k1, gw1, back1 + 1, plane(old_chip)))

    back1_plane(lambda copy: copy.start())

    @pl.when(still)
    def _():
        gw1[...] = k1[...]

    links.open.append(lambda: back1_plane(lambda copy: copy.wait_send()))

    for e in range(2):

        @pl.when(jnp.logical_or(jnp.logical_not(same), e != c))
        def _(e=e):
            links.landed(k2.at[e], back + e, (2 * m + e, mate))

    def back_plane(do):
        @pl.when(jnp.logical_not(still))
        def _():
            do(links.make(k2, gw2, back + 2, plane(old_chip)))

    back_plane(lambda copy: copy.start())

    @pl.when(still)
    def _():
        gw2[...] = k2[...]

    links.open.append(lambda: back_plane(lambda copy: copy.wait_send()))

    links.finish(before)
    exchanged(bk, home_base)

    def home(j, carry):
        p = lax.rem(mine_start + j, DP)
        v = bk[lax.div(p, 2), lax.rem(p, 2)].astype(F32)
        emb[j] = jnp.where(j < mine_count, v, 0.0).astype(BF)
        return carry

    lax.fori_loop(0, SLOTS, home, 0)

    @pl.when(jnp.logical_not(still))
    def _():
        links.landed(gw1, back1 + 1, plane(mid_chip))
        links.landed(gw2, back + 2, plane(mid_chip))

    links.finish(links.open)


def on_device(patches, norm_gain, w_first, b_first, w_second, b_second, counts, cotangent):
    patches_t = patches.T
    w2v = w_second.T.reshape(2, 2, 80, 128)
    cot = cotangent.reshape(SLOTS, ROWS, OUTW)

    vmem = pl.BlockSpec(memory_space=pltpu.VMEM)
    V = pltpu.VMEM
    S = pltpu.SMEM
    emb, gw1, gw2 = pl.pallas_call(
        kernel,
        name="merger",
        out_shape=(
            jax.ShapeDtypeStruct((SLOTS, ROWS, OUTW), BF),
            jax.ShapeDtypeStruct((80, FEAT), BF),
            jax.ShapeDtypeStruct((2, UNITS, 128), BF),
        ),
        in_specs=[pl.BlockSpec(memory_space=pltpu.SMEM)] + [vmem] * 7,
        out_specs=(vmem, vmem, vmem),
        scratch_shapes=[
            pltpu.SemaphoreType.DMA((256,)),
            pltpu.SemaphoreType.DMA((256,)),
            pltpu.SemaphoreType.DMA,
            S((DP,), jnp.int32),
            S((DP,), jnp.int32),
            S((DP,), jnp.int32),
            V((DP, ROWS, OUTW), BF),
            V((2, CHIPS, 2, ROWS, OUTW), BF),
            V((32, ROWS, OUTW), BF),
            V((SLOTS, ROWS, FEAT), BF),
            V((DP, ROWS, FEAT), BF),
            V((2, CHIPS, 2, ROWS, FEAT), BF),
            V((TP, 32, ROWS, FEAT), BF),
            V((TP, 8, TOK), F32),
            V((4, 4, 80, FEAT), BF),
            V((4, 2, UNITS, OUTW), BF),
            V((TP, UNITS, TOK), BF),
            V((4, UNITS, TOK), BF),
            V((4, UNITS, TOK), BF),
            V((UNITS, TOK), F32),
            V((UNITS, TOK), F32),
            V((TP, UNITS, TOK), BF),
            V((UNITS, TOK), BF),
            V((32, ROWS, OUTW), F32),
            V((32, ROWS, OUTW), BF),
            V((32, ROWS, OUTW), BF),
            V((32, ROWS, OUTW), BF),
            V((CHIPS, 2, ROWS, OUTW), BF),
            V((4, 4, UNITS, 256), BF),
            V((3, 4, 80, 256), BF),
            V((3, 4, 80, 256), BF),
            V((4, 80, 256), BF),
            V((4, 80, 256), BF),
            V((3, 80, 256), BF),
            V((3, 80, 256), BF),
            V((2, UNITS, 128), BF),
            V((4, 4, 80, FEAT), BF),
            V((3, 4, W1A, FEAT), BF),
            V((3, 4, 80 - W1A, FEAT), BF),
            V((4, W1A, FEAT), BF),
            V((4, 80 - W1A, FEAT), BF),
            V((3, W1A, FEAT), BF),
            V((3, 80 - W1A, FEAT), BF),
            V((80, FEAT), BF),
            V((80, FEAT), BF),
            V((2, UNITS, 128), BF),
            V((80, FEAT), BF),
            V((2, UNITS, 128), BF),
            V((2, 2, 80, 128), F32),
            V((SLOTS, ROWS, FEAT), BF),
            V((2, UNITS, 128), BF),
            V((80, FEAT), BF),
        ],
        compiler_params=pltpu.CompilerParams(
            collective_id=0, has_side_effects=True, vmem_limit_bytes=56 * 1024 * 1024
        ),
        cost_estimate=pl.CostEstimate(
            flops=3_700_000_000, bytes_accessed=3_000_000, transcendentals=200_000
        ),
    )(counts, patches_t, w_first, w2v, b_first, b_second, norm_gain, cot)
    embeddings = emb.reshape(SLOTS * ROWS, OUTW)
    grad_w1 = gw1.reshape(80, 4, 160)
    grad_w2 = gw2.reshape(2, 2, 80, 128).transpose(3, 1, 0, 2).reshape(128, 320)
    return embeddings, grad_w1, grad_w2


def solution(mesh):
    in_specs = (
        P("dp", "tensor"),
        P("tensor"),
        P("dp", None, "tensor"),
        P("tensor"),
        P("dp", "tensor"),
        P("tensor"),
        P(),
        P("dp", "tensor"),
    )
    out_specs = (P("dp", "tensor"), P("dp", None, "tensor"), P("dp", "tensor"))
    return jax.shard_map(
        on_device, mesh=mesh, in_specs=in_specs, out_specs=out_specs, check_vma=False
    )
```

```python
import functools

import jax
import jax.numpy as jnp
from jax import lax
from jax.experimental import pallas as pl
from jax.experimental.pallas import tpu as pltpu
from jax.sharding import PartitionSpec as P

D = 1280
PATCH = 64
DP = 32
TP = 8
CHIPS = 16
SLOTS = 32
ROWS = PATCH // 4
TOK = 512
UNITS = 160
FEAT = 640
OUTW = 512
W1A = 48

MESH = pl.DeviceIdType.MESH
BF = jnp.bfloat16
F32 = jnp.float32
NT = (((1,), (1,)), ((), ()))
NN = (((1,), (0,)), ((), ()))
TN = (((0,), (0,)), ((), ()))


def dot(a, b, dims):
    return lax.dot_general(a, b, dims, preferred_element_type=F32)


def up(index, size):
    return lax.rem(index + size, size)


class Copies:
    def __init__(self, send, recv):
        self.send, self.recv, self.used, self.open = send, recv, 0, []

    def take(self, count):
        base = self.used
        self.used += count
        return base

    def make(self, src, dst, sem, dev, sent=None):
        return pltpu.make_async_remote_copy(
            src_ref=src,
            dst_ref=dst,
            send_sem=self.send.at[sem if sent is None else sent],
            recv_sem=self.recv.at[sem],
            device_id=dev,
            device_id_type=MESH,
        )

    def start(self, src, dst, sem, dev):
        copy = self.make(src, dst, sem, dev)
        copy.start()
        self.open.append(copy)

    def landed(self, dst, sem, dev):
        self.make(dst, dst, sem, dev).wait_recv()

    def finish(self, items):
        for item in items:
            if callable(item):
                item()
            else:
                item.wait_send()


def kernel(
    counts, patches_t, w1v, w2v, b1, b2, gain, cot,
    emb, gw1v, gw2v,
    send, recv, lsem, starts, ends, srcs,
    sc, cc, g, nrm, sp, cp, xf, sqx,
    w1f, w2t,
    pg, zgr, zgl, og, oh,
    ht, gt,
    pe, ps, pr, sb, bk,
    g2, a2, c2, s2a, s2b, d2, e2, t2,
    g1, a1, c1, s1a, s1b, d1, e1, t1,
    i1, i2, k1, k2, b1s, pk, w2p, w1, gw1, gw2,
):
    r = lax.axis_index("dp")
    t = lax.axis_index("tensor")
    m, c = lax.div(r, 2), lax.rem(r, 2)
    X, Y = lax.rem(m, 4), lax.div(m, 4)
    a, b = lax.div(m, 2), lax.rem(m, 2)
    links = Copies(send, recv)

    def plane(chip):
        return (2 * chip + c, t)

    def along_x(d):
        return plane(4 * Y + up(X + d, 4))

    def along_y(d):
        return plane(4 * up(Y + d, 4) + X)

    sibling = (2 * m + 1 - c, t)
    right, left = (r, up(t + 1, TP)), (r, up(t - 1, TP))
    mid_chip, old_chip = lax.rem(m + 2 * t, CHIPS), up(m - 2 * t, CHIPS)
    mate = up(a - t, TP)
    same, still = mate == t, t == 0

    barrier = pltpu.get_barrier_semaphore()

    def greet(dev):
        pl.semaphore_signal(barrier, inc=1, device_id=dev, device_id_type=MESH)

    for d in range(1, CHIPS):
        greet(plane(up(m + d, CHIPS)))
    for d in range(1, TP):
        greet((r, up(t + d, TP)))
    greet(sibling)

    @pl.when(jnp.logical_not(same))
    def _():
        greet((2 * m + 1 - c, mate))

    def prefix(s, total):
        starts[s] = total
        total = total + counts[s]
        ends[s] = total
        return total

    lax.fori_loop(0, DP, prefix, jnp.int32(0))
    mine_start, mine_count = starts[r], counts[r]

    def pack_cot(p, carry):
        sc[p] = cot[up(p - mine_start + 1024, SLOTS)]
        return carry

    lax.fori_loop(0, DP, pack_cot, 0)

    lane = lax.broadcasted_iota(jnp.int32, (8, FEAT), 1)
    row = lax.broadcasted_iota(jnp.int32, (8, FEAT), 0)
    lead = jnp.logical_and(lane >= row * 160, lane < row * 160 + 160)
    pick = jnp.where(lead, 1.0, 0.0).astype(F32)
    pick_bf = pick.astype(BF)
    line = lax.broadcasted_iota(jnp.int32, (256, 256), 0)
    col = lax.broadcasted_iota(jnp.int32, (256, 256), 1)
    order = jnp.where(col == 4 * lax.rem(line, 64) + lax.div(line, 64), 1.0, 0.0).astype(BF)
    for i in range(4):
        halves = []
        for j in range(2):
            at = 512 * i + 256 * j
            v = dot(order, patches_t[:, at : at + 256], NT)
            halves.append(jnp.concatenate([v[64 * p : 64 * p + 64] for p in range(4)], axis=1))
        v = jnp.concatenate(halves, axis=0)
        pk[8 * i : 8 * i + 8] = v.astype(BF).reshape(8, ROWS, FEAT)
        sq = v * v
        high = sq.astype(BF)
        low = (sq - high.astype(F32)).astype(BF)
        sqx[t, :, 128 * i : 128 * i + 128] = dot(pick_bf, high, NT) + dot(pick_bf, low, NT)
    for i in range(2):
        for e in range(2):
            w2p[e, 80 * i : 80 * i + 80] = w2v[i, e]
    wide = w1v[...].astype(F32)
    w1[...] = jnp.concatenate([wide[:, p] for p in range(4)], axis=1).astype(BF)
    gains = jnp.concatenate([gain[...].astype(F32).reshape(1, 160)] * 4, axis=1)
    b1s[...] = jnp.broadcast_to(b1[...].astype(F32).reshape(1, 320), (128, 320)).T.reshape(2, 2, 80, 128)

    pl.semaphore_wait(barrier, 23 + jnp.where(same, 0, 1))

    sq_base = links.take(TP)
    for d in range(1, TP):
        links.start(sqx.at[t], sqx.at[t], sq_base + d, (r, up(t + d, TP)))

    relay = links.take(2)
    relay1 = links.take(1)
    relay_mid = links.take(2)

    def relay_in(e):
        return w2t.at[Y, lax.div(X, 2), :, pl.ds(pl.multiple_of(b * 256 + e * 128, 128), 128)]

    def relay_steps(do):
        @pl.when(jnp.logical_not(still))
        def _():
            do(links.make(w2p, i2, relay_mid, plane(mid_chip)))
            do(links.make(w1, i1, relay_mid + 1, plane(mid_chip)))

    def relay_along_z(do):
        @pl.when(jnp.logical_not(same))
        def _():
            for e in range(2):
                do(links.make(i2.at[e], relay_in(c), relay + c, (2 * m + e, mate), relay + e))
            do(links.make(i1, w1f.at[Y, X], relay1, (r, mate)))

        @pl.when(same)
        def _():
            do(links.make(i2.at[1 - c], relay_in(c), relay + c, sibling, relay + 1 - c))

    relay_steps(lambda copy: copy.start())

    @pl.when(still)
    def _():
        i2[...] = w2p[...]
        i1[...] = w1[...]

    links.open.append(lambda: relay_steps(lambda copy: copy.wait_send()))
    links.open.append(lambda: relay_along_z(lambda copy: copy.wait_send()))

    def exchange(out, into, base):
        def step(d, carry):
            chip = up(m + d, CHIPS)
            links.make(out.at[pl.ds(2 * chip, 2)], into.at[m], base + d, plane(chip)).start()
            return carry

        lax.fori_loop(1, CHIPS, step, 0)

        def sent(d, carry):
            chip = up(m + d, CHIPS)
            links.make(out.at[pl.ds(2 * chip, 2)], into.at[m], base + d, plane(chip)).wait_send()
            return carry

        links.open.append(lambda: lax.fori_loop(1, CHIPS, sent, 0))
        into[m] = out[pl.ds(2 * m, 2)]

    def exchanged(into, base):
        def step(d, carry):
            links.landed(into.at[up(m - d, CHIPS)], base + d, plane(up(m - d, CHIPS)))
            return carry

        lax.fori_loop(1, CHIPS, step, 0)


    def gather_first(block_a, block_b, base):
        for d in range(1, 4):
            links.start(block_a, block_a, base + d, along_x(d))
            links.start(block_b, block_b, base + 3 + d, along_y(d))

    w1a = w1f.at[Y, X, 0:W1A]
    w1b = w1f.at[Y, X, W1A:80]
    w1_base = links.take(16)
    w2_base = links.take(16)
    w2lane = pl.ds(pl.multiple_of(b * 256, 256), 256)
    xh = lax.div(X, 2)
    w2a = w2t.at[Y, xh, 0:80, w2lane]
    w2b = w2t.at[Y, xh, 80:160, w2lane]

    def gather_second(wide_a, wide_b, arrived, base):
        for d in range(1, 4):
            ra, rb = arrived(d)
            links.landed(ra, base + d, along_x(-d))
            links.landed(rb, base + 3 + d, along_y(-d))
        for d in range(1, 4):
            links.start(wide_a, wide_a, base + 6 + d, along_y(d))
            links.start(wide_b, wide_b, base + 9 + d, along_x(d))

    def w2_first(d):
        xx, yy = up(X - d, 4), up(Y - d, 4)
        ra = w2t.at[Y, lax.div(xx, 2), 0:80, pl.ds(pl.multiple_of(lax.rem(xx, 2) * 256, 256), 256)]
        rb = w2t.at[yy, xh, 80:160, w2lane]
        return ra, rb

    def w1_first(d):
        return w1f.at[Y, up(X - d, 4), 0:W1A], w1f.at[up(Y - d, 4), X, W1A:80]

    def source(k, carry):
        p0 = 32 * k + 2 * m
        n0, n1 = jnp.int32(0), jnp.int32(0)
        for s in range(DP):
            v = ends[s]
            n0 = n0 + (v <= p0).astype(jnp.int32)
            n1 = n1 + (v <= p0 + 1).astype(jnp.int32)
        srcs[k] = jnp.minimum(n0, DP - 1)
        srcs[16 + k] = jnp.minimum(n1, DP - 1)
        return carry

    lax.fori_loop(0, 16, source, 0)

    for d in range(1, TP):
        z = up(t - d, TP)
        links.landed(sqx.at[z], sq_base + d, (r, z))
    total = sqx[0]
    for z in range(1, TP):
        total = total + sqx[z]
    inv = lax.rsqrt(total / D + 1e-06)
    part1 = inv.astype(BF).astype(F32)
    part2 = (inv - part1).astype(BF).astype(F32)
    stack = jnp.concatenate([part1, part2, (inv - part1) - part2], axis=0)
    stack_t = stack.T.astype(BF)
    pick3 = jnp.concatenate([pick, pick, pick], axis=0).astype(BF)
    for i in range(4):
        scale = dot(stack_t[128 * i : 128 * i + 128], pick3, NN)
        v = pk[8 * i : 8 * i + 8].reshape(128, FEAT).astype(F32)
        nrm[8 * i : 8 * i + 8] = (v * scale * gains).astype(BF).reshape(8, ROWS, FEAT)

    def pack_rows(p, carry):
        sp[p] = nrm[up(p - mine_start + 1024, SLOTS)]
        return carry

    lax.fori_loop(0, DP, pack_rows, 0)
    row_base = links.take(CHIPS)
    exchange(sp, cp.at[c], row_base)

    @pl.when(jnp.logical_not(still))
    def _():
        links.landed(i2, relay_mid, plane(old_chip))
        links.landed(i1, relay_mid + 1, plane(old_chip))

    relay_along_z(lambda copy: copy.start())

    @pl.when(same)
    def _():
        w1f[Y, X] = i1[...]
        own = pltpu.make_async_copy(i2.at[c], relay_in(c), lsem)
        own.start()
        own.wait()

    for e in range(2):

        @pl.when(jnp.logical_or(jnp.logical_not(same), e != c))
        def _(e=e):
            links.landed(relay_in(e), relay + e, sibling)

    gather_first(w2a, w2b, w2_base)

    exchanged(cp.at[c], row_base)
    row_sib = links.take(1)
    links.start(cp.at[c, :, 1 - c], cp.at[c, :, 1 - c], row_sib, sibling)

    cot_base = links.take(CHIPS)
    exchange(sc, cc.at[c], cot_base)

    links.landed(cp.at[1 - c, :, c], row_sib, sibling)

    def choose_rows(k, carry):
        s = srcs[16 * c + k]
        xf[t, 16 * c + k] = cp[lax.rem(s, 2), lax.div(s, 2), c]
        return carry

    lax.fori_loop(0, 16, choose_rows, 0)

    def ring_sum(part, rr, rl, base, s):
        br, bl = up(t + 4 - s, TP), up(t - 4 + s, TP)
        for u in range(2):
            k = base + 8 * u
            w = slice(256 * u, 256 * u + 256)
            if s == 0:
                links.start(part.at[br, 0:80, w], rr.at[0, 0:80, w], k, right)
                links.start(part.at[bl, 80:160, w], rl.at[0, 80:160, w], k + 4, left)
                continue
            lo, hi = (slice(0, 80), slice(80, 160)) if s == 1 else (slice(0, 160),) * 2
            links.landed(rr.at[s - 1, lo, w], k + s - 1, left)
            part[br, lo, w] = (part[br, lo, w].astype(F32) + rr[s - 1, lo, w].astype(F32)).astype(BF)
            links.start(part.at[br, :, w], rr.at[s, :, w], k + s, right)
            links.landed(rl.at[s - 1, hi, w], k + 4 + s - 1, right)
            part[bl, hi, w] = (part[bl, hi, w].astype(F32) + rl[s - 1, hi, w].astype(F32)).astype(BF)
            links.start(part.at[bl, :, w], rl.at[s, :, w], k + 4 + s, left)

    def ring_end(rr, rl, base, u):
        w = slice(256 * u, 256 * u + 256)
        links.landed(rr.at[3, :, w], base + 8 * u + 3, left)
        links.landed(rl.at[3, :, w], base + 8 * u + 7, right)

    def ring_copy(buf, base, s):
        br, bl = up(t - s, TP), up(t + s, TP)
        for u in range(2):
            k = base + 8 * u
            w = slice(256 * u, 256 * u + 256)
            if s > 0:
                links.landed(buf.at[br, :, w], k + s - 1, left)
            lo, hi = (slice(0, 160),) * 2 if s < 3 else (slice(0, 80), slice(80, 160))
            links.start(buf.at[br, lo, w], buf.at[br, lo, w], k + s, right)
            if s > 0:
                links.landed(buf.at[bl, :, w], k + 4 + s - 1, right)
            links.start(buf.at[bl, hi, w], buf.at[bl, hi, w], k + 4 + s, left)

    def ring_copied(buf, base):
        far = up(t + 4, TP)
        for u in range(2):
            w = slice(256 * u, 256 * u + 256)
            links.landed(buf.at[far, 0:80, w], base + 8 * u + 3, left)
            links.landed(buf.at[far, 80:160, w], base + 8 * u + 7, right)

    def around(s, work):
        def step(i, carry):
            work(up(t + (2 * i - 1) * s, TP))
            return carry

        lax.fori_loop(0, 2, step, 0)

    x_base = links.take(16)
    xs_base = links.take(18)

    def rows_of(z, u, start, size):
        return xf.at[z, pl.ds(16 * c + 8 * u + start, size)]

    def hand_over(z, u):
        ref = rows_of(z, u, 0, 8)
        links.start(ref, ref, xs_base + 2 * z + u, sibling)

    def handed(z):
        for u in range(2):
            links.landed(xf.at[z, pl.ds(16 * (1 - c) + 8 * u, 8)], xs_base + 2 * z + u, sibling)

    def ring_rows(s):
        br, bl = up(t - s, TP), up(t + s, TP)
        for u in range(2):
            k = x_base + 8 * u
            size = 8 if s < 3 else 4
            if s > 0:
                links.landed(rows_of(br, u, 0, 8), k + s - 1, left)
            ref = rows_of(br, u, 0, size)
            links.start(ref, ref, k + s, right)
            if s > 0:
                links.landed(rows_of(bl, u, 0, 8), k + 4 + s - 1, right)
            ref = rows_of(bl, u, 8 - size, size)
            links.start(ref, ref, k + 4 + s, left)
            hand_over(br, u)
            if s > 0:
                hand_over(bl, u)

    def ring_rows_end():
        far = up(t + 4, TP)
        for u in range(2):
            links.landed(rows_of(far, u, 0, 4), x_base + 8 * u + 3, left)
            ref = rows_of(far, u, 0, 4)
            links.start(ref, ref, xs_base + 2 * far + u, sibling)
            links.landed(rows_of(far, u, 4, 4), x_base + 8 * u + 7, right)
            ref = rows_of(far, u, 4, 4)
            links.start(ref, ref, xs_base + 16 + u, sibling)

    ring_rows(0)

    gather_second(w2t.at[Y, :, 0:80], w2t.at[:, xh, 80:160, w2lane], w2_first, w2_base)

    @pl.when(jnp.logical_not(same))
    def _():
        links.landed(w1f.at[Y, X], relay1, (r, mate))

    gather_first(w1a, w1b, w1_base)

    def place(z):
        return lax.rem(z + t, TP)

    def grad_block(z):
        p = place(z)
        return dot(w2t[lax.div(p, 2), lax.rem(p, 2)], g[...].reshape(TOK, OUTW), NT)

    def grad_store(z):
        pg[z] = grad_block(z).astype(BF)

    def pre_add(z):
        p = place(z)
        rows = w1f[lax.div(p, 2), pl.ds(2 * lax.rem(p, 2), 2)].reshape(UNITS, FEAT)
        oh[...] += dot(rows, xf[z].reshape(TOK, FEAT), NT)

    pg_base = links.take(16)
    ht_base = links.take(16)
    def activate(u):
        w = slice(256 * u, 256 * u + 256)

        def step(i, carry):
            rows = pl.ds(pl.multiple_of(i * 32, 32), 32)
            v = oh[rows, w]
            cdf = 0.5 * (1.0 + lax.erf(v * 0.7071067811865476))
            density = jnp.exp(-0.5 * v * v) * 0.3989422804014327
            ht[t, rows, w] = (v * cdf).astype(BF)
            oh[rows, w] = cdf + v * density
            return carry

        lax.fori_loop(0, 5, step, 0)

    def descend(u):
        w = slice(256 * u, 256 * u + 256)

        def step(i, carry):
            rows = pl.ds(pl.multiple_of(i * 32, 32), 32)
            v = og[rows, w] + zgr[3, rows, w].astype(F32) + zgl[3, rows, w].astype(F32)
            gt[rows, w] = (v * oh[rows, w]).astype(BF)
            return carry

        lax.fori_loop(0, 5, step, 0)

    exchanged(cc.at[c], cot_base)
    cot_sib = links.take(1)
    links.start(cc.at[c], cc.at[c], cot_sib, sibling)

    ring_rows(1)
    links.landed(cc.at[1 - c], cot_sib, sibling)

    def choose(j, carry):
        s = srcs[j]
        g[j] = cc[lax.rem(s, 2), lax.div(s, 2), lax.div(j, 16)]
        return carry

    lax.fori_loop(0, 32, choose, 0)

    for d in range(1, 4):
        xx, yy = up(X - d, 4), up(Y - d, 4)
        links.landed(w2t.at[yy, :, 0:80], w2_base + 6 + d, along_y(-d))
        links.landed(
            w2t.at[:, lax.div(xx, 2), 80:160, pl.ds(pl.multiple_of(lax.rem(xx, 2) * 256, 256), 256)],
            w2_base + 9 + d,
            along_x(-d),
        )

    grad_store(up(t + 4, TP))
    ring_sum(pg, zgr, zgl, pg_base, 0)
    around(3, grad_store)
    gather_second(w1f.at[Y, :, 0:W1A], w1f.at[:, X, W1A:80], w1_first, w1_base)
    ring_rows(2)
    ring_sum(pg, zgr, zgl, pg_base, 1)
    around(2, grad_store)
    ring_rows(3)
    ring_sum(pg, zgr, zgl, pg_base, 2)
    around(1, grad_store)
    og[...] = grad_block(t)
    for d in range(1, 4):
        xx, yy = up(X - d, 4), up(Y - d, 4)
        links.landed(w1f.at[yy, :, 0:W1A], w1_base + 6 + d, along_y(-d))
        links.landed(w1f.at[:, xx, W1A:80], w1_base + 9 + d, along_x(-d))
    oh[...] = jnp.concatenate([b1s[:, c].reshape(UNITS, 128)] * 4, axis=1)
    handed(t)
    pre_add(t)
    for s in range(1, 3):
        handed(up(t - s, TP))
        handed(up(t + s, TP))
        around(s, pre_add)
    ring_sum(pg, zgr, zgl, pg_base, 3)
    ring_rows_end()
    handed(up(t - 3, TP))
    handed(up(t + 3, TP))
    around(3, pre_add)
    far_rows = xf.at[up(t + 4, TP)]
    for u in range(2):
        for i in range(2):
            ref = far_rows.at[pl.ds(16 * (1 - c) + 8 * u + 4 * i, 4)]
            links.landed(ref, xs_base + (2 * up(t + 4, TP) if i == 0 else 16) + u, sibling)
    pre_add(up(t + 4, TP))

    for u in range(2):
        activate(u)
    ring_copy(ht, ht_base, 0)
    def plane_send(part, cut, ra, rb, base, z):
        yy, par = lax.div(z, 2), lax.rem(z, 2)
        dy = up(yy - Y, 4)

        @pl.when(dy != 0)
        def _():
            links.make(
                part.at[yy, pl.ds(2 * par, 2), 0:cut],
                ra.at[dy - 1, pl.ds(2 * par, 2)],
                base + 2 * (dy - 1) + par,
                along_y(dy),
            ).start()

        for i in range(2):
            xx = 2 * par + i
            dx = up(xx - X, 4)

            @pl.when(dx != 0)
            def _(xx=xx, dx=dx):
                links.make(
                    part.at[yy, xx, cut:],
                    rb.at[dx - 1, yy],
                    base + 6 + 4 * (dx - 1) + yy,
                    along_x(dx),
                ).start()

    def plane_sent(part, cut, ra, rb, sa, sbx, rc, rd, base):
        def waits():
            for d in range(3):
                for i in range(2):
                    links.make(part.at[0, 0:2, 0:cut], ra.at[d, 0:2], base + 2 * d + i, along_y(1)).wait_send()
                for i in range(4):
                    links.make(part.at[0, 0, cut:], rb.at[d, 0], base + 6 + 4 * d + i, along_x(1)).wait_send()
                links.make(sa.at[0], rc.at[d], base + 19 + d, along_x(1)).wait_send()
                links.make(sbx.at[0], rd.at[d], base + 22 + d, along_y(1)).wait_send()

        links.open.append(waits)

    def plane_second(part, cut, ra, rb, sa, sbx, rc, rd, base, z):
        p = place(z)
        yy, par = lax.div(p, 2), lax.rem(p, 2)

        @pl.when(Y == yy)
        def _():
            for d in range(3):
                links.landed(ra.at[d, pl.ds(2 * par, 2)], base + 2 * d + par, along_y(-d - 1))
            for i in range(2):
                xx = 2 * par + i
                v = part[yy, xx, 0:cut].astype(F32)
                for d in range(3):
                    v = v + ra[d, xx].astype(F32)
                sa[xx] = v.astype(BF)
                dx = up(xx - X, 4)

                @pl.when(dx != 0)
                def _(xx=xx, dx=dx):
                    links.make(sa.at[xx], rc.at[dx - 1], base + 18 + dx, along_x(dx)).start()

        @pl.when(lax.div(X, 2) == par)
        def _():
            for d in range(3):
                links.landed(rb.at[d, yy], base + 6 + 4 * d + yy, along_x(-d - 1))
            v = part[yy, X, cut:].astype(F32)
            for d in range(3):
                v = v + rb[d, yy].astype(F32)
            sbx[yy] = v.astype(BF)
            dy = up(yy - Y, 4)

            @pl.when(dy != 0)
            def _():
                links.make(sbx.at[yy], rd.at[dy - 1], base + 21 + dy, along_y(dy)).start()

    def plane_sum_end(sa, sbx, rc, rd, base):
        for d in range(1, 4):
            links.landed(rc.at[d - 1], base + 18 + d, along_x(-d))
        va = sa[X].astype(F32)
        for d in range(3):
            va = va + rc[d].astype(F32)
        for d in range(1, 4):
            links.landed(rd.at[d - 1], base + 21 + d, along_y(-d))
        vb = sbx[Y].astype(F32)
        for d in range(3):
            vb = vb + rd[d].astype(F32)
        return va.astype(BF), vb.astype(BF)

    g2_base = links.take(25)

    def second_grad(z):
        p = place(z)
        v = dot(ht[z], g[...].reshape(TOK, OUTW), NN).astype(BF)
        for i in range(2):
            g2[lax.div(p, 2), 2 * lax.rem(p, 2) + i] = v[:, 256 * i : 256 * i + 256]
        plane_send(g2, 80, a2, c2, g2_base, p)

    def second_second(z):
        plane_second(g2, 80, a2, c2, s2a, s2b, d2, e2, g2_base, z)

    def embed(z):
        p = place(z)

        def step(i, carry):
            lanes = pl.ds(pl.multiple_of(i * 128, 128), 128)
            rows = ht[z, :, lanes].astype(F32).T.astype(BF)
            v = dot(rows, w2t[lax.div(p, 2), lax.rem(p, 2)], NN)
            pe[pl.ds(8 * i, 8)] += v.reshape(8, ROWS, OUTW)
            return carry

        lax.fori_loop(0, 4, step, 0)

    def use_hidden(z):
        second_grad(z)
        embed(z)

    plane_sent(g2, 80, a2, c2, s2a, s2b, d2, e2, g2_base)

    g1_base = links.take(25)

    def first_grad(z):
        p = place(z)
        v = dot(gt[...], xf[z].reshape(TOK, FEAT), NN).astype(BF)
        for i in range(2):
            g1[lax.div(p, 2), 2 * lax.rem(p, 2) + i] = v[80 * i : 80 * i + 80]
        plane_send(g1, W1A, a1, c1, g1_base, p)

    plane_sent(g1, W1A, a1, c1, s1a, s1b, d1, e1, g1_base)
    def first_second(z):
        plane_second(g1, W1A, a1, c1, s1a, s1b, d1, e1, g1_base, z)

    for u in range(2):
        ring_end(zgr, zgl, pg_base, u)
        descend(u)

    lax.fori_loop(0, TP, lambda z, carry: (first_grad(z), carry)[1], 0)
    pe[...] = jnp.zeros_like(pe)
    use_hidden(t)
    ring_copy(ht, ht_base, 1)
    around(1, use_hidden)
    ring_copy(ht, ht_base, 2)
    around(2, use_hidden)
    ring_copy(ht, ht_base, 3)
    around(3, use_hidden)
    lax.fori_loop(0, TP, lambda z, carry: (first_second(z), carry)[1], 0)

    ring_copied(ht, ht_base)
    use_hidden(up(t + 4, TP))

    def window_of(s, e):
        first = starts[s]
        slot = lax.rem(2 * m + e - first + 1024, SLOTS)
        return e * 16 + jnp.minimum(lax.div(first + slot, 32), 15)

    def pack_sibling(i, carry):
        for e in range(2):
            ps[2 * i + e] = pe[window_of(2 * i + 1 - c, e)].astype(BF)
        return carry

    lax.fori_loop(0, CHIPS, pack_sibling, 0)
    emb_sib = links.take(1)
    links.start(ps, pr, emb_sib, sibling)

    second_second(t)
    around(1, second_second)
    around(2, second_second)
    around(3, second_second)
    second_second(up(t + 4, TP))
    va, vb = plane_sum_end(s1a, s1b, d1, e1, g1_base)
    t1[0:W1A] = va
    t1[W1A:80] = vb
    back1 = links.take(2)

    def back1_z(do):
        @pl.when(jnp.logical_not(same))
        def _():
            do(links.make(t1, k1, back1, (r, mate)))

    back1_z(lambda copy: copy.start())

    @pl.when(same)
    def _():
        k1[...] = t1[...]

    links.open.append(lambda: back1_z(lambda copy: copy.wait_send()))

    va, vb = plane_sum_end(s2a, s2b, d2, e2, g2_base)
    for e in range(2):
        t2[e, 0:80] = va[:, 128 * e : 128 * e + 128]
        t2[e, 80:160] = vb[:, 128 * e : 128 * e + 128]
    back = links.take(3)

    def back_z(do):
        @pl.when(jnp.logical_not(same))
        def _():
            for e in range(2):
                do(links.make(t2.at[e], k2.at[c], back + c, (2 * m + e, mate), back + e))

        @pl.when(same)
        def _():
            do(links.make(t2.at[1 - c], k2.at[c], back + c, sibling, back + 1 - c))

    back_z(lambda copy: copy.start())

    @pl.when(same)
    def _():
        k2[c] = t2[c]

    links.open.append(lambda: back_z(lambda copy: copy.wait_send()))

    links.landed(pr, emb_sib, sibling)
    bias2 = b2[...].astype(F32).reshape(1, OUTW)

    def pack_home(i, carry):
        for e in range(2):
            v = pe[window_of(2 * i + c, e)] + pr[2 * i + e].astype(F32) + bias2
            sb[2 * i + e] = v.astype(BF)
        return carry

    lax.fori_loop(0, CHIPS, pack_home, 0)
    before = links.open
    links.open = []
    home_base = links.take(CHIPS)
    exchange(sb, bk, home_base)

    @pl.when(jnp.logical_not(same))
    def _():
        links.landed(k1, back1, (r, mate))

    def back1_plane(do):
        @pl.when(jnp.logical_not(still))
        def _():
            do(links.make(k1, gw1, back1 + 1, plane(old_chip)))

    back1_plane(lambda copy: copy.start())

    @pl.when(still)
    def _():
        gw1[...] = k1[...]

    links.open.append(lambda: back1_plane(lambda copy: copy.wait_send()))

    for e in range(2):

        @pl.when(jnp.logical_or(jnp.logical_not(same), e != c))
        def _(e=e):
            links.landed(k2.at[e], back + e, (2 * m + e, mate))

    def back_plane(do):
        @pl.when(jnp.logical_not(still))
        def _():
            do(links.make(k2, gw2, back + 2, plane(old_chip)))

    back_plane(lambda copy: copy.start())

    @pl.when(still)
    def _():
        gw2[...] = k2[...]

    links.open.append(lambda: back_plane(lambda copy: copy.wait_send()))

    links.finish(before)
    exchanged(bk, home_base)

    def home(j, carry):
        p = lax.rem(mine_start + j, DP)
        v = bk[lax.div(p, 2), lax.rem(p, 2)].astype(F32)
        emb[j] = jnp.where(j < mine_count, v, 0.0).astype(BF)
        return carry

    lax.fori_loop(0, SLOTS, home, 0)

    @pl.when(jnp.logical_not(still))
    def _():
        links.landed(gw1, back1 + 1, plane(mid_chip))
        links.landed(gw2, back + 2, plane(mid_chip))

    for i in range(2):
        for e in range(2):
            gw2v[i, e] = gw2[e, 80 * i : 80 * i + 80]
    wide = gw1[...].astype(F32)
    parts = [wide[:, 160 * p : 160 * p + 160] for p in range(4)]
    gw1v[...] = jnp.stack(parts, axis=1).astype(BF)
    links.finish(links.open)


def on_device(patches, norm_gain, w_first, b_first, w_second, b_second, counts, cotangent):
    patches_t = patches.T
    w2v = w_second.T.reshape(2, 2, 80, 128)
    cot = cotangent.reshape(SLOTS, ROWS, OUTW)

    vmem = pl.BlockSpec(memory_space=pltpu.VMEM)
    V = pltpu.VMEM
    S = pltpu.SMEM
    emb, gw1, gw2 = pl.pallas_call(
        kernel,
        name="merger",
        out_shape=(
            jax.ShapeDtypeStruct((SLOTS, ROWS, OUTW), BF),
            jax.ShapeDtypeStruct((80, 4, 160), BF),
            jax.ShapeDtypeStruct((2, 2, 80, 128), BF),
        ),
        in_specs=[pl.BlockSpec(memory_space=pltpu.SMEM)] + [vmem] * 7,
        out_specs=(vmem, vmem, vmem),
        scratch_shapes=[
            pltpu.SemaphoreType.DMA((256,)),
            pltpu.SemaphoreType.DMA((256,)),
            pltpu.SemaphoreType.DMA,
            S((DP,), jnp.int32),
            S((DP,), jnp.int32),
            S((DP,), jnp.int32),
            V((DP, ROWS, OUTW), BF),
            V((2, CHIPS, 2, ROWS, OUTW), BF),
            V((32, ROWS, OUTW), BF),
            V((SLOTS, ROWS, FEAT), BF),
            V((DP, ROWS, FEAT), BF),
            V((2, CHIPS, 2, ROWS, FEAT), BF),
            V((TP, 32, ROWS, FEAT), BF),
            V((TP, 8, TOK), F32),
            V((4, 4, 80, FEAT), BF),
            V((4, 2, UNITS, OUTW), BF),
            V((TP, UNITS, TOK), BF),
            V((4, UNITS, TOK), BF),
            V((4, UNITS, TOK), BF),
            V((UNITS, TOK), F32),
            V((UNITS, TOK), F32),
            V((TP, UNITS, TOK), BF),
            V((UNITS, TOK), BF),
            V((32, ROWS, OUTW), F32),
            V((32, ROWS, OUTW), BF),
            V((32, ROWS, OUTW), BF),
            V((32, ROWS, OUTW), BF),
            V((CHIPS, 2, ROWS, OUTW), BF),
            V((4, 4, UNITS, 256), BF),
            V((3, 4, 80, 256), BF),
            V((3, 4, 80, 256), BF),
            V((4, 80, 256), BF),
            V((4, 80, 256), BF),
            V((3, 80, 256), BF),
            V((3, 80, 256), BF),
            V((2, UNITS, 128), BF),
            V((4, 4, 80, FEAT), BF),
            V((3, 4, W1A, FEAT), BF),
            V((3, 4, 80 - W1A, FEAT), BF),
            V((4, W1A, FEAT), BF),
            V((4, 80 - W1A, FEAT), BF),
            V((3, W1A, FEAT), BF),
            V((3, 80 - W1A, FEAT), BF),
            V((80, FEAT), BF),
            V((80, FEAT), BF),
            V((2, UNITS, 128), BF),
            V((80, FEAT), BF),
            V((2, UNITS, 128), BF),
            V((2, 2, 80, 128), F32),
            V((SLOTS, ROWS, FEAT), BF),
            V((2, UNITS, 128), BF),
            V((80, FEAT), BF),
            V((80, FEAT), BF),
            V((2, UNITS, 128), BF),
        ],
        compiler_params=pltpu.CompilerParams(
            collective_id=0, has_side_effects=True, vmem_limit_bytes=56 * 1024 * 1024
        ),
        cost_estimate=pl.CostEstimate(
            flops=3_700_000_000, bytes_accessed=3_000_000, transcendentals=200_000
        ),
    )(counts, patches_t, w_first, w2v, b_first, b_second, norm_gain, cot)
    embeddings = emb.reshape(SLOTS * ROWS, OUTW)
    grad_w2 = gw2.reshape(320, 128).T
    return embeddings, gw1, grad_w2


def solution(mesh):
    in_specs = (
        P("dp", "tensor"),
        P("tensor"),
        P("dp", None, "tensor"),
        P("tensor"),
        P("dp", "tensor"),
        P("tensor"),
        P(),
        P("dp", "tensor"),
    )
    out_specs = (P("dp", "tensor"), P("dp", None, "tensor"), P("dp", "tensor"))
    return jax.shard_map(
        on_device, mesh=mesh, in_specs=in_specs, out_specs=out_specs, check_vma=False
    )
```
